128 devices in a mesh: lat: 8 (over z, x_hi), lon: 16 (over y, x_lo, core).
Axes of the slice: x: 4 (x_hi: 2, x_lo: 2; x = x_hi * 2 + x_lo), y: 4, z: 4, core: 2. Of those that a mesh axis runs over, the one named last changes fastest.
Arguments:
- grid_inputs: bfloat16 [8, 16, 1024, 474], P('lat', 'lon'), may hold values from -6 to 6
- mesh_state: bfloat16 [8, 16, 128, 512], P('lat', 'lon'), may hold values from -6 to 6
- embed_in: bfloat16 [474, 512], replicated, may hold values from -0.25 to 0.25
- embed_out: bfloat16 [512, 512], replicated, may hold values from -0.25 to 0.25
- edge_square: bfloat16 [3, 3, 512, 512], replicated, may hold values from -0.25 to 0.25
- edge_geom_weight: float32 [3, 4, 512], replicated, may hold values from -3 to 3
- node_first: bfloat16 [3, 1024, 512], replicated, may hold values from -0.1875 to 0.1875
- node_second: bfloat16 [2, 512, 512], replicated, may hold values from -0.25 to 0.25
- head: bfloat16 [512, 227], replicated, may hold values from -0.25 to 0.25
- g2m_senders: int32 [8, 16, 2048], P('lat', 'lon'), may hold values from 0 to 9215, as said below
- g2m_receivers: int32 [8, 16, 2048], P('lat', 'lon'), may hold values from 0 to 127
- g2m_counts: int32 [8, 16], P('lat', 'lon'), may hold values from 1024 to 2048, as said below
- g2m_geom: float32 [8, 16, 4, 2048], P('lat', 'lon'), may hold values from -6 to 6
- mesh_senders: int32 [8, 16, 768], P('lat', 'lon'), may hold values from 0 to 1151, as said below
- mesh_geom: float32 [8, 16, 4, 768], P('lat', 'lon'), may hold values from -6 to 6
- coarse_senders: int32 [8, 16, 256], P('lat', 'lon'), may hold values from 0 to 2047
- coarse_receivers: int32 [8, 16, 256], P('lat', 'lon'), may hold values from 0 to 2047, as said below
- coarse_geom: float32 [8, 16, 4, 256], P('lat', 'lon'), may hold values from -6 to 6
- m2g_senders: int32 [8, 16, 3072], P('lat', 'lon'), may hold values from 0 to 1151, as said below
- m2g_geom: float32 [8, 16, 4, 3072], P('lat', 'lon'), may hold values from -6 to 6
Outputs:
- grid_outputs: bfloat16 [8, 16, 1024, 227], P('lat', 'lon')
The draws below stay inside these ranges and needn't reach their ends.
Inputs may be any that keep to these rules, and one draw needn't show every extreme that they name: `g2m_senders`: index s names node s % 1024 of neighbour s // 1024 of the tile; never a neighbour beyond the first or last band. `mesh_senders`: index s names node s % 128 of neighbour s // 128 of the tile; never a neighbour beyond the first or last band. `m2g_senders`: index s names node s % 128 of neighbour s // 128 of the tile; never a neighbour beyond the first or last band. `g2m_counts`: sector 0 of the first and last bands uses all 2048 slots; sector 0 of the band or bands farthest from both ends uses 2048 // 2. `coarse_receivers`: an edge of a tile enters a coarse node of that tile, of the tile before it in the numbering (counted round), or of the tile half the numbering away.
All inputs are finite; a program needn't handle non-finite values.
Results may differ from the reference program's by a relative error of at most 0.019.
Values may be sent and summed in bfloat16 or wider, within the bound.
No kernel may reach another device: no remote copies, remote signals or barrier semaphores. Data moves between devices by JAX's collectives and lax.ppermute only.
A program may use at most 128 MiB of HBM per device.

```python
import math
import jax
import jax.numpy as jnp
import numpy as np
from jax import lax

D = 512
C_IN = 474
C_OUT = 227
GEOMETRY = 4
MESH_DEGREE = 6
GRID_DEGREE = 3
GRID_DEV = 1024
MESH_DEV = 128
COARSE_DEV = 16
G2M_CAP = 2048
COARSE_EDGES = 256
LAT_TILES = 8
LON_TILES = 16
COARSE = 2048


def tile_senders(key, per_tile, edge_total):
    shape = (LAT_TILES, LON_TILES, edge_total)
    chooser = jax.random.randint(jax.random.fold_in(key, 11), shape, 0, 16)
    choose_tile = jnp.array([4, 4, 4, 4, 4, 4, 4, 4, 0, 1, 2, 3, 5, 6, 7, 8], dtype=jnp.int32)
    tile_index = jnp.take(choose_tile, chooser)
    band_index = lax.broadcasted_iota(jnp.int32, shape, 0) + tile_index // 3 - 1
    tile_index = jnp.where((band_index < 0) | (band_index >= LAT_TILES), 4, tile_index)
    node_index = jax.random.randint(jax.random.fold_in(key, 12), shape, 0, per_tile)
    return (tile_index * per_tile + node_index).astype(jnp.int32)


def draw_g2m_senders(key, part):
    key = jax.random.fold_in(key, 1)
    return tile_senders(key, GRID_DEV, G2M_CAP)


def draw_mesh_senders(key, part):
    key = jax.random.fold_in(key, 2)
    return tile_senders(key, MESH_DEV, MESH_DEGREE * MESH_DEV)


def draw_m2g_senders(key, part):
    key = jax.random.fold_in(key, 3)
    return tile_senders(key, MESH_DEV, GRID_DEGREE * GRID_DEV)


def draw_g2m_counts(key, part):
    key = jax.random.fold_in(key, 4)
    shape = (LAT_TILES, LON_TILES)
    band_index = lax.broadcasted_iota(jnp.int32, shape, 0)
    sector_index = lax.broadcasted_iota(jnp.int32, shape, 1)
    distance = jnp.minimum(band_index, LAT_TILES - 1 - band_index)
    farthest = max((LAT_TILES - 1) // 2, 1)
    base = G2M_CAP - G2M_CAP // 2 * distance // farthest
    jitter = jax.random.randint(key, shape, 0, G2M_CAP // (8 * farthest) + 1) * (sector_index > 0).astype(jnp.int32)
    sign = jnp.where((distance == farthest) & (base == G2M_CAP // 2), 1, -1).astype(jnp.int32)
    return (base + sign * jitter).astype(jnp.int32)


def draw_coarse_receivers(key, part):
    key = jax.random.fold_in(key, 5)
    shape = (LAT_TILES, LON_TILES, COARSE_EDGES)
    tiles = LAT_TILES * LON_TILES
    own = lax.broadcasted_iota(jnp.int32, shape, 0) * LON_TILES + lax.broadcasted_iota(jnp.int32, shape, 1)
    chooser = jax.random.randint(jax.random.fold_in(key, 21), shape, 0, 3)
    offsets = jnp.array([0, tiles - 1, tiles // 2], dtype=jnp.int32)
    target_tile = (own + jnp.take(offsets, chooser)) % tiles
    node_index = jax.random.randint(jax.random.fold_in(key, 22), shape, 0, COARSE_DEV)
    return (target_tile * COARSE_DEV + node_index).astype(jnp.int32)


def touch_ends(result, own_key, smallest, high):
    extent = result.shape
    spot = [jax.random.randint(jax.random.fold_in(own_key, axis), (), 0, extent[axis]) for axis in range(len(extent))]
    result = result.at[tuple(spot)].set(smallest)
    longest = extent.index(max(extent))
    spot[longest] = (spot[longest] + 1) % extent[longest]
    return result.at[tuple(spot)].set(high)


def level_of(own_key, shape, pieces, least, high):
    def one(position, blocks):
        draws = jax.random.uniform(jax.random.fold_in(jax.random.fold_in(own_key, 6), position), (blocks,), jnp.float32, least / len(pieces), high / len(pieces))
        return jnp.repeat(jnp.exp(draws), shape[position] // blocks).reshape((-1,) + (1,) * (len(shape) - position - 1))

    factor_of = one(*pieces[0])
    for cut in pieces[1:]:
        factor_of = factor_of * one(*cut)
    return factor_of


def cumulative_ranks(amount, skew):
    portions = [(1 << 20) // math.isqrt(rank ** skew) + 1 for rank in range(1, amount + 1)]
    deviation = 1 + sum(portions) // (1 << 30)
    return np.cumsum(np.array([max(1, weight // deviation) for weight in portions]))


def ranked(rng, shape, amount, lean):
    grid = cumulative_ranks(amount, lean)
    lot = jax.random.randint(jax.random.fold_in(rng, 1), shape, 0, int(grid[amount - 1]))
    grade = jnp.searchsorted(jnp.asarray(grid, jnp.int32), lot, side="right")
    return jax.random.permutation(jax.random.fold_in(rng, 2), amount)[grade].astype(jnp.int32)


def noise(own_key, shape, scale, limit, shards=(), kind=jnp.bfloat16):
    drawn = jax.random.normal(own_key, shape, jnp.float32) * scale
    if len(shards) > 0:
        drawn = level_of(own_key, shape, shards, -0.22, 0.18) * drawn
    return jnp.clip(drawn, min=-limit, max=limit).astype(kind)


def setup_inputs(seed: int = 0) -> dict:
    streams_of = jax.random.split(jax.random.key(seed), 21)
    grid_inputs = noise(streams_of[0], (LAT_TILES, LON_TILES, GRID_DEV, C_IN), 1.0, 6.0, ((0, 8), (1, 16)))
    mesh_state = noise(streams_of[1], (LAT_TILES, LON_TILES, MESH_DEV, D), 1.0, 6.0, ((0, 8), (1, 16)))
    embed_in = noise(streams_of[2], (C_IN, D), C_IN ** -0.5, 0.25)
    embed_out = noise(streams_of[3], (D, D), D ** -0.5, 0.25)
    edge_square = noise(streams_of[4], (3, 3, D, D), D ** -0.5, 0.25)
    edge_geom_weight = noise(streams_of[5], (3, GEOMETRY, D), GEOMETRY ** -0.5, 3.0, (), jnp.float32)
    node_first = noise(streams_of[6], (3, 2 * D, D), (2 * D) ** -0.5, 0.1875)
    node_second = noise(streams_of[7], (2, D, D), D ** -0.5, 0.25)
    head = noise(streams_of[8], (D, C_OUT), D ** -0.5, 0.25)
    g2m_senders = draw_g2m_senders(jax.random.fold_in(streams_of[20], 71), 0)
    g2m_receivers = touch_ends(jax.random.randint(streams_of[10], (LAT_TILES, LON_TILES, G2M_CAP), 0, MESH_DEV), jax.random.fold_in(streams_of[10], 1), 0, MESH_DEV - 1).astype(jnp.int32)
    g2m_counts = draw_g2m_counts(jax.random.fold_in(streams_of[20], 71), 0)
    g2m_geom = noise(streams_of[12], (LAT_TILES, LON_TILES, GEOMETRY, G2M_CAP), 1.0, 6.0, ((0, 8), (1, 16)), jnp.float32)
    mesh_senders = draw_mesh_senders(jax.random.fold_in(streams_of[20], 71), 0)
    mesh_geom = noise(streams_of[14], (LAT_TILES, LON_TILES, GEOMETRY, MESH_DEGREE * MESH_DEV), 1.0, 6.0, ((0, 8), (1, 16)), jnp.float32)
    coarse_senders = touch_ends(ranked(streams_of[15], (LAT_TILES, LON_TILES, COARSE_EDGES), COARSE, 2), jax.random.fold_in(streams_of[15], 3), 0, COARSE - 1).astype(jnp.int32)
    coarse_receivers = draw_coarse_receivers(jax.random.fold_in(streams_of[20], 71), 0)
    coarse_geom = noise(streams_of[17], (LAT_TILES, LON_TILES, GEOMETRY, COARSE_EDGES), 1.0, 6.0, ((0, 8), (1, 16)), jnp.float32)
    m2g_senders = draw_m2g_senders(jax.random.fold_in(streams_of[20], 71), 0)
    m2g_geom = noise(streams_of[19], (LAT_TILES, LON_TILES, GEOMETRY, GRID_DEGREE * GRID_DEV), 1.0, 6.0, ((0, 8), (1, 16)), jnp.float32)
    return dict(grid_inputs=grid_inputs, mesh_state=mesh_state, embed_in=embed_in, embed_out=embed_out, edge_square=edge_square, edge_geom_weight=edge_geom_weight, node_first=node_first, node_second=node_second, head=head, g2m_senders=g2m_senders, g2m_receivers=g2m_receivers, g2m_counts=g2m_counts, g2m_geom=g2m_geom, mesh_senders=mesh_senders, mesh_geom=mesh_geom, coarse_senders=coarse_senders, coarse_receivers=coarse_receivers, coarse_geom=coarse_geom, m2g_senders=m2g_senders, m2g_geom=m2g_geom)


def product(left, right):
    return jnp.dot(left, right, preferred_element_type=jnp.float32)


def messages(sender_rows, receiver_rows, geometry, geom_weight, second):
    embedded = jnp.einsum("ce,cd->ed", geometry.astype(jnp.float32), geom_weight.astype(jnp.float32), precision=lax.Precision.HIGHEST)
    pre = embedded + sender_rows.astype(jnp.float32) + receiver_rows.astype(jnp.float32)
    hidden = jax.nn.silu(pre).astype(jnp.bfloat16)
    return product(hidden, second).astype(jnp.bfloat16)


def node_update(node_rows, summed, first_layer, second_layer):
    latent_width = node_rows.shape[1]
    inner = product(node_rows, first_layer[:latent_width]) + product(summed.astype(jnp.bfloat16), first_layer[latent_width:])
    hidden = jax.nn.silu(inner).astype(jnp.bfloat16)
    return (node_rows.astype(jnp.float32) + product(hidden, second_layer)).astype(jnp.bfloat16)


def pad_tiles(field):
    wrapped = jnp.concatenate([field[:, -1:], field, field[:, :1]], axis=1)
    zeros = jnp.zeros_like(wrapped[:1])
    return jnp.concatenate([zeros, wrapped, zeros], axis=0)


def beside_all(padded, band, sector, per_tile):
    anchor = jnp.zeros((), jnp.int32)
    block = lax.dynamic_slice(padded, (band.astype(jnp.int32), sector.astype(jnp.int32), anchor, anchor), (3, 3, per_tile, padded.shape[3]))
    return block.reshape(9 * per_tile, padded.shape[3])


def reference(grid_inputs, mesh_state, embed_in, embed_out, edge_square, edge_geom_weight, node_first, node_second, head, g2m_senders, g2m_receivers, g2m_counts, g2m_geom, mesh_senders, mesh_geom, coarse_senders, coarse_receivers, coarse_geom, m2g_senders, m2g_geom):
    tiles = LAT_TILES * LON_TILES
    order = jnp.arange(tiles, dtype=jnp.int32)
    bands = order // LON_TILES
    sectors = order % LON_TILES

    def embed(inputs):
        hidden_in = jax.nn.silu(product(inputs, embed_in)).astype(jnp.bfloat16)
        latent = product(hidden_in, embed_out).astype(jnp.bfloat16)
        return latent, product(latent, edge_square[0, 0]).astype(jnp.bfloat16), product(latent, edge_square[2, 1]).astype(jnp.bfloat16)

    grid_latent, grid_send, grid_recv = lax.map(embed, grid_inputs.reshape(tiles, GRID_DEV, C_IN))
    grid_pad = pad_tiles(grid_send.reshape(LAT_TILES, LON_TILES, GRID_DEV, D))

    def encode(item):
        band, sector, mesh_node, senders, receivers, edge_count, geometry = item
        nearby = beside_all(grid_pad, band, sector, GRID_DEV)
        mesh_recv = product(mesh_node, edge_square[0, 1]).astype(jnp.bfloat16)
        message = messages(jnp.take(nearby, senders, axis=0), jnp.take(mesh_recv, receivers, axis=0), geometry, edge_geom_weight[0], edge_square[0, 2])
        active = jnp.arange(G2M_CAP, dtype=jnp.int32) < edge_count
        weighted = jnp.where(active[:, None], message.astype(jnp.float32), jnp.zeros((), jnp.float32))
        summed = jax.ops.segment_sum(weighted, receivers, num_segments=MESH_DEV)
        return node_update(mesh_node, summed, node_first[0], node_second[0])

    mesh_one = lax.map(encode, (bands, sectors, mesh_state.reshape(tiles, MESH_DEV, D), g2m_senders.reshape(tiles, G2M_CAP), g2m_receivers.reshape(tiles, G2M_CAP), g2m_counts.reshape(tiles), g2m_geom.reshape(tiles, GEOMETRY, G2M_CAP)))

    flat_one = mesh_one.reshape(tiles * MESH_DEV, D)
    proc_send = product(flat_one, edge_square[1, 0]).astype(jnp.bfloat16).reshape(tiles, MESH_DEV, D)
    proc_recv = product(flat_one, edge_square[1, 1]).astype(jnp.bfloat16).reshape(tiles, MESH_DEV, D)
    coarse_send = proc_send[:, :COARSE_DEV].reshape(COARSE, D)
    coarse_recv = proc_recv[:, :COARSE_DEV].reshape(COARSE, D)

    def coarse_edge(item):
        senders, receivers, geometry = item
        return messages(jnp.take(coarse_send, senders, axis=0), jnp.take(coarse_recv, receivers, axis=0), geometry, edge_geom_weight[1], edge_square[1, 2])

    coarse_message = lax.map(coarse_edge, (coarse_senders.reshape(tiles, COARSE_EDGES), coarse_receivers.reshape(tiles, COARSE_EDGES), coarse_geom.reshape(tiles, GEOMETRY, COARSE_EDGES)))
    coarse_total = jax.ops.segment_sum(coarse_message.reshape(tiles * COARSE_EDGES, D).astype(jnp.float32), coarse_receivers.reshape(tiles * COARSE_EDGES), num_segments=COARSE)
    coarse_part = coarse_total.reshape(tiles, COARSE_DEV, D)
    proc_pad = pad_tiles(proc_send.reshape(LAT_TILES, LON_TILES, MESH_DEV, D))

    def process(item):
        band, sector, mesh_node, recv_rows, senders, geometry, coarse_rows = item
        nearby = beside_all(proc_pad, band, sector, MESH_DEV)
        message = messages(jnp.take(nearby, senders, axis=0), jnp.repeat(recv_rows, MESH_DEGREE, axis=0), geometry, edge_geom_weight[1], edge_square[1, 2])
        summed = message.astype(jnp.float32).reshape(MESH_DEV, MESH_DEGREE, D).sum(axis=1)
        summed = summed + jnp.pad(coarse_rows, ((0, MESH_DEV - COARSE_DEV), (0, 0)))
        return node_update(mesh_node, summed, node_first[1], node_second[1])

    mesh_two = lax.map(process, (bands, sectors, mesh_one, proc_recv, mesh_senders.reshape(tiles, MESH_DEGREE * MESH_DEV), mesh_geom.reshape(tiles, GEOMETRY, MESH_DEGREE * MESH_DEV), coarse_part))

    dec_send = product(mesh_two.reshape(tiles * MESH_DEV, D), edge_square[2, 0]).astype(jnp.bfloat16)
    dec_pad = pad_tiles(dec_send.reshape(LAT_TILES, LON_TILES, MESH_DEV, D))

    def decode(item):
        band, sector, latent, recv_rows, senders, geometry = item
        nearby = beside_all(dec_pad, band, sector, MESH_DEV)
        message = messages(jnp.take(nearby, senders, axis=0), jnp.repeat(recv_rows, GRID_DEGREE, axis=0), geometry, edge_geom_weight[2], edge_square[2, 2])
        summed = message.astype(jnp.float32).reshape(GRID_DEV, GRID_DEGREE, D).sum(axis=1)
        inner = product(latent, node_first[2][:D]) + product(summed.astype(jnp.bfloat16), node_first[2][D:])
        hidden = jax.nn.silu(inner).astype(jnp.bfloat16)
        return product(hidden, head).astype(jnp.bfloat16)

    outputs = lax.map(decode, (bands, sectors, grid_latent, grid_recv, m2g_senders.reshape(tiles, GRID_DEGREE * GRID_DEV), m2g_geom.reshape(tiles, GEOMETRY, GRID_DEGREE * GRID_DEV)))
    return outputs.reshape(LAT_TILES, LON_TILES, GRID_DEV, C_OUT)
```

```python
import functools

import jax
import jax.numpy as jnp
from jax import lax
from jax.experimental import pallas as pl
from jax.experimental.pallas import tpu as pltpu
from jax.sharding import PartitionSpec as P

BF = jnp.bfloat16
F32 = jnp.float32
I32 = jnp.int32
WIDTH = 512
GRID_NODES = 1024
MESH_NODES = 128
MESH_DEGREE = 6
GRID_DEGREE = 3
COARSE_DEV = 16
SLOTS = 2048
CHUNK = 512
CHUNKS = SLOTS // CHUNK
PAYLOAD = MESH_NODES + 16 * CHUNKS
LON = 16
VMEM_BYTES = 40 * 1024 * 1024


def mm(left, right):
    return jnp.dot(left, right, preferred_element_type=F32)


def mm_t(left, right):
    return lax.dot_general(left, right, (((0,), (0,)), ((), ())), preferred_element_type=F32)


def mm_nt(left, right):
    return lax.dot_general(left, right, (((1,), (1,)), ((), ())), preferred_element_type=F32)


def silu(v):
    half = 0.5 * v
    return half + half * jnp.tanh(half)


def one_hot(column, width):
    spots = lax.broadcasted_iota(I32, (column.shape[0], width), 1)
    return jnp.where(spots == column, 1.0, 0.0).astype(BF)


def whole(shape=None, index=None):
    if shape is None:
        return pl.BlockSpec(memory_space=pltpu.VMEM)
    return pl.BlockSpec(shape, lambda i: index)


SMEM = pl.BlockSpec(memory_space=pltpu.SMEM)


def square(block, kind):
    return whole((None, None, WIDTH, WIDTH), (block, kind, 0, 0))


def first_half(block, half):
    return whole((None, WIDTH, WIDTH), (block, half, 0))


def second_of(block):
    return whole((None, WIDTH, WIDTH), (block, 0, 0))


def kernel_call(body, outs, specs, args, scratch=(), flops=0, moved=0, name=None):
    return pl.pallas_call(
        body,
        grid=(1,),
        out_shape=outs,
        in_specs=specs,
        scratch_shapes=list(scratch),
        compiler_params=pltpu.CompilerParams(vmem_limit_bytes=VMEM_BYTES),
        cost_estimate=pl.CostEstimate(flops=flops, bytes_accessed=moved, transcendentals=0),
        name=name,
    )(*args)


def shaped(shape, dtype):
    return jax.ShapeDtypeStruct(shape, dtype)


def fill_list(scr, width, indices, geometry):
    for row, value in enumerate(indices):
        scr[row : row + 1, 0:width] = value.astype(F32)
    high = geometry.astype(BF).astype(F32)
    scr[4:8, 0:width] = high
    scr[8:12, 0:width] = geometry - high
    scr[12:16, 0:width] = high


def pack_body(count, senders, receivers, geometry, state, c_senders, c_receivers, c_geometry, out, c_out, scr):
    out[0:MESH_NODES, :] = state[...]
    for c in range(CHUNKS):
        cols = slice(c * CHUNK, (c + 1) * CHUNK)
        s = senders[:, cols]
        edge = lax.broadcasted_iota(I32, (1, CHUNK), 1) + c * CHUNK
        code = jnp.where(edge < count[0, 0], lax.shift_right_logical(s, 10) + 1, 0)
        local = s & (GRID_NODES - 1)
        fill_list(
            scr, CHUNK, (code, lax.shift_right_logical(local, 8), local & 255, receivers[:, cols]), geometry[:, cols]
        )
        out[MESH_NODES + 16 * c : MESH_NODES + 16 * (c + 1), :] = scr[...].astype(BF)
    s = c_senders[...]
    r = c_receivers[...]
    n = s.shape[1]
    fill_list(
        scr, n, (lax.shift_right_logical(s, 8), s & 255, lax.shift_right_logical(r, 4), r & 15), c_geometry[...]
    )
    c_out[...] = scr[:, 0:n].astype(BF)


def prep_body(m_senders, m_geometry, d_senders, d_geometry, weight, m_out, d_out, w_out, scr, turned):
    for senders, geometry, degree, out in (
        (m_senders, m_geometry, MESH_DEGREE, m_out),
        (d_senders, d_geometry, GRID_DEGREE, d_out),
    ):
        n = senders.shape[1]
        s = senders[...]
        near = lax.shift_right_logical(s, 7)
        band = lax.shift_right_logical(near * 11, 5)
        spot = ((near - 3 * band) * 3 + band) * MESH_NODES + (s & (MESH_NODES - 1))
        zero = jnp.zeros((1, n), F32)
        fill_list(scr, n, (spot, zero, zero, zero), geometry[...])
        turned[0:n, :] = scr[:, 0:n].T
        for t in range(degree):
            out[t] = turned[pl.ds(t, n // degree, stride=degree), :]
    for k in range(3):
        w = weight[k]
        high = w.astype(BF).astype(F32)
        scr[0:4, 0:WIDTH] = jnp.zeros((4, WIDTH), F32)
        scr[4:8, 0:WIDTH] = high
        scr[8:12, 0:WIDTH] = high
        scr[12:16, 0:WIDTH] = w - high
        w_out[k] = scr[:, 0:WIDTH].astype(BF)


def embed_body(x, w_in, w_out, w_send, latent, send):
    for b in range(4):
        rows = slice(256 * b, 256 * (b + 1))
        hidden = silu(mm(x[rows, :], w_in[...])).astype(BF)
        lat = mm(hidden, w_out[...]).astype(BF)
        latent[rows, :] = lat
        send[rows, :] = mm(lat, w_send[...]).astype(BF)


def grid_body(latent, w_recv, w_first, recv, base):
    for b in range(4):
        rows = slice(256 * b, 256 * (b + 1))
        recv[rows, :] = mm(latent[rows, :], w_recv[...]).astype(BF)
        base[rows, :] = mm(latent[rows, :], w_first[...])


def self_body(payload, send, w_recv, w_geom, out, q):
    q[...] = mm(payload[0:MESH_NODES, :], w_recv[...]).astype(BF)
    out[...] = jnp.zeros_like(out)

    @pl.loop(0, CHUNKS)
    def _(c):
        rows = pl.ds(pl.multiple_of(MESH_NODES + 16 * c, 16), 16)
        d = payload[rows, :].astype(F32).T
        for h in range(2):
            part = d[256 * h : 256 * (h + 1), :]
            s = (part[:, 1:2] * 256.0 + part[:, 2:3]).astype(I32)
            r = jnp.where(part[:, 0:1] == 5.0, part[:, 3:4], -1.0).astype(I32)
            pick = one_hot(r, MESH_NODES)
            pre = mm(one_hot(s, GRID_NODES), send[...]) + mm(pick, q[...]) + mm(part.astype(BF), w_geom[...])
            out[...] += mm_t(pick, silu(pre).astype(BF))


def near_body(left, centre, right, send, w_recv, w_geom, o_left, o_centre, o_right, masks, ranks, q):
    lists = []
    for a in range(3):
        lists.append((left, a, (2 - a) * 3 + 2, o_left, a))
        if a != 1:
            lists.append((centre, a, (2 - a) * 3 + 1, o_centre, a // 2))
        lists.append((right, a, (2 - a) * 3, o_right, a))
    for i, (src, a, bucket, _, _) in enumerate(lists):
        for c in range(CHUNKS):
            code = src[a, MESH_NODES + 16 * c : MESH_NODES + 16 * (c + 1), :].astype(F32)[0:1, :]
            row = i * CHUNKS + c
            masks[row : row + 1, :] = jnp.where(code == float(bucket + 1), 1.0, 0.0)
    n = masks.shape[0]
    mask = masks[...]
    before = lax.broadcasted_iota(I32, (CHUNK, CHUNK), 0) < lax.broadcasted_iota(I32, (CHUNK, CHUNK), 1)
    inside = mm(mask.astype(BF), jnp.where(before, 1.0, 0.0).astype(BF))
    mine = lax.broadcasted_iota(I32, (n, n), 0)
    other = lax.broadcasted_iota(I32, (n, n), 1)
    earlier = jnp.where((other < mine) & (mine // CHUNKS == other // CHUNKS), 1.0, 0.0).astype(BF)
    carried = mm(earlier, mask.astype(BF)).sum(axis=1, keepdims=True)
    ranks[...] = jnp.where(mask > 0.5, inside + carried, -1.0).astype(I32)
    for i, (src, a, _, dst, at) in enumerate(lists):
        q[i] = mm(src[a, 0:MESH_NODES, :], w_recv[...]).astype(BF)

    for i, (src, a, bucket, dst, at) in enumerate(lists):

        def hidden_sum(k, src=src, a=a, bucket=bucket, i=i):
            slot = lax.broadcasted_iota(I32, (128, CHUNK), 0) + k * 128
            d = jnp.zeros((128, 16), F32)
            for c in range(CHUNKS):
                row = i * CHUNKS + c
                chosen = jnp.where(slot == ranks[row : row + 1, :], 1.0, 0.0).astype(BF)
                d += mm_nt(chosen, src[a, MESH_NODES + 16 * c : MESH_NODES + 16 * (c + 1), :])
            s = (d[:, 1:2] * 256.0 + d[:, 2:3]).astype(I32)
            r = jnp.where(d[:, 0:1] == float(bucket + 1), d[:, 3:4], -1.0).astype(I32)
            pick = one_hot(r, MESH_NODES)
            pre = mm(one_hot(s, GRID_NODES), send[...]) + mm(pick, q[i]) + mm(d.astype(BF), w_geom[...])
            return mm_t(pick, silu(pre).astype(BF))

        used = jnp.sum(masks[i * CHUNKS : (i + 1) * CHUNKS, :]).astype(I32)
        blocks = lax.shift_right_logical(used + 127, 7)
        total = lax.fori_loop(1, blocks, lambda k, t, f=hidden_sum: t + f(k), hidden_sum(0))
        dst[at] = total.astype(BF)


def side_sum_body(o_centre, from_left, from_right, out):
    for k, a in ((0, 0), (1, 2)):
        total = o_centre[k].astype(F32) + from_left[a].astype(F32) + from_right[a].astype(F32)
        out[k] = total.astype(BF)


def split_mm(value, weight):
    high = value.astype(BF)
    low = (value - high.astype(F32)).astype(BF)
    return mm(high, weight) + mm(low, weight)


def node_rows(v, hidden_total, w_second, first_node, first_sum, second):
    m = split_mm(hidden_total, w_second).astype(BF)
    u = silu(mm(v, first_node) + mm(m, first_sum)).astype(BF)
    return (v.astype(F32) + mm(u, second)).astype(BF)


def node_body(
    own, from_left, from_right, up, down, state, w_second, first_node, first_sum, second, w_send, w_recv,
    mesh_one, send, recv,
):
    total = own[...] + from_left[...].astype(F32) + from_right[...].astype(F32)
    total = total + up[...].astype(F32) + down[...].astype(F32)
    one = node_rows(state[...], total, w_second[...], first_node[...], first_sum[...], second[...])
    mesh_one[...] = one
    send[...] = mm(one, w_send[...]).astype(BF)
    recv[...] = mm(one, w_recv[...]).astype(BF)


def fine_body(edges, left, centre, right, recv, w_geom, out):
    q = recv[...].astype(F32)
    n = 3 * MESH_NODES
    total = jnp.zeros((MESH_NODES, WIDTH), F32)
    for t in range(MESH_DEGREE):
        d = edges[t]
        spread = one_hot(d[:, 0:1].astype(I32), 3 * n)
        pre = q + mm(d.astype(BF), w_geom[...])
        pre += mm(spread[:, 0:n], left[...]) + mm(spread[:, n : 2 * n], centre[...])
        pre += mm(spread[:, 2 * n :], right[...])
        total += silu(pre)
    out[...] = total


def mesh_body(
    place, fine, list_a, list_b, list_c, coarse_a, coarse_b, recv, mesh_one, w_geom, w_second, first_node, first_sum,
    second, w_send, send,
):
    z, y, x, core, tile = (place[0, k] for k in range(5))
    half = coarse_a.shape[0]
    q = recv[0:COARSE_DEV, :]
    total = jnp.zeros((MESH_NODES, WIDTH), F32)
    for edges in (list_a, list_b, list_c):
        d = edges[...].astype(F32).T
        s = (d[:, 0:1] * 256.0 + d[:, 1:2]).astype(I32)
        t = lax.shift_right_logical(s, 4)
        lat = lax.shift_right_logical(t, 4)
        lon = t & 15
        gz = (z - lax.shift_right_logical(lat, 1)) & 3
        gy = (y - lax.shift_right_logical(lon, 2)) & 3
        gx = (x - ((lat & 1) * 2 + (lax.shift_right_logical(lon, 1) & 1))) & 3
        gc = (core + lon) & 1
        spot = (((gc * 4 + gx) * 4 + gy) * 4 + gz) * 16 + (s & 15)
        mine = d[:, 2:3].astype(I32) == tile
        r = jnp.where(mine, d[:, 3:4].astype(I32), -1)
        pick = one_hot(r, MESH_NODES)
        spread = one_hot(spot, 2 * half)
        pre = mm(spread[:, 0:half], coarse_a[...]) + mm(spread[:, half:], coarse_b[...])
        pre += mm(pick[:, 0:COARSE_DEV], q) + mm(d.astype(BF), w_geom[...])
        total += mm_t(pick, silu(pre).astype(BF))
    two = node_rows(
        mesh_one[...], total + fine[...], w_second[...], first_node[...], first_sum[...], second[...]
    )
    send[...] = mm(two, w_send[...]).astype(BF)


def decode_body(edges, left, centre, right, recv, base, w_geom, w_second, first_sum, head, out):
    n = 3 * MESH_NODES

    @pl.loop(0, 4)
    def _(b):
        rows = pl.ds(pl.multiple_of(256 * b, 256), 256)
        q = recv[rows, :].astype(F32)
        total = jnp.zeros((256, WIDTH), F32)
        for t in range(GRID_DEGREE):
            d = edges[t, rows, :]
            spread = one_hot(d[:, 0:1].astype(I32), 3 * n)
            pre = q + mm(d.astype(BF), w_geom[...])
            pre += mm(spread[:, 0:n], left[...]) + mm(spread[:, n : 2 * n], centre[...])
            pre += mm(spread[:, 2 * n :], right[...])
            total += silu(pre)
        summed = mm(total.astype(BF), w_second[...]).astype(BF)
        hidden = silu(base[rows, :] + mm(summed, first_sum[...])).astype(BF)
        out[rows, :] = mm(hidden, head[...]).astype(BF)


def shift(value, axis, step, periodic):
    n = lax.axis_size(axis)
    pairs = [(i, (i + step) % n) for i in range(n) if periodic or 0 <= i + step < n]
    return lax.ppermute(value, axis, pairs)


def columns(value):
    up = shift(value, "lat", 1, False)
    down = shift(value, "lat", -1, False)
    centre = jnp.stack([up, value, down])
    return shift(centre, "lon", 1, True), centre, shift(centre, "lon", -1, True)


def coarse_gather(rows):
    def joined(value, pairs_of, axis):
        return jnp.concatenate([value] + [lax.ppermute(value, axis, pairs_of(s)) for s in (1, 2, 3)], axis=0)

    def along_z(s):
        return [(i, ((i // 2 + s) % 4) * 2 + i % 2) for i in range(8)]

    def along_y(s):
        return [(i, ((i // 4 + s) % 4) * 4 + i % 4) for i in range(16)]

    def along_x(s):
        pairs = []
        for lat in range(8):
            for lon in range(16):
                x = ((lat % 2) * 2 + (lon // 2) % 2 + s) % 4
                to_lat = lat // 2 * 2 + x // 2
                to_lon = lon // 4 * 4 + (x % 2) * 2 + lon % 2
                pairs.append((lat * 16 + lon, to_lat * 16 + to_lon))
        return pairs

    rows = joined(rows, along_z, "lat")
    rows = joined(rows, along_y, "lon")
    rows = joined(rows, along_x, ("lat", "lon"))
    return rows, lax.ppermute(rows, "lon", [(i, i ^ 1) for i in range(16)])


def per_device(
    grid_inputs,
    mesh_state,
    embed_in,
    embed_out,
    edge_square,
    edge_geom_weight,
    node_first,
    node_second,
    head,
    g2m_senders,
    g2m_receivers,
    g2m_counts,
    g2m_geom,
    mesh_senders,
    mesh_geom,
    coarse_senders,
    coarse_receivers,
    coarse_geom,
    m2g_senders,
    m2g_geom,
):
    v = whole()
    mesh_rows = (MESH_NODES, WIDTH)
    grid_rows = (GRID_NODES, WIDTH)
    grid_flops = 2 * GRID_NODES * WIDTH * WIDTH
    mesh_flops = grid_flops // 8
    state = mesh_state[0, 0]
    payload, coarse_list = kernel_call(
        pack_body,
        (shaped((PAYLOAD, WIDTH), BF), shaped((16, coarse_senders.shape[2]), BF)),
        [SMEM] + [v] * 7,
        (
            g2m_counts, g2m_senders[0], g2m_receivers[0], g2m_geom[0, 0], state,
            coarse_senders[0], coarse_receivers[0], coarse_geom[0, 0],
        ),
        [pltpu.VMEM((16, CHUNK), F32)],
        name="pack",
    )
    near_left, near_centre, near_right = columns(payload)
    tiles = lax.axis_size(("lat", "lon"))
    both = ("lat", "lon")
    list_next = lax.ppermute(coarse_list, both, [(t, (t - 1) % tiles) for t in range(tiles)])
    list_far = lax.ppermute(coarse_list, both, [(t, (t + tiles // 2) % tiles) for t in range(tiles)])

    m_edges, d_edges, geom = kernel_call(
        prep_body,
        (
            shaped((MESH_DEGREE, MESH_NODES, 16), F32),
            shaped((GRID_DEGREE, GRID_NODES, 16), F32),
            shaped((3, 16, WIDTH), BF),
        ),
        [v] * 5,
        (mesh_senders[0], mesh_geom[0, 0], m2g_senders[0], m2g_geom[0, 0], edge_geom_weight),
        [pltpu.VMEM((16, 3072), F32), pltpu.VMEM((3072, 16), F32)],
        flops=grid_flops,
        name="prep",
    )
    latent, grid_send = kernel_call(
        embed_body,
        (shaped(grid_rows, BF), shaped(grid_rows, BF)),
        [v, v, v, square(0, 0)],
        (grid_inputs[0, 0], embed_in, embed_out, edge_square),
        flops=3 * grid_flops,
        moved=5 << 20,
        name="embed",
    )

    def geom_of(k):
        return whole((None, 16, WIDTH), (k, 0, 0))

    own_sum = kernel_call(
        self_body,
        shaped(mesh_rows, F32),
        [v, v, square(0, 1), geom_of(0)],
        (payload, grid_send, edge_square, geom),
        [pltpu.VMEM(mesh_rows, BF)],
        flops=5 * grid_flops,
        moved=3 << 20,
        name="own",
    )
    three = (3,) + mesh_rows
    to_left, to_centre, to_right = kernel_call(
        near_body,
        (shaped(three, BF), shaped((2,) + mesh_rows, BF), shaped(three, BF)),
        [v, v, v, v, square(0, 1), geom_of(0)],
        (near_left, near_centre, near_right, grid_send, edge_square, geom),
        [
            pltpu.VMEM((8 * CHUNKS, CHUNK), F32),
            pltpu.VMEM((8 * CHUNKS, CHUNK), I32),
            pltpu.VMEM((8,) + mesh_rows, BF),
        ],
        flops=4 * grid_flops,
        moved=5 << 20,
        name="near",
    )
    from_right = shift(to_left, "lon", -1, True)
    from_left = shift(to_right, "lon", 1, True)
    grid_recv, grid_base = kernel_call(
        grid_body,
        (shaped(grid_rows, BF), shaped(grid_rows, F32)),
        [v, square(2, 1), first_half(2, 0)],
        (latent, edge_square, node_first),
        flops=2 * grid_flops,
        moved=5 << 20,
        name="grid",
    )
    sides = kernel_call(
        side_sum_body, shaped((2,) + mesh_rows, BF), [v] * 3, (to_centre, from_left, from_right), name="sides"
    )
    down = shift(sides[0], "lat", -1, False)
    up = shift(sides[1], "lat", 1, False)
    middle = whole((None,) + mesh_rows, (1, 0, 0))
    mesh_one, proc_send, proc_recv = kernel_call(
        node_body,
        (shaped(mesh_rows, BF),) * 3,
        [
            v, middle, middle, v, v, v, square(0, 2), first_half(0, 0), first_half(0, 1), second_of(0),
            square(1, 0), square(1, 1),
        ],
        (
            own_sum, from_left, from_right, up, down, state, edge_square, node_first, node_first, node_second,
            edge_square, edge_square,
        ),
        flops=7 * mesh_flops,
        moved=4 << 20,
        name="node",
    )
    coarse_a, coarse_b = coarse_gather(proc_send[:COARSE_DEV])
    joined = (3 * MESH_NODES, WIDTH)
    near = [part.reshape(joined) for part in columns(proc_send)]
    fine = kernel_call(
        fine_body,
        shaped(mesh_rows, F32),
        [v, v, v, v, v, geom_of(1)],
        (m_edges, *near, proc_recv, geom),
        flops=2 * grid_flops,
        moved=3 << 20,
        name="fine",
    )
    lat, lon = lax.axis_index("lat"), lax.axis_index("lon")
    place = jnp.stack([lat // 2, lon // 4, (lat % 2) * 2 + (lon // 2) % 2, lon % 2, lat * LON + lon])[None]
    dec_send = kernel_call(
        mesh_body,
        shaped(mesh_rows, BF),
        [
            SMEM, v, v, v, v, v, v, v, v, geom_of(1), square(1, 2), first_half(1, 0), first_half(1, 1),
            second_of(1), square(2, 0),
        ],
        (
            place.astype(I32), fine, coarse_list, list_next, list_far, coarse_a, coarse_b, proc_recv, mesh_one, geom,
            edge_square, node_first, node_first, node_second, edge_square,
        ),
        flops=4 * grid_flops,
        moved=6 << 20,
        name="mesh",
    )
    near = [part.reshape(joined) for part in columns(dec_send)]
    outputs = kernel_call(
        decode_body,
        shaped((GRID_NODES, head.shape[1]), BF),
        [v, v, v, v, v, v, geom_of(2), square(2, 2), first_half(2, 1), v],
        (d_edges, *near, grid_recv, grid_base, geom, edge_square, node_first, head),
        flops=8 * grid_flops,
        moved=8 << 20,
        name="decode",
    )
    return outputs[None, None]


def solution(mesh):
    return jax.shard_map(
        per_device,
        mesh=mesh,
        in_specs=(
            P("lat", "lon", None, None),
            P("lat", "lon", None, None),
            P(),
            P(),
            P(),
            P(),
            P(),
            P(),
            P(),
            P("lat", "lon", None),
            P("lat", "lon", None),
            P("lat", "lon"),
            P("lat", "lon", None, None),
            P("lat", "lon", None),
            P("lat", "lon", None, None),
            P("lat", "lon", None),
            P("lat", "lon", None),
            P("lat", "lon", None, None),
            P("lat", "lon", None),
            P("lat", "lon", None, None),
        ),
        out_specs=P("lat", "lon", None, None),
        check_vma=False,
    )
```

```python
import functools

import jax
import jax.numpy as jnp
from jax import lax
from jax.experimental import pallas as pl
from jax.experimental.pallas import tpu as pltpu
from jax.sharding import PartitionSpec as P

BF = jnp.bfloat16
F32 = jnp.float32
I32 = jnp.int32
WIDTH = 512
GRID_NODES = 1024
MESH_NODES = 128
MESH_DEGREE = 6
GRID_DEGREE = 3
COARSE_DEV = 16
SLOTS = 2048
CHUNK = 512
CHUNKS = SLOTS // CHUNK
PAYLOAD = MESH_NODES + 16 * CHUNKS
LON = 16
NEAR_SLOTS = 160
COARSE_SLOTS = 320
GROUPS = (5, 3, 7, 0, 1, 2, 6, 4, 8)
VMEM_BYTES = 20 * 1024 * 1024


def mm(left, right):
    return jnp.dot(left, right, preferred_element_type=F32)


def mm_t(left, right):
    return lax.dot_general(left, right, (((0,), (0,)), ((), ())), preferred_element_type=F32)


def mm_nt(left, right):
    return lax.dot_general(left, right, (((1,), (1,)), ((), ())), preferred_element_type=F32)


def silu(v):
    half = 0.5 * v
    return half + half * jnp.tanh(half)


def one_hot(column, width):
    spots = lax.broadcasted_iota(I32, (column.shape[0], width), 1)
    return jnp.where(spots == column, 1.0, 0.0).astype(BF)


class Load:
    def __init__(self, index, shape):
        self.index, self.shape = index, shape


class View:
    def __init__(self, index):
        self.index = index


class Arriving:
    def __init__(self, copy, ref):
        self.copy, self.ref = copy, ref
        self.shape = ref.shape

    def ready(self):
        if self.copy is not None:
            self.copy.wait()
            self.copy = None
        return self.ref

    def __getitem__(self, index):
        return self.ready()[index]


V = pl.BlockSpec(memory_space=pltpu.VMEM)
SMEM = pl.BlockSpec(memory_space=pltpu.SMEM)
ANY = pl.BlockSpec(memory_space=pl.ANY)
HBM = pl.BlockSpec(memory_space=pltpu.HBM)


def square(block, kind):
    return Load((block, kind), (WIDTH, WIDTH))


def first_half(block, half):
    return Load((block, slice(WIDTH * half, WIDTH * (half + 1))), (WIDTH, WIDTH))


def second_of(block):
    return Load((block,), (WIDTH, WIDTH))


def kernel_call(body, outs, specs, args, scratch=(), flops=0, moved=0, name=None, out_specs=None):
    loads = [(k, spec, args[k].dtype) for k, spec in enumerate(specs) if isinstance(spec, Load)]
    n_in, n_loads = len(specs), len(loads)

    def run(*refs):
        given, rest = list(refs[:n_in]), list(refs[n_in:])
        if n_loads:
            sems = rest[-1]
            buffers = rest[-1 - n_loads : -1]
            rest = rest[: -1 - n_loads]
            for at, ((k, spec, _), buffer) in enumerate(zip(loads, buffers)):
                source = given[k].at[spec.index] if spec.index else given[k]
                copy = pltpu.make_async_copy(source, buffer, sems.at[at])
                copy.start()
                given[k] = Arriving(copy, buffer)
        for k, spec in enumerate(specs):
            if isinstance(spec, View):
                given[k] = given[k].at[spec.index]
        body(*given, *rest)
        for part in given:
            if isinstance(part, Arriving):
                part.ready()

    extra = [pltpu.VMEM(spec.shape, dtype) for _, spec, dtype in loads]
    if loads:
        extra.append(pltpu.SemaphoreType.DMA((n_loads,)))
    many = isinstance(outs, tuple)
    args = [
        pltpu.with_memory_space_constraint(arg, pltpu.HBM) if isinstance(spec, Load) else arg
        for spec, arg in zip(specs, args)
    ]
    return pl.pallas_call(
        run,
        out_shape=outs,
        in_specs=[HBM if isinstance(q, Load) else V if isinstance(q, View) else q for q in specs],
        out_specs=out_specs if out_specs is not None else (V,) * len(outs) if many else V,
        scratch_shapes=list(scratch) + extra,
        compiler_params=pltpu.CompilerParams(vmem_limit_bytes=VMEM_BYTES),
        cost_estimate=pl.CostEstimate(flops=flops, bytes_accessed=moved, transcendentals=0),
        name=name,
    )(*args)


def shaped(shape, dtype):
    return jax.ShapeDtypeStruct(shape, dtype)


def fill_list(scr, width, indices, geometry):
    for row, value in enumerate(indices):
        scr[row : row + 1, 0:width] = value.astype(F32)
    high = geometry.astype(BF).astype(F32)
    scr[4:8, 0:width] = high
    scr[8:12, 0:width] = geometry - high
    scr[12:16, 0:width] = high


def pack_body(count, senders, receivers, geometry, state, c_senders, c_receivers, c_geometry, out, c_out, scr):
    out[0:MESH_NODES, :] = state[...]
    for c in range(CHUNKS):
        cols = slice(c * CHUNK, (c + 1) * CHUNK)
        s = senders[:, cols]
        edge = lax.broadcasted_iota(I32, (1, CHUNK), 1) + c * CHUNK
        code = jnp.where(edge < count[0, 0], lax.shift_right_logical(s, 10) + 1, 0)
        local = s & (GRID_NODES - 1)
        fill_list(
            scr, CHUNK, (code, lax.shift_right_logical(local, 8), local & 255, receivers[:, cols]), geometry[:, cols]
        )
        out[MESH_NODES + 16 * c : MESH_NODES + 16 * (c + 1), :] = scr[...].astype(BF)
    s = c_senders[...]
    r = c_receivers[...]
    n = s.shape[1]
    fill_list(
        scr, n, (lax.shift_right_logical(s, 8), s & 255, lax.shift_right_logical(r, 4), r & 15), c_geometry[...]
    )
    c_out[...] = scr[:, 0:n].astype(BF)


def prep_body(m_senders, m_geometry, d_senders, d_geometry, weight, m_out, d_out, w_out, scr, turned):
    for senders, geometry, degree, out in (
        (m_senders, m_geometry, MESH_DEGREE, m_out),
        (d_senders, d_geometry, GRID_DEGREE, d_out),
    ):
        n = senders.shape[1]
        s = senders[...]
        near = lax.shift_right_logical(s, 7)
        spot = jnp.zeros_like(near)
        for place, group in enumerate(GROUPS):
            spot = jnp.where(near == place, group, spot)
        spot = spot * MESH_NODES + (s & (MESH_NODES - 1))
        zero = jnp.zeros((1, n), F32)
        fill_list(scr, n, (spot, zero, zero, zero), geometry[...])
        turned[0:n, :] = scr[:, 0:n].T
        for t in range(degree):
            out[t] = turned[pl.ds(t, n // degree, stride=degree), :]
    for k in range(3):
        w = weight[k]
        high = w.astype(BF).astype(F32)
        scr[0:4, 0:WIDTH] = jnp.zeros((4, WIDTH), F32)
        scr[4:8, 0:WIDTH] = high
        scr[8:12, 0:WIDTH] = high
        scr[12:16, 0:WIDTH] = w - high
        w_out[k] = scr[:, 0:WIDTH].astype(BF)


def embed_body(x, w_in, w_out, w_send, latent, send):
    for b in range(4):
        rows = slice(256 * b, 256 * (b + 1))
        hidden = silu(mm(x[rows, :], w_in[...])).astype(BF)
        lat = mm(hidden, w_out[...]).astype(BF)
        latent[rows, :] = lat
        send[rows, :] = mm(lat, w_send[...]).astype(BF)


def grid_body(latent, w_recv, w_first, recv, base):
    for b in range(4):
        rows = slice(256 * b, 256 * (b + 1))
        recv[rows, :] = mm(latent[rows, :], w_recv[...]).astype(BF)
        base[rows, :] = mm(latent[rows, :], w_first[...])


def self_body(payload, send, w_recv, w_geom, out, q):
    q[...] = mm(payload[0:MESH_NODES, :], w_recv[...]).astype(BF)
    out[...] = jnp.zeros_like(out)

    @pl.loop(0, CHUNKS)
    def _(c):
        rows = pl.ds(pl.multiple_of(MESH_NODES + 16 * c, 16), 16)
        d = payload[rows, :].astype(F32).T
        for h in range(2):
            part = d[256 * h : 256 * (h + 1), :]
            s = (part[:, 1:2] * 256.0 + part[:, 2:3]).astype(I32)
            r = jnp.where(part[:, 0:1] == 5.0, part[:, 3:4], -1.0).astype(I32)
            pick = one_hot(r, MESH_NODES)
            pre = mm(one_hot(s, GRID_NODES), send[...]) + mm(pick, q[...]) + mm(part.astype(BF), w_geom[...])
            out[...] += mm_t(pick, silu(pre).astype(BF))


def near_body(
    left, right, middle, left_pair, right_pair, send, w_recv, w_geom, order,
    o_left, o_right, o_middle, o_left_pair, o_right_pair, masks, ranks, q, edges, sums,
):
    lists = (
        (left, 5, o_left),
        (right, 3, o_right),
        (middle.at[0], 7, o_middle.at[0]),
        (middle.at[1], 1, o_middle.at[1]),
        (left_pair.at[0], 8, o_left_pair.at[0]),
        (left_pair.at[1], 2, o_left_pair.at[1]),
        (right_pair.at[0], 6, o_right_pair.at[0]),
        (right_pair.at[1], 0, o_right_pair.at[1]),
    )
    q[4 * MESH_NODES : 5 * MESH_NODES, :] = jnp.zeros((MESH_NODES, WIDTH), BF)

    def listed(src, c):
        return src[MESH_NODES + 16 * c : MESH_NODES + 16 * (c + 1), :]

    for i, (src, bucket, _) in enumerate(lists):
        q[MESH_NODES * bucket : MESH_NODES * (bucket + 1), :] = mm(src[0:MESH_NODES, :], w_recv[...]).astype(BF)
        for c in range(CHUNKS):
            row = i * CHUNKS + c
            code = listed(src, c).astype(F32)[0:1, :]
            masks[row : row + 1, :] = jnp.where(code == float(bucket + 1), 1.0, 0.0)
    n = masks.shape[0]
    mask = masks[...]
    before = lax.broadcasted_iota(I32, (CHUNK, CHUNK), 0) < lax.broadcasted_iota(I32, (CHUNK, CHUNK), 1)
    inside = mm(mask.astype(BF), jnp.where(before, 1.0, 0.0).astype(BF))
    mine = lax.broadcasted_iota(I32, (n, n), 0)
    other = lax.broadcasted_iota(I32, (n, n), 1)
    same = mine // CHUNKS == other // CHUNKS
    earlier = jnp.where((other < mine) & same, 1.0, 0.0).astype(BF)
    carried = mm(earlier, mask.astype(BF)).sum(axis=1, keepdims=True)
    ranks[...] = jnp.where(mask > 0.5, inside + carried, -1.0).astype(I32)

    slot = lax.broadcasted_iota(I32, (NEAR_SLOTS, CHUNK), 0)
    for i, (src, _, _) in enumerate(lists):
        d = jnp.zeros((NEAR_SLOTS, 16), F32)
        for c in range(CHUNKS):
            row = i * CHUNKS + c
            d += mm_nt(jnp.where(slot == ranks[row : row + 1, :], 1.0, 0.0).astype(BF), listed(src, c))
        edges[NEAR_SLOTS * i : NEAR_SLOTS * (i + 1), :] = d
    for j in range(4):
        d = edges[2 * NEAR_SLOTS * j : 2 * NEAR_SLOTS * (j + 1), :]
        s = (d[:, 1:2] * 256.0 + d[:, 2:3]).astype(I32)
        pre = mm(one_hot(s, GRID_NODES), send[...]) + mm(d.astype(BF), w_geom[...])
        r = jnp.where(d[:, 0:1] > 0.5, d[:, 3:4], -1.0).astype(I32)
        for h in range(2):
            bucket = lists[2 * j + h][1]
            part = slice(NEAR_SLOTS * h, NEAR_SLOTS * (h + 1))
            rows = slice(MESH_NODES * bucket, MESH_NODES * (bucket + 1))
            pick = one_hot(r[part, :], MESH_NODES)
            sums[rows, :] = mm_t(pick, silu(pre[part, :] + mm(pick, q[rows, :])).astype(BF))

    count = mm(jnp.where(same, 1.0, 0.0).astype(BF), mask.astype(BF)).sum(axis=1, keepdims=True)
    over = jnp.maximum(count - NEAR_SLOTS, 0.0)
    total = lax.shift_right_logical(jnp.sum(over).astype(I32), 2)

    @pl.when(total > 0)
    def _():
        across = lax.broadcasted_iota(I32, (n, 1), 0) // CHUNKS
        base = jnp.zeros((n, 1), F32)
        for i in range(len(lists) - 1):
            base += jnp.where(across > i, over[i * CHUNKS : i * CHUNKS + 1, :], 0.0)
        rank = ranks[...]
        ranks[...] = jnp.where(rank >= NEAR_SLOTS, rank - NEAR_SLOTS + base.astype(I32), -1)

        @pl.loop(0, lax.shift_right_logical(total + 127, 7))
        def _(k):
            late = lax.broadcasted_iota(I32, (128, CHUNK), 0) + k * 128
            d = jnp.zeros((128, 16), F32)
            for i, (src, _, _) in enumerate(lists):
                for c in range(CHUNKS):
                    row = i * CHUNKS + c
                    d += mm_nt(jnp.where(late == ranks[row : row + 1, :], 1.0, 0.0).astype(BF), listed(src, c))
            s = (d[:, 1:2] * 256.0 + d[:, 2:3]).astype(I32)
            code = d[:, 0:1]
            r = jnp.where(code > 0.5, (code - 1.0) * float(MESH_NODES) + d[:, 3:4], -1.0).astype(I32)
            pick = one_hot(r, 9 * MESH_NODES)
            pre = mm(one_hot(s, GRID_NODES), send[...]) + mm(pick, q[...]) + mm(d.astype(BF), w_geom[...])
            sums[...] += mm_t(pick, silu(pre).astype(BF))

    for _, bucket, dst in lists:
        dst[...] = sums[MESH_NODES * bucket : MESH_NODES * (bucket + 1), :].astype(BF)


def side_sum_body(middle, from_left, from_right, order, up, down):
    for k, out in ((0, up), (1, down)):
        total = middle[k].astype(F32) + from_left[k].astype(F32) + from_right[k].astype(F32)
        out[...] = total.astype(BF)


def join_body(parts, out):
    n = parts[0].shape[0]
    for k, part in enumerate(parts):
        out[n * k : n * (k + 1), :] = part[...]


def pair_body(up, down, order, out):
    out[0] = up[...]
    out[1] = down[...]


def four_body(a, b, c, d, out):
    join_body((a, b, c, d), out)


def four_pair_body(a, b, c, d, up, down, out, pair):
    join_body((a, b, c, d), out)
    pair[0] = up[...]
    pair[1] = down[...]


def split_mm(value, weight):
    high = value.astype(BF)
    low = (value - high.astype(F32)).astype(BF)
    return mm(high, weight) + mm(low, weight)


def node_rows(v, hidden_total, w_second, first_node, first_sum, second):
    m = split_mm(hidden_total, w_second).astype(BF)
    u = silu(mm(v, first_node) + mm(m, first_sum)).astype(BF)
    return (v.astype(F32) + mm(u, second)).astype(BF)


def node_body(
    own, from_left, from_right, up, down, state, w_second, first_node, first_sum, second, w_send, w_recv, order,
    mesh_one, send, recv,
):
    total = own[...] + from_left[...].astype(F32) + from_right[...].astype(F32)
    total = total + up[...].astype(F32) + down[...].astype(F32)
    one = node_rows(state[...], total, w_second[...], first_node[...], first_sum[...], second[...])
    mesh_one[...] = one
    send[...] = mm(one, w_send[...]).astype(BF)
    recv[...] = mm(one, w_recv[...]).astype(BF)


def near_groups(left, own, right, pair, left_pair, right_pair):
    pairs = (pair.at[0], pair.at[1], left_pair.at[0], left_pair.at[1], right_pair.at[0], right_pair.at[1])
    return (left, own, right) + pairs


def fine_body(edges, left, own, right, pair, left_pair, right_pair, recv, w_geom, out, rows):
    for k, part in enumerate(near_groups(left, own, right, pair, left_pair, right_pair)):
        rows[MESH_NODES * k : MESH_NODES * (k + 1), :] = part[...]
    rows[9 * MESH_NODES :, :] = jnp.zeros((MESH_NODES, WIDTH), BF)
    rows[9 * MESH_NODES : 9 * MESH_NODES + 16, :] = w_geom[...]
    q = recv[...].astype(F32)
    total = jnp.zeros((MESH_NODES, WIDTH), F32)
    for t in range(MESH_DEGREE):
        d = edges[t]
        spread = one_hot(d[:, 0:1].astype(I32), 9 * MESH_NODES)
        pre = q + mm(spread, rows[0 : 9 * MESH_NODES, :]) + mm(d.astype(BF), w_geom[...])
        total += silu(pre)
    out[...] = total


def coarse_prep_body(place, list_a, list_b, list_c, out, count, row):
    z, y, x, core, tile = (place[0, k] for k in range(5))
    n = list_a.shape[1]
    lists = (list_a, list_b, list_c)
    for k, edges in enumerate(lists):
        owner = edges[...].astype(F32)[2:3, :].astype(I32)
        row[k : k + 1, :] = jnp.where(owner == tile, 1.0, 0.0)
    row[3:8, :] = jnp.zeros((5, n), F32)
    mask = row[...]
    before = lax.broadcasted_iota(I32, (n, n), 0) < lax.broadcasted_iota(I32, (n, n), 1)
    inside = mm(mask.astype(BF), jnp.where(before, 1.0, 0.0).astype(BF))
    earlier = lax.broadcasted_iota(I32, (8, 8), 1) < lax.broadcasted_iota(I32, (8, 8), 0)
    carried = mm(jnp.where(earlier, 1.0, 0.0).astype(BF), mask.astype(BF)).sum(axis=1, keepdims=True)
    rank = jnp.where(mask > 0.5, inside + carried, -1.0).astype(I32)
    slot = lax.broadcasted_iota(I32, (3 * n, n), 0)
    d = jnp.zeros((3 * n, 16), F32)
    for k, edges in enumerate(lists):
        d += mm_nt(jnp.where(slot == rank[k : k + 1, :], 1.0, 0.0).astype(BF), edges[...])
    s = (d[:, 0:1] * 256.0 + d[:, 1:2]).astype(I32)
    t = lax.shift_right_logical(s, 4)
    lat = lax.shift_right_logical(t, 4)
    lon = t & 15
    gz = (z - lax.shift_right_logical(lat, 1)) & 3
    gy = (y - lax.shift_right_logical(lon, 2)) & 3
    gx = (x - ((lat & 1) * 2 + (lax.shift_right_logical(lon, 1) & 1))) & 3
    gc = (core + lon) & 1
    spot = (((gc * 4 + gx) * 4 + gy) * 4 + gz) * 16 + (s & 15)
    total = jnp.sum(mask).astype(I32)
    used = lax.broadcasted_iota(I32, (3 * n, 1), 0) < total
    r = jnp.where(used, d[:, 3:4], -1.0)
    lane = lax.broadcasted_iota(I32, (3 * n, 16), 1)
    out[...] = jnp.where(lane == 0, spot.astype(F32), jnp.where(lane == 1, r, d))
    count[0, 0] = total


def mesh_body(
    count, fine, edges, a0, a1, a2, a3, b0, b1, b2, b3, recv, mesh_one, w_geom, w_second, first_node, first_sum,
    second, w_send, send, rows, total,
):
    parts = (a0, a1, a2, a3, b0, b1, b2, b3)
    n = a0.shape[0]
    for k, part in enumerate(parts):
        rows[n * k : n * (k + 1), :] = part[...]
    q = recv[0:COARSE_DEV, :]

    def hidden_sum(d):
        pick = one_hot(d[:, 1:2].astype(I32), MESH_NODES)
        pre = mm(one_hot(d[:, 0:1].astype(I32), len(parts) * n), rows[...])
        pre += mm(pick[:, 0:COARSE_DEV], q) + mm(d.astype(BF), w_geom[...])
        return mm_t(pick, silu(pre).astype(BF))

    total[...] = fine[...] + hidden_sum(edges[0:COARSE_SLOTS, :])

    @pl.loop(COARSE_SLOTS // 64, lax.shift_right_logical(count[0, 0] + 63, 6))
    def _(k):
        total[...] += hidden_sum(edges[pl.ds(pl.multiple_of(64 * k, 64), 64), :])

    two = node_rows(mesh_one[...], total[...], w_second[...], first_node[...], first_sum[...], second[...])
    send[...] = mm(two, w_send[...]).astype(BF)


def decode_early_body(edges, left, own, right, pair, recv, w_geom, out, rows):
    for k, part in enumerate((left, own, right, pair.at[0], pair.at[1])):
        rows[MESH_NODES * k : MESH_NODES * (k + 1), :] = part[...]
    n = 5 * MESH_NODES
    rows[n : n + 128, :] = jnp.zeros((128, WIDTH), BF)
    rows[n : n + 16, :] = w_geom[...]

    @pl.loop(0, 4)
    def _(b):
        span = pl.ds(pl.multiple_of(256 * b, 256), 256)
        q = recv[span, :].astype(F32)
        for t in range(GRID_DEGREE):
            d = edges[t, span, :]
            spread = one_hot(d[:, 0:1].astype(I32), n)
            out[t, span, :] = q + mm(spread, rows[0:n, :]) + mm(d.astype(BF), w_geom[...])


def decode_body(edges, early, left_pair, right_pair, base, w_second, first_sum, head, out, rows):
    w_second, first_sum = w_second.ready(), first_sum.ready()
    for k, part in enumerate((left_pair.at[0], left_pair.at[1], right_pair.at[0], right_pair.at[1])):
        rows[MESH_NODES * k : MESH_NODES * (k + 1), :] = part[...]

    @pl.loop(0, 4)
    def _(b):
        span = pl.ds(pl.multiple_of(256 * b, 256), 256)
        total = jnp.zeros((256, WIDTH), F32)
        for t in range(GRID_DEGREE):
            spot = edges[t, span, :][:, 0:1].astype(I32) - 5 * MESH_NODES
            total += silu(early[t, span, :] + mm(one_hot(spot, 4 * MESH_NODES), rows[...]))
        summed = mm(total.astype(BF), w_second[...]).astype(BF)
        hidden = silu(base[span, :] + mm(summed, first_sum[...])).astype(BF)
        out[:, span] = mm_nt(head[...], hidden).astype(BF)


def shift(value, axis, step, periodic):
    n = lax.axis_size(axis)
    pairs = [(i, (i + step) % n) for i in range(n) if periodic or 0 <= i + step < n]
    return lax.ppermute(value, axis, pairs)


def first_stage(value):
    up = shift(value, "lat", 1, False)
    down = shift(value, "lat", -1, False)
    return up, down, shift(value, "lon", 1, True), shift(value, "lon", -1, True)


def second_stage(pair):
    return shift(pair, "lon", 1, True), shift(pair, "lon", -1, True)


def along_z(s):
    return [(i, ((i // 2 + s) % 4) * 2 + i % 2) for i in range(8)]


def along_y(s):
    return [(i, ((i // 4 + s) % 4) * 4 + i % 4) for i in range(16)]


def along_x(s):
    pairs = []
    for lat in range(8):
        for lon in range(16):
            x = ((lat % 2) * 2 + (lon // 2) % 2 + s) % 4
            to_lat = lat // 2 * 2 + x // 2
            to_lon = lon // 4 * 4 + (x % 2) * 2 + lon % 2
            pairs.append((lat * 16 + lon, to_lat * 16 + to_lon))
    return pairs


def four(value, axis, pairs_of):
    return [value] + [lax.ppermute(value, axis, pairs_of(s)) for s in (1, 2, 3)]


def per_device(
    grid_inputs,
    mesh_state,
    embed_in,
    embed_out,
    edge_square,
    edge_geom_weight,
    node_first,
    node_second,
    head,
    g2m_senders,
    g2m_receivers,
    g2m_counts,
    g2m_geom,
    mesh_senders,
    mesh_geom,
    coarse_senders,
    coarse_receivers,
    coarse_geom,
    m2g_senders,
    m2g_geom,
):
    mesh_rows = (MESH_NODES, WIDTH)
    grid_rows = (GRID_NODES, WIDTH)
    pair_rows = (2,) + mesh_rows
    grid_flops = 2 * GRID_NODES * WIDTH * WIDTH
    mesh_flops = grid_flops // 8
    both = ("lat", "lon")
    tiles = lax.axis_size(both)
    lat, lon = lax.axis_index("lat"), lax.axis_index("lon")
    place = jnp.stack([lat // 2, lon // 4, (lat % 2) * 2 + (lon // 2) % 2, lon % 2, lat * LON + lon])[None]

    pack_args = (
        g2m_senders, g2m_receivers, g2m_geom, mesh_state, coarse_senders, coarse_receivers, coarse_geom
    )

    def part_of(array):
        n = array.ndim - 2
        return Load((0,) if n == 1 else (0, 0), array.shape[1:] if n == 1 else array.shape[2:])

    payload, coarse_list = kernel_call(
        pack_body,
        (shaped((PAYLOAD, WIDTH), BF), shaped((16, coarse_senders.shape[2]), BF)),
        [SMEM] + [part_of(a) for a in pack_args],
        (g2m_counts,) + pack_args,
        [pltpu.VMEM((16, CHUNK), F32)],
        name="pack",
    )
    up, down, near_left, near_right = first_stage(payload)
    prep_args = (mesh_senders, mesh_geom, m2g_senders, m2g_geom)
    m_edges, d_edges, geom = kernel_call(
        prep_body,
        (
            shaped((MESH_DEGREE, MESH_NODES, 16), F32),
            shaped((GRID_DEGREE, GRID_NODES, 16), F32),
            shaped((3, 16, WIDTH), BF),
        ),
        [part_of(a) for a in prep_args] + [Load((), edge_geom_weight.shape)],
        prep_args + (edge_geom_weight,),
        [pltpu.VMEM((16, 3072), F32), pltpu.VMEM((3072, 16), F32)],
        flops=grid_flops,
        name="prep",
    )
    latent, grid_send = kernel_call(
        embed_body,
        (shaped(grid_rows, BF), shaped(grid_rows, BF)),
        [V, Load((), embed_in.shape), Load((), embed_out.shape), square(0, 0)],
        (grid_inputs[0, 0], embed_in, embed_out, edge_square),
        flops=3 * grid_flops,
        moved=5 << 20,
        name="embed",
    )

    def geom_of(k):
        return View(k)

    def paired(up, down, order):
        shape = (2,) + up.shape
        return kernel_call(pair_body, shaped(shape, BF), [V, V, ANY], (up, down, order), name="pair")

    near_middle = paired(up, down, grid_send)
    near_left_pair, near_right_pair = second_stage(near_middle)
    own_sum = kernel_call(
        self_body,
        shaped(mesh_rows, F32),
        [V, V, square(0, 1), geom_of(0)],
        (payload, grid_send, edge_square, geom),
        [pltpu.VMEM(mesh_rows, BF)],
        flops=5 * grid_flops,
        moved=3 << 20,
        name="own",
    )
    to_left, to_right, to_middle, to_left_pair, to_right_pair = kernel_call(
        near_body,
        (shaped(mesh_rows, BF),) * 2 + (shaped(pair_rows, BF),) * 3,
        [V, V, V, V, V, V, square(0, 1), geom_of(0), ANY],
        (near_left, near_right, near_middle, near_left_pair, near_right_pair, grid_send, edge_square, geom, own_sum),
        [
            pltpu.VMEM((8 * CHUNKS, CHUNK), F32),
            pltpu.VMEM((8 * CHUNKS, CHUNK), I32),
            pltpu.VMEM((9 * MESH_NODES, WIDTH), BF),
            pltpu.VMEM((8 * NEAR_SLOTS, 16), F32),
            pltpu.VMEM((9 * MESH_NODES, WIDTH), F32),
        ],
        flops=4 * grid_flops,
        moved=5 << 20,
        name="near",
    )
    pair_left = shift(to_right_pair, "lon", 1, True)
    pair_right = shift(to_left_pair, "lon", -1, True)
    list_next = lax.ppermute(coarse_list, both, [(t, (t - 1) % tiles) for t in range(tiles)])
    list_far = lax.ppermute(coarse_list, both, [(t, (t + tiles // 2) % tiles) for t in range(tiles)])
    grid_recv, grid_base = kernel_call(
        grid_body,
        (shaped(grid_rows, BF), shaped(grid_rows, F32)),
        [V, square(2, 1), first_half(2, 0)],
        (latent, edge_square, node_first),
        flops=2 * grid_flops,
        moved=5 << 20,
        name="grid",
    )
    to_up, to_down = kernel_call(
        side_sum_body,
        (shaped(mesh_rows, BF),) * 2,
        [V, V, V, ANY],
        (to_middle, pair_left, pair_right, grid_recv),
        name="sides",
    )
    from_left = shift(to_right, "lon", 1, True)
    from_right = shift(to_left, "lon", -1, True)
    down = shift(to_up, "lat", -1, False)
    up = shift(to_down, "lat", 1, False)
    edge_total = 3 * coarse_list.shape[1]
    c_edges, c_count = kernel_call(
        coarse_prep_body,
        (shaped((edge_total, 16), F32), shaped((1, 1), I32)),
        [SMEM, V, V, V],
        (place.astype(I32), coarse_list, list_next, list_far),
        [pltpu.VMEM((8, coarse_list.shape[1]), F32)],
        flops=mesh_flops,
        name="coarse_edges",
        out_specs=(V, SMEM),
    )
    mesh_one, proc_send, proc_recv = kernel_call(
        node_body,
        (shaped(mesh_rows, BF),) * 3,
        [
            V, V, V, V, V, part_of(mesh_state), square(0, 2), first_half(0, 0), first_half(0, 1), second_of(0),
            square(1, 0), square(1, 1), ANY,
        ],
        (
            own_sum, from_left, from_right, up, down, mesh_state, edge_square, node_first, node_first, node_second,
            edge_square, edge_square, c_edges,
        ),
        flops=7 * mesh_flops,
        moved=4 << 20,
        name="node",
    )
    quarter = four(proc_send[:COARSE_DEV], "lat", along_z)
    rows = kernel_call(four_body, shaped((4 * COARSE_DEV, WIDTH), BF), [V] * 4, quarter, name="join_z")
    quarter = four(rows, "lon", along_y)
    up, down, left, right = first_stage(proc_send)
    rows, pair = kernel_call(
        four_pair_body,
        (shaped((16 * COARSE_DEV, WIDTH), BF), shaped(pair_rows, BF)),
        [V] * 6,
        (*quarter, up, down),
        name="join_y",
    )
    quarter = four(rows, both, along_x)
    left_pair, right_pair = second_stage(pair)
    across = [lax.ppermute(part, "lon", [(i, i ^ 1) for i in range(LON)]) for part in quarter]
    fine = kernel_call(
        fine_body,
        shaped(mesh_rows, F32),
        [V] * 8 + [geom_of(1)],
        (m_edges, left, proc_send, right, pair, left_pair, right_pair, proc_recv, geom),
        [pltpu.VMEM((10 * MESH_NODES, WIDTH), BF)],
        flops=2 * grid_flops,
        moved=3 << 20,
        name="fine",
    )
    dec_send = kernel_call(
        mesh_body,
        shaped(mesh_rows, BF),
        [SMEM] + [V] * 12
        + [geom_of(1), square(1, 2), first_half(1, 0), first_half(1, 1), second_of(1), square(2, 0)],
        (
            c_count, fine, c_edges, *quarter, *across, proc_recv, mesh_one, geom,
            edge_square, node_first, node_first, node_second, edge_square,
        ),
        [pltpu.VMEM((128 * COARSE_DEV, WIDTH), BF), pltpu.VMEM(mesh_rows, F32)],
        flops=4 * grid_flops,
        moved=6 << 20,
        name="mesh",
    )
    up, down, left, right = first_stage(dec_send)
    pair = paired(up, down, dec_send)
    left_pair, right_pair = second_stage(pair)
    early = kernel_call(
        decode_early_body,
        shaped((GRID_DEGREE,) + grid_rows, F32),
        [V, V, V, V, V, V, geom_of(2)],
        (d_edges, left, dec_send, right, pair, grid_recv, geom),
        [pltpu.VMEM((6 * MESH_NODES, WIDTH), BF)],
        flops=4 * grid_flops,
        moved=8 << 20,
        name="early",
    )
    outputs = kernel_call(
        decode_body,
        shaped((head.shape[1], GRID_NODES), BF),
        [V, V, V, V, V, square(2, 2), first_half(2, 1), V],
        (d_edges, early, left_pair, right_pair, grid_base, edge_square, node_first, head.T),
        [pltpu.VMEM((4 * MESH_NODES, WIDTH), BF)],
        flops=5 * grid_flops,
        moved=8 << 20,
        name="decode",
    )
    return outputs.T[None, None]


def solution(mesh):
    return jax.shard_map(
        per_device,
        mesh=mesh,
        in_specs=(
            P("lat", "lon", None, None),
            P("lat", "lon", None, None),
            P(),
            P(),
            P(),
            P(),
            P(),
            P(),
            P(),
            P("lat", "lon", None),
            P("lat", "lon", None),
            P("lat", "lon"),
            P("lat", "lon", None, None),
            P("lat", "lon", None),
            P("lat", "lon", None, None),
            P("lat", "lon", None),
            P("lat", "lon", None),
            P("lat", "lon", None, None),
            P("lat", "lon", None),
            P("lat", "lon", None, None),
        ),
        out_specs=P("lat", "lon", None, None),
        check_vma=False,
    )
```

```python
import functools

import jax
import jax.numpy as jnp
from jax import lax
from jax.experimental import pallas as pl
from jax.experimental.pallas import tpu as pltpu
from jax.sharding import PartitionSpec as P

BF = jnp.bfloat16
F32 = jnp.float32
I32 = jnp.int32
WIDTH = 512
GRID_NODES = 1024
MESH_NODES = 128
MESH_DEGREE = 6
GRID_DEGREE = 3
COARSE_DEV = 16
SLOTS = 2048
CHUNK = 512
CHUNKS = SLOTS // CHUNK
LISTED = MESH_NODES + 8 * CHUNKS
PAYLOAD = LISTED + 16
COARSE_EDGES = 256
LON = 16
NEAR_SLOTS = 160
COARSE_SLOTS = 320
GROUPS = (5, 3, 7, 0, 1, 2, 6, 4, 8)
VMEM_BYTES = 14 * 1024 * 1024


def mm(left, right):
    return jnp.dot(left, right, preferred_element_type=F32)


def mm_t(left, right):
    return lax.dot_general(left, right, (((0,), (0,)), ((), ())), preferred_element_type=F32)


def mm_nt(left, right):
    return lax.dot_general(left, right, (((1,), (1,)), ((), ())), preferred_element_type=F32)


def silu(v):
    half = 0.5 * v
    return half + half * jnp.tanh(half)


def one_hot(column, width):
    spots = lax.broadcasted_iota(I32, (column.shape[0], width), 1)
    return jnp.where(spots == column, 1.0, 0.0).astype(BF)


class Load:
    def __init__(self, index, shape):
        self.index, self.shape = index, shape


class View:
    def __init__(self, index):
        self.index = index


class Arriving:
    def __init__(self, copy, ref):
        self.copy, self.ref = copy, ref
        self.shape = ref.shape

    def ready(self):
        if self.copy is not None:
            self.copy.wait()
            self.copy = None
        return self.ref

    def __getitem__(self, index):
        return self.ready()[index]


V = pl.BlockSpec(memory_space=pltpu.VMEM)
SMEM = pl.BlockSpec(memory_space=pltpu.SMEM)
ANY = pl.BlockSpec(memory_space=pl.ANY)
HBM = pl.BlockSpec(memory_space=pltpu.HBM)


def square(block, kind):
    return Load((block, kind), (WIDTH, WIDTH))


def first_half(block, half):
    return Load((block, slice(WIDTH * half, WIDTH * (half + 1))), (WIDTH, WIDTH))


def second_of(block):
    return Load((block,), (WIDTH, WIDTH))


KEPT = (
    ("square", square(0, 2)), ("first", first_half(0, 0)), ("first", first_half(0, 1)), ("second", second_of(0)),
    ("square", square(1, 0)), ("square", square(1, 1)), ("square", square(1, 2)), ("first", first_half(1, 0)),
    ("first", first_half(1, 1)), ("second", second_of(1)), ("square", square(2, 0)), ("square", square(2, 2)),
    ("first", first_half(2, 1)),
)
ENCODER = (square(0, 0), square(0, 1))


def kernel_call(body, outs, specs, args, scratch=(), flops=0, moved=0, name=None, out_specs=None):
    loads = [(k, spec, args[k].dtype) for k, spec in enumerate(specs) if isinstance(spec, Load)]
    n_in, n_loads = len(specs), len(loads)

    def run(*refs):
        given, rest = list(refs[:n_in]), list(refs[n_in:])
        if n_loads:
            sems = rest[-1]
            buffers = rest[-1 - n_loads : -1]
            rest = rest[: -1 - n_loads]
            for at, ((k, spec, _), buffer) in enumerate(zip(loads, buffers)):
                source = given[k].at[spec.index] if spec.index else given[k]
                copy = pltpu.make_async_copy(source, buffer, sems.at[at])
                copy.start()
                given[k] = Arriving(copy, buffer)
        for k, spec in enumerate(specs):
            if isinstance(spec, View):
                given[k] = given[k].at[spec.index]
        body(*given, *rest)
        for part in given:
            if isinstance(part, Arriving):
                part.ready()

    extra = [pltpu.VMEM(spec.shape, dtype) for _, spec, dtype in loads]
    if loads:
        extra.append(pltpu.SemaphoreType.DMA((n_loads,)))
    many = isinstance(outs, tuple)
    args = [
        pltpu.with_memory_space_constraint(arg, pltpu.HBM) if spec is HBM or isinstance(spec, Load) else arg
        for spec, arg in zip(specs, args)
    ]
    return pl.pallas_call(
        run,
        out_shape=outs,
        in_specs=[HBM if isinstance(q, Load) else V if isinstance(q, View) else q for q in specs],
        out_specs=out_specs if out_specs is not None else (V,) * len(outs) if many else V,
        scratch_shapes=list(scratch) + extra,
        compiler_params=pltpu.CompilerParams(vmem_limit_bytes=VMEM_BYTES),
        cost_estimate=pl.CostEstimate(flops=flops, bytes_accessed=moved, transcendentals=0),
        name=name,
    )(*args)


def shaped(shape, dtype):
    return jax.ShapeDtypeStruct(shape, dtype)


def fill_list(scr, width, indices, geometry):
    for row, value in enumerate(indices):
        scr[row : row + 1, 0:width] = value.astype(F32)
    high = geometry.astype(BF).astype(F32)
    scr[4:8, 0:width] = high
    scr[8:12, 0:width] = geometry - high
    scr[12:16, 0:width] = high


def pack_body(
    count, senders, receivers, geometry, state, c_senders, c_receivers, c_geometry, weight,
    out, own, coarse, w_out, scr, short,
):
    for c in range(CHUNKS):
        cols = slice(c * CHUNK, (c + 1) * CHUNK)
        s = senders[:, cols]
        edge = lax.broadcasted_iota(I32, (1, CHUNK), 1) + c * CHUNK
        code = jnp.where(edge < count[0, 0], lax.shift_right_logical(s, 10) + 1, 0)
        local = s & (GRID_NODES - 1)
        fill_list(
            scr, CHUNK, (code, lax.shift_right_logical(local, 8), local & 255, receivers[:, cols]), geometry[:, cols]
        )
        own[16 * c : 16 * (c + 1), :] = scr[...].astype(BF)
        short[8 * c : 8 * (c + 1), :] = scr[0:8, :]
    out[MESH_NODES:LISTED, :] = short[...].astype(BF)
    s = c_senders[...]
    r = c_receivers[...]
    n = s.shape[1]
    fill_list(
        scr, n, (lax.shift_right_logical(s, 8), s & 255, lax.shift_right_logical(r, 4), r & 15), c_geometry[...]
    )
    out[LISTED:PAYLOAD, :] = scr[...].astype(BF)
    coarse[...] = scr[:, 0:n].astype(BF)
    zero = jnp.zeros((4, WIDTH), F32)
    for k in range(3):
        w = weight[k]
        high = w.astype(BF).astype(F32)
        scr[0:4, :] = zero
        scr[4:8, :] = high
        scr[8:12, :] = high
        scr[12:16, :] = w - high
        w_out[k] = scr[...].astype(BF)
        if k == 0:
            scr[8:12, :] = zero
            w_out[3] = scr[...].astype(BF)
    out[0:MESH_NODES, :] = state[...]


def prep_body(m_senders, m_geometry, d_senders, d_geometry, order, *refs):
    n = len(KEPT)
    sources, (m_out, d_out), kept, (scr, turned, sems) = refs[:n], refs[n : n + 2], refs[n + 2 : -3], refs[-3:]
    copies = bring(sources, [load for _, load in KEPT], kept, sems)
    for senders, geometry, degree, out in (
        (m_senders, m_geometry, MESH_DEGREE, m_out),
        (d_senders, d_geometry, GRID_DEGREE, d_out),
    ):
        n = senders.shape[1]
        s = senders[...]
        near = lax.shift_right_logical(s, 7)
        spot = jnp.zeros_like(near)
        for place, group in enumerate(GROUPS):
            spot = jnp.where(near == place, group, spot)
        spot = spot * MESH_NODES + (s & (MESH_NODES - 1))
        zero = jnp.zeros((1, n), F32)
        fill_list(scr, n, (spot, zero, zero, zero), geometry[...])
        turned[0:n, :] = scr[:, 0:n].T
        for t in range(degree):
            out[t] = turned[pl.ds(t, n // degree, stride=degree), :]
    for copy in copies:
        copy.wait()


def embed_body(x, w_in, w_out, source, source_too, latent, w_send, w_recv, sems):
    copies = bring((source, source_too), ENCODER, (w_send, w_recv), sems)
    for b in range(4):
        rows = slice(256 * b, 256 * (b + 1))
        hidden = silu(mm(x[rows, :], w_in[...])).astype(BF)
        latent[rows, :] = mm(hidden, w_out[...]).astype(BF)
    for copy in copies:
        copy.wait()


def send_body(latent, w_send, order, order_too, send):
    for b in range(4):
        rows = slice(256 * b, 256 * (b + 1))
        send[rows, :] = mm(latent[rows, :], w_send[...]).astype(BF)


def grid_body(latent, w_recv, w_first, order, recv, base):
    for b in range(4):
        rows = slice(256 * b, 256 * (b + 1))
        recv[rows, :] = mm(latent[rows, :], w_recv[...]).astype(BF)
        base[rows, :] = mm(latent[rows, :], w_first[...])


def bring(sources, loads, outs, sems):
    copies = []
    for k, load in enumerate(loads):
        copies.append(pltpu.make_async_copy(sources[k].at[load.index], outs[k], sems.at[k]))
        copies[-1].start()
    return copies


def self_body(state, listed, send, w_recv, w_geom, out):
    total = jnp.zeros((MESH_NODES, WIDTH), F32)
    q = None
    for c in range(CHUNKS):
        d = listed[16 * c : 16 * (c + 1), :].astype(F32).T
        s = (d[:, 1:2] * 256.0 + d[:, 2:3]).astype(I32)
        r = jnp.where(d[:, 0:1] == 5.0, d[:, 3:4], -1.0).astype(I32)
        pick = one_hot(r, MESH_NODES)
        pre = mm(one_hot(s, GRID_NODES), send[...]) + mm(d.astype(BF), w_geom[...])
        if q is None:
            q = mm(state[...], w_recv[...]).astype(BF)
        total += mm_t(pick, silu(pre + mm(pick, q)).astype(BF))
    out[...] = total


def near_body(buckets, place, *refs):
    sources, refs = refs[: len(buckets)], refs[len(buckets) :]
    if len(refs) == 16:
        beside, order_first, order_last, *refs = refs
    send, w_recv, w_geom, *refs = refs
    outs, refs = refs[: len(buckets)], refs[len(buckets) :]
    if len(refs) == 6 and buckets[0] != 5:
        following, *refs = refs
        n = COARSE_EDGES
        last = (place[0, 4] & (LON - 1)) == LON - 1
        following[...] = jnp.where(
            last, sources[-1][LISTED:PAYLOAD, 0:n].astype(F32), beside[...].astype(F32)
        ).astype(BF)
    if len(buckets) == 4 and buckets[0] == 5:
        following, *refs = refs
        following[...] = sources[1][LISTED:PAYLOAD, 0:COARSE_EDGES]
    masks, ranks, q, edges, sums = refs
    last = lax.shift_right_logical(place[0, 4], 4) == 7
    lists = tuple(zip(sources, buckets, outs))
    q[...] = jnp.zeros_like(q)

    def listed(src, c):
        return src[MESH_NODES:LISTED, :].astype(F32)[8 * c : 8 * (c + 1), :]

    def geometry_part(d):
        return mm(jnp.concatenate([d, d], axis=1).astype(BF), w_geom[...])

    for i, (src, bucket, _) in enumerate(lists):
        for c in range(CHUNKS):
            row = i * CHUNKS + c
            code = listed(src, c)[0:1, :]
            wanted = jnp.where(last, -1.0, float(bucket + 1)) if bucket < 3 else float(bucket + 1)
            masks[row : row + 1, :] = jnp.where(code == wanted, 1.0, 0.0)
    n = masks.shape[0]
    mask = masks[...]
    before = lax.broadcasted_iota(I32, (CHUNK, CHUNK), 0) < lax.broadcasted_iota(I32, (CHUNK, CHUNK), 1)
    inside = mm(mask.astype(BF), jnp.where(before, 1.0, 0.0).astype(BF))
    mine = lax.broadcasted_iota(I32, (n, n), 0)
    other = lax.broadcasted_iota(I32, (n, n), 1)
    same = mine // CHUNKS == other // CHUNKS
    earlier = jnp.where((other < mine) & same, 1.0, 0.0).astype(BF)
    carried = mm(earlier, mask.astype(BF)).sum(axis=1, keepdims=True)
    ranks[...] = jnp.where(mask > 0.5, inside + carried, -1.0).astype(I32)

    slot = lax.broadcasted_iota(I32, (NEAR_SLOTS, CHUNK), 0)
    for i, (src, _, _) in enumerate(lists):
        d = jnp.zeros((NEAR_SLOTS, 8), F32)
        for c in range(CHUNKS):
            row = i * CHUNKS + c
            d += mm_nt(jnp.where(slot == ranks[row : row + 1, :], 1.0, 0.0).astype(BF), listed(src, c).astype(BF))
        edges[NEAR_SLOTS * i : NEAR_SLOTS * (i + 1), :] = d
    for src, bucket, _ in lists:
        q[MESH_NODES * bucket : MESH_NODES * (bucket + 1), :] = mm(src[0:MESH_NODES, :], w_recv[...]).astype(BF)
    for j in range(len(lists) // 2):
        d = edges[2 * NEAR_SLOTS * j : 2 * NEAR_SLOTS * (j + 1), :]
        s = (d[:, 1:2] * 256.0 + d[:, 2:3]).astype(I32)
        pre = mm(one_hot(s, GRID_NODES), send[...]) + geometry_part(d)
        r = jnp.where(d[:, 0:1] > 0.5, d[:, 3:4], -1.0).astype(I32)
        for h in range(2):
            bucket = lists[2 * j + h][1]
            part = slice(NEAR_SLOTS * h, NEAR_SLOTS * (h + 1))
            rows = slice(MESH_NODES * bucket, MESH_NODES * (bucket + 1))
            pick = one_hot(r[part, :], MESH_NODES)
            sums[rows, :] = mm_t(pick, silu(pre[part, :] + mm(pick, q[rows, :])).astype(BF))

    count = mm(jnp.where(same, 1.0, 0.0).astype(BF), mask.astype(BF)).sum(axis=1, keepdims=True)
    over = jnp.maximum(count - NEAR_SLOTS, 0.0)
    total = lax.shift_right_logical(jnp.sum(over).astype(I32), 2)

    @pl.when(total > 0)
    def _():
        across = lax.broadcasted_iota(I32, (n, 1), 0) // CHUNKS
        base = jnp.zeros((n, 1), F32)
        for i in range(len(lists) - 1):
            base += jnp.where(across > i, over[i * CHUNKS : i * CHUNKS + 1, :], 0.0)
        rank = ranks[...]
        ranks[...] = jnp.where(rank >= NEAR_SLOTS, rank - NEAR_SLOTS + base.astype(I32), -1)

        @pl.loop(0, lax.shift_right_logical(total + 127, 7))
        def _(k):
            late = lax.broadcasted_iota(I32, (128, CHUNK), 0) + k * 128
            d = jnp.zeros((128, 8), F32)
            for i, (src, _, _) in enumerate(lists):
                for c in range(CHUNKS):
                    row = i * CHUNKS + c
                    d += mm_nt(jnp.where(late == ranks[row : row + 1, :], 1.0, 0.0).astype(BF), listed(src, c).astype(BF))
            s = (d[:, 1:2] * 256.0 + d[:, 2:3]).astype(I32)
            code = d[:, 0:1]
            r = jnp.where(code > 0.5, (code - 1.0) * float(MESH_NODES) + d[:, 3:4], -1.0).astype(I32)
            pick = one_hot(r, 9 * MESH_NODES)
            pre = mm(one_hot(s, GRID_NODES), send[...]) + mm(pick, q[...]) + geometry_part(d)
            sums[...] += mm_t(pick, silu(pre).astype(BF))

    for _, bucket, dst in lists:
        dst[...] = sums[MESH_NODES * bucket : MESH_NODES * (bucket + 1), :].astype(BF)


def corner_body(a, b, c, d, left, right):
    left[0] = a[...]
    left[1] = b[...]
    right[0] = c[...]
    right[1] = d[...]


def side_sum_body(above, below, from_left, from_right, left, right, order, up, down, o_left, o_right):
    for k, middle, out in ((0, above, up), (1, below, down)):
        total = middle[...].astype(F32) + from_left[k].astype(F32) + from_right[k].astype(F32)
        out[...] = total.astype(BF)
    o_left[...] = left[...]
    o_right[...] = right[...]


def join_body(parts, out):
    n = parts[0].shape[0]
    for k, part in enumerate(parts):
        out[n * k : n * (k + 1), :] = part[...]


def pair_body(up, down, order, out):
    out[0] = up[...]
    out[1] = down[...]


def partner_body(own, partner, coarse, order, near, far):
    near[0:MESH_NODES, :] = partner[...]
    near[MESH_NODES : MESH_NODES + COARSE_DEV, :] = own[0:COARSE_DEV, :]
    far[0:COARSE_DEV, :] = own[0:COARSE_DEV, :]
    far[COARSE_DEV : 2 * COARSE_DEV, :] = partner[0:COARSE_DEV, :]
    far[2 * COARSE_DEV : 3 * COARSE_DEV, :] = jnp.zeros((COARSE_DEV, WIDTH), BF)
    far[2 * COARSE_DEV : 3 * COARSE_DEV, 0:COARSE_EDGES] = coarse[...]


def bands_body(own, partner, below, across, above, coarse):
    n = COARSE_DEV
    coarse[0:n, :] = own[0:n, :]
    coarse[n : 2 * n, :] = partner[0:n, :]
    coarse[2 * n : 3 * n, :] = below[MESH_NODES : MESH_NODES + n, :]
    coarse[3 * n : 4 * n, :] = below[0:n, :]
    coarse[4 * n : 6 * n, :] = across[0 : 2 * n, :]
    coarse[6 * n : 7 * n, :] = above[MESH_NODES : MESH_NODES + n, :]
    coarse[7 * n : 8 * n, :] = above[0:n, :]


def both_body(place, a, b, own, partner, below, above, out, triple):
    join_body((a, b), out)
    triple[1] = own[...]
    odd = place[0, 2] >= 2

    @pl.when(odd)
    def _():
        triple[0] = partner[...]
        triple[2] = above[0:MESH_NODES, :]

    @pl.when(jnp.logical_not(odd))
    def _():
        triple[0] = below[0:MESH_NODES, :]
        triple[2] = partner[...]


def split_mm(value, weight):
    high = value.astype(BF)
    low = (value - high.astype(F32)).astype(BF)
    return mm(high, weight) + mm(low, weight)


def node_rows(v, hidden_total, w_second, first_node, first_sum, second):
    m = split_mm(hidden_total, w_second).astype(BF)
    u = silu(mm(v, first_node) + mm(m, first_sum)).astype(BF)
    return (v.astype(F32) + mm(u, second)).astype(BF)


def node_body(
    own, from_left, from_right, up, down, state, w_second, first_node, first_sum, second, w_send, w_recv,
    mesh_one, send, recv,
):
    total = own[...] + from_left[...].astype(F32) + from_right[...].astype(F32)
    total = total + up[...].astype(F32) + down[...].astype(F32)
    one = node_rows(state[...], total, w_second[...], first_node[...], first_sum[...], second[...])
    mesh_one[...] = one
    send[...] = mm(one, w_send[...]).astype(BF)
    recv[...] = mm(one, w_recv[...]).astype(BF)


def fine_body(edges, left, own, right, recv, w_geom, order, order_too, out, rows):
    parts = (left[1], own[1], right[1], own[0], own[2], left[0], left[2], right[0], right[2])
    for k, part in enumerate(parts):
        rows[MESH_NODES * k : MESH_NODES * (k + 1), :] = part
    q = recv[...].astype(F32)
    total = jnp.zeros((MESH_NODES, WIDTH), F32)
    for t in range(MESH_DEGREE):
        d = edges[t]
        spread = one_hot(d[:, 0:1].astype(I32), 9 * MESH_NODES)
        pre = q + mm(spread, rows[...]) + mm(d.astype(BF), w_geom[...])
        total += silu(pre)
    out[...] = total


def coarse_prep_body(place, own, following, far, out, count, row):
    z, y, x, core, tile = (place[0, k] for k in range(5))
    n = COARSE_EDGES
    lists = (own[...], following[...], far[2 * COARSE_DEV : 3 * COARSE_DEV, 0:n])
    for k, edges in enumerate(lists):
        owner = edges.astype(F32)[2:3, :].astype(I32)
        row[k : k + 1, :] = jnp.where(owner == tile, 1.0, 0.0)
    row[3:8, :] = jnp.zeros((5, n), F32)
    mask = row[...]
    before = lax.broadcasted_iota(I32, (n, n), 0) < lax.broadcasted_iota(I32, (n, n), 1)
    inside = mm(mask.astype(BF), jnp.where(before, 1.0, 0.0).astype(BF))
    earlier = lax.broadcasted_iota(I32, (8, 8), 1) < lax.broadcasted_iota(I32, (8, 8), 0)
    carried = mm(jnp.where(earlier, 1.0, 0.0).astype(BF), mask.astype(BF)).sum(axis=1, keepdims=True)
    rank = jnp.where(mask > 0.5, inside + carried, -1.0).astype(I32)
    slot = lax.broadcasted_iota(I32, (3 * n, n), 0)
    d = jnp.zeros((3 * n, 16), F32)
    for k, edges in enumerate(lists):
        d += mm_nt(jnp.where(slot == rank[k : k + 1, :], 1.0, 0.0).astype(BF), edges)
    s = (d[:, 0:1] * 256.0 + d[:, 1:2]).astype(I32)
    t = lax.shift_right_logical(s, 4)
    lat = lax.shift_right_logical(t, 4)
    lon = t & 15
    gz = (z - lax.shift_right_logical(lat, 1)) & 3
    gy = (y - lax.shift_right_logical(lon, 2)) & 3
    g_high = (lax.shift_right_logical(x, 1) + lat) & 1
    g_low = (x + lax.shift_right_logical(lon, 1)) & 1
    gc = (core + lon) & 1
    spot = ((((gc * 4 + gy) * 2 + g_low) * 4 + gz) * 2 + g_high) * 16 + (s & 15)
    total = jnp.sum(mask).astype(I32)
    used = lax.broadcasted_iota(I32, (3 * n, 1), 0) < total
    r = jnp.where(used, d[:, 3:4], -1.0)
    lane = lax.broadcasted_iota(I32, (3 * n, 16), 1)
    out[...] = jnp.where(lane == 0, spot.astype(F32), jnp.where(lane == 1, r, d))
    count[0, 0] = total


def mesh_body(
    count, fine, edges, a0, a1, a2, a3, b0, b1, b2, b3, recv, mesh_one, w_geom, w_second, first_node, first_sum,
    second, w_send, send, rows, total,
):
    parts = (a0, a1, a2, a3, b0, b1, b2, b3)
    n = a0.shape[0]
    for k, part in enumerate(parts):
        rows[n * k : n * (k + 1), :] = part[...]
    q = recv[0:COARSE_DEV, :]

    def hidden_sum(d):
        pick = one_hot(d[:, 1:2].astype(I32), MESH_NODES)
        pre = mm(one_hot(d[:, 0:1].astype(I32), len(parts) * n), rows[...])
        pre += mm(pick[:, 0:COARSE_DEV], q) + mm(d.astype(BF), w_geom[...])
        return mm_t(pick, silu(pre).astype(BF))

    total[...] = fine[...] + hidden_sum(edges[0:COARSE_SLOTS, :])

    @pl.loop(COARSE_SLOTS // 64, lax.shift_right_logical(count[0, 0] + 63, 6))
    def _(k):
        total[...] += hidden_sum(edges[pl.ds(pl.multiple_of(64 * k, 64), 64), :])

    two = node_rows(mesh_one[...], total[...], w_second[...], first_node[...], first_sum[...], second[...])
    send[...] = mm(two, w_send[...]).astype(BF)


def decode_early_body(edges, left, own, right, pair, recv, w_geom, out, rows):
    for k, part in enumerate((left, own, right, pair.at[0], pair.at[1])):
        rows[MESH_NODES * k : MESH_NODES * (k + 1), :] = part[...]
    n = 5 * MESH_NODES

    @pl.loop(0, 4)
    def _(b):
        span = pl.ds(pl.multiple_of(256 * b, 256), 256)
        q = recv[span, :].astype(F32)
        for t in range(GRID_DEGREE):
            d = edges[t, span, :]
            spread = one_hot(d[:, 0:1].astype(I32), n)
            out[t, span, :] = q + mm(spread, rows[0:n, :]) + mm(d.astype(BF), w_geom[...])


def decode_body(edges, early, left_pair, right_pair, base, w_second, first_sum, head, out, rows, totals):
    for k, part in enumerate((left_pair.at[0], left_pair.at[1], right_pair.at[0], right_pair.at[1])):
        rows[MESH_NODES * k : MESH_NODES * (k + 1), :] = part[...]
    for b in range(4):
        span = slice(256 * b, 256 * (b + 1))
        total = jnp.zeros((256, WIDTH), F32)
        for t in range(GRID_DEGREE):
            spot = edges[t, span, :][:, 0:1].astype(I32) - 5 * MESH_NODES
            total += silu(early[t, span, :] + mm(one_hot(spot, 4 * MESH_NODES), rows[...]))
        totals[span, :] = total.astype(BF)
    for b in range(2):
        span = slice(512 * b, 512 * (b + 1))
        summed = mm(totals[span, :], w_second[...]).astype(BF)
        hidden = silu(base[span, :] + mm(summed, first_sum[...])).astype(BF)
        out[:, span] = mm_nt(head[...], hidden).astype(BF)


def shift(value, axis, step, periodic):
    n = lax.axis_size(axis)
    pairs = [(i, (i + step) % n) for i in range(n) if periodic or 0 <= i + step < n]
    return lax.ppermute(value, axis, pairs)


def first_stage(value, round_down=False):
    up = shift(value, "lat", 1, False)
    down = shift(value, "lat", -1, round_down)
    return up, down, shift(value, "lon", 1, True), shift(value, "lon", -1, True)


def second_stage(pair):
    return shift(pair, "lon", 1, True), shift(pair, "lon", -1, True)


def along_z(s):
    return [(i, ((i // 2 + s) % 4) * 2 + i % 2) for i in range(8)]


def along_y(s):
    return [(i, ((i // 4 + s) % 4) * 4 + i % 4) for i in range(16)]


def four(value, axis, pairs_of):
    return [value] + [lax.ppermute(value, axis, pairs_of(s)) for s in (1, 2, 3)]


def per_device(
    grid_inputs,
    mesh_state,
    embed_in,
    embed_out,
    edge_square,
    edge_geom_weight,
    node_first,
    node_second,
    head,
    g2m_senders,
    g2m_receivers,
    g2m_counts,
    g2m_geom,
    mesh_senders,
    mesh_geom,
    coarse_senders,
    coarse_receivers,
    coarse_geom,
    m2g_senders,
    m2g_geom,
):
    mesh_rows = (MESH_NODES, WIDTH)
    grid_rows = (GRID_NODES, WIDTH)
    pair_rows = (2,) + mesh_rows
    grid_flops = 2 * GRID_NODES * WIDTH * WIDTH
    mesh_flops = grid_flops // 8
    both = ("lat", "lon")
    tiles = lax.axis_size(both)
    lat, lon = lax.axis_index("lat"), lax.axis_index("lon")
    place = jnp.stack([lat // 2, lon // 4, (lat % 2) * 2 + (lon // 2) % 2, lon % 2, lat * LON + lon])[None]
    place = place.astype(I32)

    pack_args = (
        g2m_senders, g2m_receivers, g2m_geom, mesh_state, coarse_senders, coarse_receivers, coarse_geom
    )

    def part_of(array):
        n = array.ndim - 2
        return Load((0,) if n == 1 else (0, 0), array.shape[1:] if n == 1 else array.shape[2:])

    payload, own_list, coarse_list, geom = kernel_call(
        pack_body,
        (
            shaped((PAYLOAD, WIDTH), BF), shaped((16 * CHUNKS, WIDTH), BF), shaped((16, COARSE_EDGES), BF),
            shaped((4, 16, WIDTH), BF),
        ),
        [SMEM] + [part_of(a) for a in pack_args] + [Load((), edge_geom_weight.shape)],
        (g2m_counts,) + pack_args + (edge_geom_weight,),
        [pltpu.VMEM((16, CHUNK), F32), pltpu.VMEM((8 * CHUNKS, CHUNK), F32)],
        name="pack",
    )
    up, down, near_left, near_right = first_stage(payload, True)
    latent, w_send, w_recv = kernel_call(
        embed_body,
        (shaped(grid_rows, BF),) + (shaped((WIDTH, WIDTH), BF),) * 2,
        [V, Load((), embed_in.shape), Load((), embed_out.shape), HBM, HBM],
        (grid_inputs[0, 0], embed_in, embed_out, edge_square, edge_square),
        [pltpu.SemaphoreType.DMA((2,))],
        flops=2 * grid_flops,
        moved=4 << 20,
        name="embed",
    )
    grid_send = kernel_call(
        send_body,
        shaped(grid_rows, BF),
        [V, V, ANY, ANY],
        (latent, w_send, near_left, near_right),
        flops=grid_flops,
        moved=3 << 20,
        name="send",
    )

    def geom_of(k):
        return View(k)

    def paired(up, down, order):
        shape = (2,) + up.shape
        return kernel_call(pair_body, shaped(shape, BF), [V, V, ANY], (up, down, order), name="pair")

    near_middle = paired(up, down, grid_send)
    near_left_pair, near_right_pair = second_stage(near_middle)
    own_sum = kernel_call(
        self_body,
        shaped(mesh_rows, F32),
        [part_of(mesh_state), V, V, V, geom_of(0)],
        (mesh_state, own_list, grid_send, w_recv, geom),
        flops=5 * grid_flops,
        moved=3 << 20,
        name="own",
    )
    near_scratch = [
        pltpu.VMEM((4 * CHUNKS, CHUNK), F32),
        pltpu.VMEM((4 * CHUNKS, CHUNK), I32),
        pltpu.VMEM((9 * MESH_NODES, WIDTH), BF),
        pltpu.VMEM((4 * NEAR_SLOTS, 8), F32),
        pltpu.VMEM((9 * MESH_NODES, WIDTH), F32),
    ]
    near_weights = [V, V, geom_of(3)]
    to_left, to_right, to_above, to_below, right_list = kernel_call(
        functools.partial(near_body, (5, 3, 7, 1)),
        (shaped(mesh_rows, BF),) * 4 + (shaped((16, COARSE_EDGES), BF),),
        [SMEM, V, V, View(0), View(1)] + near_weights,
        (place, near_left, near_right, near_middle, near_middle, grid_send, w_recv, geom),
        near_scratch,
        flops=2 * grid_flops,
        moved=5 << 20,
        name="beside",
    )
    *to_corners, coarse_next = kernel_call(
        functools.partial(near_body, (8, 2, 6, 0)),
        (shaped(mesh_rows, BF),) * 4 + (shaped((16, COARSE_EDGES), BF),),
        [SMEM, View(0), View(1), View(0), View(1), V, ANY, ANY] + near_weights,
        (
            place, near_left_pair, near_left_pair, near_right_pair, near_right_pair, right_list, own_sum, to_left,
            grid_send, w_recv, geom,
        ),
        near_scratch,
        flops=2 * grid_flops,
        moved=5 << 20,
        name="corners",
    )
    to_left_pair, to_right_pair = kernel_call(
        corner_body, (shaped(pair_rows, BF),) * 2, [V] * 4, tuple(to_corners), name="corner_pairs"
    )
    pair_left = shift(to_right_pair, "lon", 1, True)
    pair_right = shift(to_left_pair, "lon", -1, True)
    prep_args = (mesh_senders, mesh_geom, m2g_senders, m2g_geom)
    stored = {"square": edge_square, "first": node_first, "second": node_second}
    m_edges, d_edges, *kept = kernel_call(
        prep_body,
        (
            shaped((MESH_DEGREE, MESH_NODES, 16), F32),
            shaped((GRID_DEGREE, GRID_NODES, 16), F32),
        ) + (shaped((WIDTH, WIDTH), BF),) * len(KEPT),
        [part_of(a) for a in prep_args] + [ANY] + [HBM] * len(KEPT),
        prep_args + (to_left_pair,) + tuple(stored[name] for name, _ in KEPT),
        [pltpu.VMEM((16, 3072), F32), pltpu.VMEM((3072, 16), F32), pltpu.SemaphoreType.DMA((len(KEPT),))],
        flops=grid_flops,
        name="prep",
    )
    to_up, to_down, to_left, to_right = kernel_call(
        side_sum_body,
        (shaped(mesh_rows, BF),) * 4,
        [V, V, V, V, V, V, ANY],
        (to_above, to_below, pair_left, pair_right, to_left, to_right, m_edges),
        name="sides",
    )
    down = shift(to_up, "lat", -1, False)
    up = shift(to_down, "lat", 1, False)
    from_left = shift(to_right, "lon", 1, True)
    from_right = shift(to_left, "lon", -1, True)
    mesh_one, proc_send, proc_recv = kernel_call(
        node_body,
        (shaped(mesh_rows, BF),) * 3,
        [V] * 5 + [part_of(mesh_state)] + [V] * 6,
        (own_sum, from_left, from_right, up, down, mesh_state, *kept[0:6]),
        flops=7 * mesh_flops,
        moved=4 << 20,
        name="node",
    )
    grid_recv, grid_base = kernel_call(
        grid_body,
        (shaped(grid_rows, BF), shaped(grid_rows, F32)),
        [V, square(2, 1), first_half(2, 0), ANY],
        (latent, edge_square, node_first, proc_send),
        flops=2 * grid_flops,
        moved=5 << 20,
        name="grid",
    )
    partner = lax.ppermute(proc_send, "lat", [(i, i ^ 1) for i in range(8)])
    beside, apart = kernel_call(
        partner_body,
        (shaped((MESH_NODES + COARSE_DEV, WIDTH), BF), shaped((3 * COARSE_DEV, WIDTH), BF)),
        [V, V, V, ANY],
        (proc_send, partner, coarse_list, grid_recv),
        name="partner",
    )
    below = lax.ppermute(beside, "lat", along_z(1))
    above = lax.ppermute(beside, "lat", along_z(3))
    across = lax.ppermute(apart, "lat", along_z(2))
    rows = kernel_call(
        bands_body,
        shaped((8 * COARSE_DEV, WIDTH), BF),
        [V] * 5,
        (proc_send, partner, below, across, above),
        name="bands",
    )
    other = lax.ppermute(rows, "lon", [(i, i ^ 2) for i in range(LON)])
    rows, triple = kernel_call(
        both_body,
        (shaped((16 * COARSE_DEV, WIDTH), BF), shaped((3,) + mesh_rows, BF)),
        [SMEM] + [V] * 6,
        (place, rows, other, proc_send, partner, below, above),
        name="join_x",
    )
    left, right = second_stage(triple)
    quarter = four(rows, "lon", along_y)
    swapped = [lax.ppermute(part, "lon", [(i, i ^ 1) for i in range(LON)]) for part in quarter]
    edge_total = 3 * COARSE_EDGES
    c_edges, c_count = kernel_call(
        coarse_prep_body,
        (shaped((edge_total, 16), F32), shaped((1, 1), I32)),
        [SMEM, V, V, V],
        (place, coarse_list, coarse_next, across),
        [pltpu.VMEM((8, COARSE_EDGES), F32)],
        flops=mesh_flops,
        name="coarse_edges",
        out_specs=(V, SMEM),
    )
    fine = kernel_call(
        fine_body,
        shaped(mesh_rows, F32),
        [V] * 5 + [geom_of(1), ANY, ANY],
        (m_edges, left, triple, right, proc_recv, geom, quarter[1], c_edges),
        [pltpu.VMEM((9 * MESH_NODES, WIDTH), BF)],
        flops=2 * grid_flops,
        moved=3 << 20,
        name="fine",
    )
    dec_send = kernel_call(
        mesh_body,
        shaped(mesh_rows, BF),
        [SMEM] + [V] * 12 + [geom_of(1)] + [V] * 5,
        (c_count, fine, c_edges, *quarter, *swapped, proc_recv, mesh_one, geom, *kept[6:11]),
        [pltpu.VMEM((128 * COARSE_DEV, WIDTH), BF), pltpu.VMEM(mesh_rows, F32)],
        flops=4 * grid_flops,
        moved=6 << 20,
        name="mesh",
    )
    up, down, left, right = first_stage(dec_send)
    pair = paired(up, down, dec_send)
    left_pair, right_pair = second_stage(pair)
    early = kernel_call(
        decode_early_body,
        shaped((GRID_DEGREE,) + grid_rows, F32),
        [V, V, V, V, V, V, geom_of(2)],
        (d_edges, left, dec_send, right, pair, grid_recv, geom),
        [pltpu.VMEM((5 * MESH_NODES, WIDTH), BF)],
        flops=4 * grid_flops,
        moved=8 << 20,
        name="early",
    )
    outputs = kernel_call(
        decode_body,
        shaped((head.shape[1], GRID_NODES), BF),
        [V] * 8,
        (d_edges, early, left_pair, right_pair, grid_base, *kept[11:13], head.T),
        [pltpu.VMEM((4 * MESH_NODES, WIDTH), BF), pltpu.VMEM(grid_rows, BF)],
        flops=5 * grid_flops,
        moved=8 << 20,
        name="decode",
    )
    return outputs.T[None, None]


def solution(mesh):
    return jax.shard_map(
        per_device,
        mesh=mesh,
        in_specs=(
            P("lat", "lon", None, None),
            P("lat", "lon", None, None),
            P(),
            P(),
            P(),
            P(),
            P(),
            P(),
            P(),
            P("lat", "lon", None),
            P("lat", "lon", None),
            P("lat", "lon"),
            P("lat", "lon", None, None),
            P("lat", "lon", None),
            P("lat", "lon", None, None),
            P("lat", "lon", None),
            P("lat", "lon", None),
            P("lat", "lon", None, None),
            P("lat", "lon", None),
            P("lat", "lon", None, None),
        ),
        out_specs=P("lat", "lon", None, None),
        check_vma=False,
    )
```

```python
import functools

import jax
import jax.numpy as jnp
from jax import lax
from jax.experimental import pallas as pl
from jax.experimental.pallas import tpu as pltpu
from jax.sharding import PartitionSpec as P

BF = jnp.bfloat16
F32 = jnp.float32
I32 = jnp.int32
WIDTH = 512
GRID_NODES = 1024
MESH_NODES = 128
MESH_DEGREE = 6
GRID_DEGREE = 3
COARSE_DEV = 16
SLOTS = 2048
CHUNK = 512
CHUNKS = SLOTS // CHUNK
LISTED = MESH_NODES + 8 * CHUNKS
PAYLOAD = LISTED + 16
COARSE_EDGES = 256
LON = 16
NEAR_SLOTS = 160
COARSE_SLOTS = 320
GROUPS = (5, 3, 7, 0, 1, 2, 6, 4, 8)
VMEM_BYTES = 14 * 1024 * 1024


def mm(left, right):
    return jnp.dot(left, right, preferred_element_type=F32)


def mm_t(left, right):
    return lax.dot_general(left, right, (((0,), (0,)), ((), ())), preferred_element_type=F32)


def mm_nt(left, right):
    return lax.dot_general(left, right, (((1,), (1,)), ((), ())), preferred_element_type=F32)


def silu(v):
    half = 0.5 * v
    return half + half * jnp.tanh(half)


def one_hot(column, width):
    spots = lax.broadcasted_iota(I32, (column.shape[0], width), 1)
    return jnp.where(spots == column, 1.0, 0.0).astype(BF)


class Load:
    def __init__(self, index, shape):
        self.index, self.shape = index, shape


class View:
    def __init__(self, index):
        self.index = index


class Arriving:
    def __init__(self, copy, ref):
        self.copy, self.ref = copy, ref
        self.shape = ref.shape

    def ready(self):
        if self.copy is not None:
            self.copy.wait()
            self.copy = None
        return self.ref

    def __getitem__(self, index):
        return self.ready()[index]


V = pl.BlockSpec(memory_space=pltpu.VMEM)
SMEM = pl.BlockSpec(memory_space=pltpu.SMEM)
ANY = pl.BlockSpec(memory_space=pl.ANY)
HBM = pl.BlockSpec(memory_space=pltpu.HBM)


def square(block, kind):
    return Load((block, kind), (WIDTH, WIDTH))


def first_half(block, half):
    return Load((block, slice(WIDTH * half, WIDTH * (half + 1))), (WIDTH, WIDTH))


def second_of(block):
    return Load((block,), (WIDTH, WIDTH))


KEPT = (
    ("square", square(0, 2)), ("first", first_half(0, 0)), ("first", first_half(0, 1)), ("second", second_of(0)),
    ("square", square(1, 0)), ("square", square(1, 1)), ("square", square(1, 2)), ("first", first_half(1, 0)),
    ("first", first_half(1, 1)), ("second", second_of(1)), ("square", square(2, 0)), ("square", square(2, 2)),
    ("first", first_half(2, 1)),
)
ENCODER = (square(0, 0),)


def kernel_call(body, outs, specs, args, scratch=(), flops=0, moved=0, name=None, out_specs=None):
    loads = [(k, spec, args[k].dtype) for k, spec in enumerate(specs) if isinstance(spec, Load)]
    n_in, n_loads = len(specs), len(loads)

    def run(*refs):
        given, rest = list(refs[:n_in]), list(refs[n_in:])
        if n_loads:
            sems = rest[-1]
            buffers = rest[-1 - n_loads : -1]
            rest = rest[: -1 - n_loads]
            for at, ((k, spec, _), buffer) in enumerate(zip(loads, buffers)):
                source = given[k].at[spec.index] if spec.index else given[k]
                copy = pltpu.make_async_copy(source, buffer, sems.at[at])
                copy.start()
                given[k] = Arriving(copy, buffer)
        for k, spec in enumerate(specs):
            if isinstance(spec, View):
                given[k] = given[k].at[spec.index]
        body(*given, *rest)
        for part in given:
            if isinstance(part, Arriving):
                part.ready()

    extra = [pltpu.VMEM(spec.shape, dtype) for _, spec, dtype in loads]
    if loads:
        extra.append(pltpu.SemaphoreType.DMA((n_loads,)))
    many = isinstance(outs, tuple)
    args = [
        pltpu.with_memory_space_constraint(arg, pltpu.HBM) if spec is HBM or isinstance(spec, Load) else arg
        for spec, arg in zip(specs, args)
    ]
    return pl.pallas_call(
        run,
        out_shape=outs,
        in_specs=[HBM if isinstance(q, Load) else V if isinstance(q, View) else q for q in specs],
        out_specs=out_specs if out_specs is not None else (V,) * len(outs) if many else V,
        scratch_shapes=list(scratch) + extra,
        compiler_params=pltpu.CompilerParams(vmem_limit_bytes=VMEM_BYTES),
        cost_estimate=pl.CostEstimate(flops=flops, bytes_accessed=moved, transcendentals=0),
        name=name,
    )(*args)


def shaped(shape, dtype):
    return jax.ShapeDtypeStruct(shape, dtype)


def fill_list(scr, width, indices, geometry):
    for row, value in enumerate(indices):
        scr[row : row + 1, 0:width] = value.astype(F32)
    high = geometry.astype(BF).astype(F32)
    scr[4:8, 0:width] = high
    scr[8:12, 0:width] = geometry - high
    scr[12:16, 0:width] = high


def pack_body(
    count, senders, receivers, geometry, state, c_senders, c_receivers, c_geometry, weight,
    out, own, coarse, w_out, scr, short,
):
    for c in range(CHUNKS):
        cols = slice(c * CHUNK, (c + 1) * CHUNK)
        s = senders[:, cols]
        edge = lax.broadcasted_iota(I32, (1, CHUNK), 1) + c * CHUNK
        code = jnp.where(edge < count[0, 0], lax.shift_right_logical(s, 10) + 1, 0)
        local = s & (GRID_NODES - 1)
        fill_list(
            scr, CHUNK, (code, lax.shift_right_logical(local, 8), local & 255, receivers[:, cols]), geometry[:, cols]
        )
        own[16 * c : 16 * (c + 1), :] = scr[...].astype(BF)
        short[8 * c : 8 * (c + 1), :] = scr[0:8, :]
    out[MESH_NODES:LISTED, :] = short[...].astype(BF)
    s = c_senders[...]
    r = c_receivers[...]
    n = s.shape[1]
    fill_list(
        scr, n, (lax.shift_right_logical(s, 8), s & 255, lax.shift_right_logical(r, 4), r & 15), c_geometry[...]
    )
    out[LISTED:PAYLOAD, :] = scr[...].astype(BF)
    coarse[...] = scr[:, 0:n].astype(BF)
    zero = jnp.zeros((4, WIDTH), F32)
    for k in range(3):
        w = weight[k]
        high = w.astype(BF).astype(F32)
        scr[0:4, :] = zero
        scr[4:8, :] = high
        scr[8:12, :] = high
        scr[12:16, :] = w - high
        w_out[k] = scr[...].astype(BF)
        if k == 0:
            scr[8:12, :] = zero
            w_out[3] = scr[...].astype(BF)
    out[0:MESH_NODES, :] = state[...]


def prep_body(m_senders, m_geometry, d_senders, d_geometry, left, right, order, *refs):
    n = len(KEPT)
    sources, (m_out, d_out, o_left, o_right) = refs[:n], refs[n : n + 4]
    kept, (scr, turned, sems) = refs[n + 4 : -3], refs[-3:]
    o_left[...] = left[...]
    o_right[...] = right[...]
    copies = bring(sources, [load for _, load in KEPT], kept, sems)
    for senders, geometry, degree, out in (
        (m_senders, m_geometry, MESH_DEGREE, m_out),
        (d_senders, d_geometry, GRID_DEGREE, d_out),
    ):
        n = senders.shape[1]
        s = senders[...]
        near = lax.shift_right_logical(s, 7)
        spot = jnp.zeros_like(near)
        for place, group in enumerate(GROUPS):
            spot = jnp.where(near == place, group, spot)
        spot = spot * MESH_NODES + (s & (MESH_NODES - 1))
        zero = jnp.zeros((1, n), F32)
        fill_list(scr, n, (spot, zero, zero, zero), geometry[...])
        turned[0:n, :] = scr[:, 0:n].T
        for t in range(degree):
            out[t] = turned[pl.ds(t, n // degree, stride=degree), :]
    for copy in copies:
        copy.wait()


def embed_body(x, w_in, w_out, source, latent, w_send, sems):
    copies = bring((source,), ENCODER, (w_send,), sems)
    for b in range(4):
        rows = slice(256 * b, 256 * (b + 1))
        hidden = silu(mm(x[rows, :], w_in[...])).astype(BF)
        latent[rows, :] = mm(hidden, w_out[...]).astype(BF)
    for copy in copies:
        copy.wait()


def send_body(latent, w_send, order, order_too, send):
    for b in range(4):
        rows = slice(256 * b, 256 * (b + 1))
        send[rows, :] = mm(latent[rows, :], w_send[...]).astype(BF)


def grid_body(latent, w_recv, w_first, order, recv, base):
    for b in range(4):
        rows = slice(256 * b, 256 * (b + 1))
        recv[rows, :] = mm(latent[rows, :], w_recv[...]).astype(BF)
        base[rows, :] = mm(latent[rows, :], w_first[...])


def bring(sources, loads, outs, sems):
    copies = []
    for k, load in enumerate(loads):
        copies.append(pltpu.make_async_copy(sources[k].at[load.index], outs[k], sems.at[k]))
        copies[-1].start()
    return copies


def self_body(chunks, state, listed, send, w_recv, w_geom, *refs):
    total = jnp.zeros((MESH_NODES, WIDTH), F32) if len(refs) == 1 else refs[0][...]
    if len(refs) == 2 and refs[1].shape == (32, WIDTH):
        refs[1][...] = listed[32:64, :]
        out = refs[0]
        total = jnp.zeros((MESH_NODES, WIDTH), F32)
    else:
        out = refs[-1]
    q = None
    for c in chunks:
        d = listed[16 * c : 16 * (c + 1), :].astype(F32).T
        s = (d[:, 1:2] * 256.0 + d[:, 2:3]).astype(I32)
        r = jnp.where(d[:, 0:1] == 5.0, d[:, 3:4], -1.0).astype(I32)
        pick = one_hot(r, MESH_NODES)
        pre = mm(one_hot(s, GRID_NODES), send[...]) + mm(d.astype(BF), w_geom[...])
        if q is None:
            q = mm(state[...], w_recv[...]).astype(BF)
        total += mm_t(pick, silu(pre + mm(pick, q)).astype(BF))
    out[...] = total


def near_body(buckets, place, *refs):
    sources, refs = refs[: len(buckets)], refs[len(buckets) :]
    if len(refs) == 16:
        beside, order_first, order_last, *refs = refs
    send, w_recv, w_geom, *refs = refs
    outs, refs = refs[: len(buckets)], refs[len(buckets) :]
    if len(refs) == 6 and buckets[0] != 5:
        following, *refs = refs
        n = COARSE_EDGES
        last = (place[0, 4] & (LON - 1)) == LON - 1
        following[...] = jnp.where(
            last, sources[-1][LISTED:PAYLOAD, 0:n].astype(F32), beside[...].astype(F32)
        ).astype(BF)
    if len(buckets) == 4 and buckets[0] == 5:
        following, *refs = refs
        following[...] = sources[1][LISTED:PAYLOAD, 0:COARSE_EDGES]
    masks, ranks, q, edges, sums = refs
    last = lax.shift_right_logical(place[0, 4], 4) == 7
    lists = tuple(zip(sources, buckets, outs))
    q[...] = jnp.zeros_like(q)

    def listed(src, c):
        return src[MESH_NODES:LISTED, :].astype(F32)[8 * c : 8 * (c + 1), :]

    def geometry_part(d):
        return mm(jnp.concatenate([d, d], axis=1).astype(BF), w_geom[...])

    for i, (src, bucket, _) in enumerate(lists):
        for c in range(CHUNKS):
            row = i * CHUNKS + c
            code = listed(src, c)[0:1, :]
            wanted = jnp.where(last, -1.0, float(bucket + 1)) if bucket < 3 else float(bucket + 1)
            masks[row : row + 1, :] = jnp.where(code == wanted, 1.0, 0.0)
    n = masks.shape[0]
    mask = masks[...]
    before = lax.broadcasted_iota(I32, (CHUNK, CHUNK), 0) < lax.broadcasted_iota(I32, (CHUNK, CHUNK), 1)
    inside = mm(mask.astype(BF), jnp.where(before, 1.0, 0.0).astype(BF))
    mine = lax.broadcasted_iota(I32, (n, n), 0)
    other = lax.broadcasted_iota(I32, (n, n), 1)
    same = mine // CHUNKS == other // CHUNKS
    earlier = jnp.where((other < mine) & same, 1.0, 0.0).astype(BF)
    carried = mm(earlier, mask.astype(BF)).sum(axis=1, keepdims=True)
    ranks[...] = jnp.where(mask > 0.5, inside + carried, -1.0).astype(I32)

    slot = lax.broadcasted_iota(I32, (NEAR_SLOTS, CHUNK), 0)
    for i, (src, _, _) in enumerate(lists):
        d = jnp.zeros((NEAR_SLOTS, 8), F32)
        for c in range(CHUNKS):
            row = i * CHUNKS + c
            d += mm_nt(jnp.where(slot == ranks[row : row + 1, :], 1.0, 0.0).astype(BF), listed(src, c).astype(BF))
        edges[NEAR_SLOTS * i : NEAR_SLOTS * (i + 1), :] = d
    for src, bucket, _ in lists:
        q[MESH_NODES * bucket : MESH_NODES * (bucket + 1), :] = mm(src[0:MESH_NODES, :], w_recv[...]).astype(BF)
    for j in range(len(lists) // 2):
        d = edges[2 * NEAR_SLOTS * j : 2 * NEAR_SLOTS * (j + 1), :]
        s = (d[:, 1:2] * 256.0 + d[:, 2:3]).astype(I32)
        pre = mm(one_hot(s, GRID_NODES), send[...]) + geometry_part(d)
        r = jnp.where(d[:, 0:1] > 0.5, d[:, 3:4], -1.0).astype(I32)
        for h in range(2):
            bucket = lists[2 * j + h][1]
            part = slice(NEAR_SLOTS * h, NEAR_SLOTS * (h + 1))
            rows = slice(MESH_NODES * bucket, MESH_NODES * (bucket + 1))
            pick = one_hot(r[part, :], MESH_NODES)
            sums[rows, :] = mm_t(pick, silu(pre[part, :] + mm(pick, q[rows, :])).astype(BF))

    count = mm(jnp.where(same, 1.0, 0.0).astype(BF), mask.astype(BF)).sum(axis=1, keepdims=True)
    over = jnp.maximum(count - NEAR_SLOTS, 0.0)
    total = lax.shift_right_logical(jnp.sum(over).astype(I32), 2)

    @pl.when(total > 0)
    def _():
        across = lax.broadcasted_iota(I32, (n, 1), 0) // CHUNKS
        base = jnp.zeros((n, 1), F32)
        for i in range(len(lists) - 1):
            base += jnp.where(across > i, over[i * CHUNKS : i * CHUNKS + 1, :], 0.0)
        rank = ranks[...]
        ranks[...] = jnp.where(rank >= NEAR_SLOTS, rank - NEAR_SLOTS + base.astype(I32), -1)

        @pl.loop(0, lax.shift_right_logical(total + 127, 7))
        def _(k):
            late = lax.broadcasted_iota(I32, (128, CHUNK), 0) + k * 128
            d = jnp.zeros((128, 8), F32)
            for i, (src, _, _) in enumerate(lists):
                for c in range(CHUNKS):
                    row = i * CHUNKS + c
                    d += mm_nt(jnp.where(late == ranks[row : row + 1, :], 1.0, 0.0).astype(BF), listed(src, c).astype(BF))
            s = (d[:, 1:2] * 256.0 + d[:, 2:3]).astype(I32)
            code = d[:, 0:1]
            r = jnp.where(code > 0.5, (code - 1.0) * float(MESH_NODES) + d[:, 3:4], -1.0).astype(I32)
            pick = one_hot(r, 9 * MESH_NODES)
            pre = mm(one_hot(s, GRID_NODES), send[...]) + mm(pick, q[...]) + geometry_part(d)
            sums[...] += mm_t(pick, silu(pre).astype(BF))

    for _, bucket, dst in lists:
        dst[...] = sums[MESH_NODES * bucket : MESH_NODES * (bucket + 1), :].astype(BF)


def corner_body(a, b, c, d, left, right):
    left[0] = a[...]
    left[1] = b[...]
    right[0] = c[...]
    right[1] = d[...]


def side_sum_body(above, below, from_left, from_right, order, up, down):
    for k, middle, out in ((0, above, up), (1, below, down)):
        total = middle[...].astype(F32) + from_left[k].astype(F32) + from_right[k].astype(F32)
        out[...] = total.astype(BF)


def join_body(parts, out):
    n = parts[0].shape[0]
    for k, part in enumerate(parts):
        out[n * k : n * (k + 1), :] = part[...]


def pair_body(up, down, order, out):
    out[0] = up[...]
    out[1] = down[...]


def partner_body(own, partner, low, both, order, out, onward):
    n = COARSE_DEV
    onward[...] = partner[...]
    for k, part in enumerate((own[...], partner[0:n, :], low[...], both[...])):
        out[n * k : n * (k + 1), :] = part


def bands_body(place, own, partner, below, above, a, b, c, d, order, out, triple):
    join_body((a, b, c, d), out)
    triple[1] = own[...]
    odd = place[0, 2] >= 2

    @pl.when(odd)
    def _():
        triple[0] = partner[...]
        triple[2] = above[...]

    @pl.when(jnp.logical_not(odd))
    def _():
        triple[0] = below[...]
        triple[2] = partner[...]


def split_mm(value, weight):
    high = value.astype(BF)
    low = (value - high.astype(F32)).astype(BF)
    return mm(high, weight) + mm(low, weight)


def node_rows(v, hidden_total, w_second, first_node, first_sum, second):
    m = split_mm(hidden_total, w_second).astype(BF)
    u = silu(mm(v, first_node) + mm(m, first_sum)).astype(BF)
    return (v.astype(F32) + mm(u, second)).astype(BF)


def node_body(
    own, from_left, from_right, up, down, state, w_second, first_node, first_sum, second, w_send, w_recv, order,
    mesh_one, send, recv, coarse,
):
    total = own[...] + from_left[...].astype(F32) + from_right[...].astype(F32)
    total = total + up[...].astype(F32) + down[...].astype(F32)
    one = node_rows(state[...], total, w_second[...], first_node[...], first_sum[...], second[...])
    mesh_one[...] = one
    sent = mm(one, w_send[...]).astype(BF)
    send[...] = sent
    coarse[...] = sent[0:COARSE_DEV, :]
    recv[...] = mm(one, w_recv[...]).astype(BF)


def fine_body(edges, left, own, right, recv, w_geom, order, order_too, out, rows):
    parts = (left[1], own[1], right[1], own[0], own[2], left[0], left[2], right[0], right[2])
    for k, part in enumerate(parts):
        rows[MESH_NODES * k : MESH_NODES * (k + 1), :] = part
    q = recv[...].astype(F32)
    total = jnp.zeros((MESH_NODES, WIDTH), F32)
    for t in range(MESH_DEGREE):
        d = edges[t]
        spread = one_hot(d[:, 0:1].astype(I32), 9 * MESH_NODES)
        pre = q + mm(spread, rows[...]) + mm(d.astype(BF), w_geom[...])
        total += silu(pre)
    out[...] = total


def coarse_prep_body(place, own, following, far, out, count, row):
    z, y, x, core, tile = (place[0, k] for k in range(5))
    n = COARSE_EDGES
    lists = (own[...], following[...], far[...])
    for k, edges in enumerate(lists):
        owner = edges.astype(F32)[2:3, :].astype(I32)
        row[k : k + 1, :] = jnp.where(owner == tile, 1.0, 0.0)
    row[3:8, :] = jnp.zeros((5, n), F32)
    mask = row[...]
    before = lax.broadcasted_iota(I32, (n, n), 0) < lax.broadcasted_iota(I32, (n, n), 1)
    inside = mm(mask.astype(BF), jnp.where(before, 1.0, 0.0).astype(BF))
    earlier = lax.broadcasted_iota(I32, (8, 8), 1) < lax.broadcasted_iota(I32, (8, 8), 0)
    carried = mm(jnp.where(earlier, 1.0, 0.0).astype(BF), mask.astype(BF)).sum(axis=1, keepdims=True)
    rank = jnp.where(mask > 0.5, inside + carried, -1.0).astype(I32)
    slot = lax.broadcasted_iota(I32, (3 * n, n), 0)
    d = jnp.zeros((3 * n, 16), F32)
    for k, edges in enumerate(lists):
        d += mm_nt(jnp.where(slot == rank[k : k + 1, :], 1.0, 0.0).astype(BF), edges)
    s = (d[:, 0:1] * 256.0 + d[:, 1:2]).astype(I32)
    t = lax.shift_right_logical(s, 4)
    lat = lax.shift_right_logical(t, 4)
    lon = t & 15
    gz = (z - lax.shift_right_logical(lat, 1)) & 3
    gy = (y - lax.shift_right_logical(lon, 2)) & 3
    g_high = (lax.shift_right_logical(x, 1) + lat) & 1
    g_low = (x + lax.shift_right_logical(lon, 1)) & 1
    gc = (core + lon) & 1
    spot = ((((gc * 4 + gz) * 4 + gy) * 2 + g_low) * 2 + g_high) * 16 + (s & 15)
    total = jnp.sum(mask).astype(I32)
    used = lax.broadcasted_iota(I32, (3 * n, 1), 0) < total
    r = jnp.where(used, d[:, 3:4], -1.0)
    lane = lax.broadcasted_iota(I32, (3 * n, 16), 1)
    out[...] = jnp.where(lane == 0, spot.astype(F32), jnp.where(lane == 1, r, d))
    count[0, 0] = total


def mesh_body(
    count, fine, edges, a0, a1, a2, a3, b0, b1, b2, b3, recv, mesh_one, w_geom, w_second, first_node, first_sum,
    second, w_send, send, rows, total,
):
    parts = (a0, a1, a2, a3, b0, b1, b2, b3)
    n = a0.shape[0]
    for k, part in enumerate(parts):
        rows[n * k : n * (k + 1), :] = part[...]
    q = recv[0:COARSE_DEV, :]

    def hidden_sum(d):
        pick = one_hot(d[:, 1:2].astype(I32), MESH_NODES)
        pre = mm(one_hot(d[:, 0:1].astype(I32), len(parts) * n), rows[...])
        pre += mm(pick[:, 0:COARSE_DEV], q) + mm(d.astype(BF), w_geom[...])
        return mm_t(pick, silu(pre).astype(BF))

    total[...] = fine[...] + hidden_sum(edges[0:COARSE_SLOTS, :])

    @pl.loop(COARSE_SLOTS // 64, lax.shift_right_logical(count[0, 0] + 63, 6))
    def _(k):
        total[...] += hidden_sum(edges[pl.ds(pl.multiple_of(64 * k, 64), 64), :])

    two = node_rows(mesh_one[...], total[...], w_second[...], first_node[...], first_sum[...], second[...])
    send[...] = mm(two, w_send[...]).astype(BF)


def decode_early_body(edges, left, own, right, pair, recv, w_geom, out, rows):
    for k, part in enumerate((left, own, right, pair.at[0], pair.at[1])):
        rows[MESH_NODES * k : MESH_NODES * (k + 1), :] = part[...]
    n = 5 * MESH_NODES

    @pl.loop(0, 4)
    def _(b):
        span = pl.ds(pl.multiple_of(256 * b, 256), 256)
        q = recv[span, :].astype(F32)
        for t in range(GRID_DEGREE):
            d = edges[t, span, :]
            spread = one_hot(d[:, 0:1].astype(I32), n)
            out[t, span, :] = q + mm(spread, rows[0:n, :]) + mm(d.astype(BF), w_geom[...])


def decode_body(edges, early, left_pair, right_pair, base, w_second, first_sum, head, out, rows, totals):
    for k, part in enumerate((left_pair.at[0], left_pair.at[1], right_pair.at[0], right_pair.at[1])):
        rows[MESH_NODES * k : MESH_NODES * (k + 1), :] = part[...]
    for b in range(4):
        span = slice(256 * b, 256 * (b + 1))
        total = jnp.zeros((256, WIDTH), F32)
        for t in range(GRID_DEGREE):
            spot = edges[t, span, :][:, 0:1].astype(I32) - 5 * MESH_NODES
            total += silu(early[t, span, :] + mm(one_hot(spot, 4 * MESH_NODES), rows[...]))
        totals[span, :] = total.astype(BF)
    for b in range(2):
        span = slice(512 * b, 512 * (b + 1))
        summed = mm(totals[span, :], w_second[...]).astype(BF)
        hidden = silu(base[span, :] + mm(summed, first_sum[...])).astype(BF)
        out[:, span] = mm_nt(head[...], hidden).astype(BF)


def shift(value, axis, step, periodic):
    n = lax.axis_size(axis)
    pairs = [(i, (i + step) % n) for i in range(n) if periodic or 0 <= i + step < n]
    return lax.ppermute(value, axis, pairs)


def first_stage(value, round_down=False):
    up = shift(value, "lat", 1, False)
    down = shift(value, "lat", -1, round_down)
    return up, down, shift(value, "lon", 1, True), shift(value, "lon", -1, True)


def second_stage(pair):
    return shift(pair, "lon", 1, True), shift(pair, "lon", -1, True)


def along_z(s):
    return [(i, ((i // 2 + s) % 4) * 2 + i % 2) for i in range(8)]


def along_y(s):
    return [(i, ((i // 4 + s) % 4) * 4 + i % 4) for i in range(16)]


def per_device(
    grid_inputs,
    mesh_state,
    embed_in,
    embed_out,
    edge_square,
    edge_geom_weight,
    node_first,
    node_second,
    head,
    g2m_senders,
    g2m_receivers,
    g2m_counts,
    g2m_geom,
    mesh_senders,
    mesh_geom,
    coarse_senders,
    coarse_receivers,
    coarse_geom,
    m2g_senders,
    m2g_geom,
):
    mesh_rows = (MESH_NODES, WIDTH)
    grid_rows = (GRID_NODES, WIDTH)
    pair_rows = (2,) + mesh_rows
    grid_flops = 2 * GRID_NODES * WIDTH * WIDTH
    mesh_flops = grid_flops // 8
    both = ("lat", "lon")
    tiles = lax.axis_size(both)
    lat, lon = lax.axis_index("lat"), lax.axis_index("lon")
    place = jnp.stack([lat // 2, lon // 4, (lat % 2) * 2 + (lon // 2) % 2, lon % 2, lat * LON + lon])[None]
    place = place.astype(I32)

    pack_args = (
        g2m_senders, g2m_receivers, g2m_geom, mesh_state, coarse_senders, coarse_receivers, coarse_geom
    )

    def part_of(array):
        n = array.ndim - 2
        return Load((0,) if n == 1 else (0, 0), array.shape[1:] if n == 1 else array.shape[2:])

    payload, own_list, coarse_list, geom = kernel_call(
        pack_body,
        (
            shaped((PAYLOAD, WIDTH), BF), shaped((16 * CHUNKS, WIDTH), BF), shaped((16, COARSE_EDGES), BF),
            shaped((4, 16, WIDTH), BF),
        ),
        [SMEM] + [part_of(a) for a in pack_args] + [Load((), edge_geom_weight.shape)],
        (g2m_counts,) + pack_args + (edge_geom_weight,),
        [pltpu.VMEM((16, CHUNK), F32), pltpu.VMEM((8 * CHUNKS, CHUNK), F32)],
        name="pack",
    )
    up, down, near_left, near_right = first_stage(payload, True)
    latent, w_send = kernel_call(
        embed_body,
        (shaped(grid_rows, BF), shaped((WIDTH, WIDTH), BF)),
        [V, Load((), embed_in.shape), Load((), embed_out.shape), HBM],
        (grid_inputs[0, 0], embed_in, embed_out, edge_square),
        [pltpu.SemaphoreType.DMA((1,))],
        flops=2 * grid_flops,
        moved=4 << 20,
        name="embed",
    )
    grid_send = kernel_call(
        send_body,
        shaped(grid_rows, BF),
        [V, V, ANY, ANY],
        (latent, w_send, near_left, near_right),
        flops=grid_flops,
        moved=3 << 20,
        name="send",
    )

    def geom_of(k):
        return View(k)

    own_specs = [part_of(mesh_state), V, V, square(0, 1), geom_of(0)]
    own_args = (mesh_state, own_list, grid_send, edge_square, geom)

    def paired(up, down, order):
        shape = (2,) + up.shape
        return kernel_call(pair_body, shaped(shape, BF), [V, V, ANY], (up, down, order), name="pair")

    own_first, list_rest = kernel_call(
        functools.partial(self_body, (0, 1)),
        (shaped(mesh_rows, F32), shaped((32, WIDTH), BF)),
        own_specs,
        own_args,
        flops=2 * grid_flops,
        moved=3 << 20,
        name="own_first",
    )
    near_middle = paired(up, down, own_first)
    near_left_pair, near_right_pair = second_stage(near_middle)
    own_sum = kernel_call(
        functools.partial(self_body, (0, 1)),
        shaped(mesh_rows, F32),
        own_specs + [V],
        (mesh_state, list_rest, grid_send, edge_square, geom, own_first),
        flops=2 * grid_flops,
        moved=3 << 20,
        name="own_last",
    )
    near_scratch = [
        pltpu.VMEM((4 * CHUNKS, CHUNK), F32),
        pltpu.VMEM((4 * CHUNKS, CHUNK), I32),
        pltpu.VMEM((9 * MESH_NODES, WIDTH), BF),
        pltpu.VMEM((4 * NEAR_SLOTS, 8), F32),
        pltpu.VMEM((9 * MESH_NODES, WIDTH), F32),
    ]
    near_weights = [V, square(0, 1), geom_of(3)]
    to_left, to_right, to_above, to_below, right_list = kernel_call(
        functools.partial(near_body, (5, 3, 7, 1)),
        (shaped(mesh_rows, BF),) * 4 + (shaped((16, COARSE_EDGES), BF),),
        [SMEM, V, V, View(0), View(1)] + near_weights,
        (place, near_left, near_right, near_middle, near_middle, grid_send, edge_square, geom),
        near_scratch,
        flops=2 * grid_flops,
        moved=5 << 20,
        name="beside",
    )
    *to_corners, coarse_next = kernel_call(
        functools.partial(near_body, (8, 2, 6, 0)),
        (shaped(mesh_rows, BF),) * 4 + (shaped((16, COARSE_EDGES), BF),),
        [SMEM, View(0), View(1), View(0), View(1), V, ANY, ANY] + near_weights,
        (
            place, near_left_pair, near_left_pair, near_right_pair, near_right_pair, right_list, own_sum, to_left,
            grid_send, edge_square, geom,
        ),
        near_scratch,
        flops=2 * grid_flops,
        moved=5 << 20,
        name="corners",
    )
    to_left_pair, to_right_pair = kernel_call(
        corner_body, (shaped(pair_rows, BF),) * 2, [V] * 4, tuple(to_corners), name="corner_pairs"
    )
    pair_left = shift(to_right_pair, "lon", 1, True)
    pair_right = shift(to_left_pair, "lon", -1, True)
    prep_args = (mesh_senders, mesh_geom, m2g_senders, m2g_geom)
    stored = {"square": edge_square, "first": node_first, "second": node_second}
    m_edges, d_edges, to_left, to_right, *kept = kernel_call(
        prep_body,
        (
            shaped((MESH_DEGREE, MESH_NODES, 16), F32),
            shaped((GRID_DEGREE, GRID_NODES, 16), F32),
            shaped(mesh_rows, BF),
            shaped(mesh_rows, BF),
        ) + (shaped((WIDTH, WIDTH), BF),) * len(KEPT),
        [part_of(a) for a in prep_args] + [V, V, ANY] + [HBM] * len(KEPT),
        prep_args + (to_left, to_right, to_left_pair) + tuple(stored[name] for name, _ in KEPT),
        [pltpu.VMEM((16, 3072), F32), pltpu.VMEM((3072, 16), F32), pltpu.SemaphoreType.DMA((len(KEPT),))],
        flops=grid_flops,
        name="prep",
    )
    to_up, to_down = kernel_call(
        side_sum_body,
        (shaped(mesh_rows, BF),) * 2,
        [V, V, V, V, ANY],
        (to_above, to_below, pair_left, pair_right, m_edges),
        name="sides",
    )
    down = shift(to_up, "lat", -1, False)
    up = shift(to_down, "lat", 1, False)
    from_left = shift(to_right, "lon", 1, True)
    from_right = shift(to_left, "lon", -1, True)
    far_list = lax.ppermute(coarse_list, both, [(t, (t + tiles // 2) % tiles) for t in range(tiles)])
    mesh_one, proc_send, proc_recv, coarse_own = kernel_call(
        node_body,
        (shaped(mesh_rows, BF),) * 3 + (shaped((COARSE_DEV, WIDTH), BF),),
        [V] * 5 + [part_of(mesh_state)] + [V] * 6 + [ANY],
        (own_sum, from_left, from_right, up, down, mesh_state, *kept[0:6], far_list),
        flops=7 * mesh_flops,
        moved=4 << 20,
        name="node",
    )
    grid_recv, grid_base = kernel_call(
        grid_body,
        (shaped(grid_rows, BF), shaped(grid_rows, F32)),
        [V, square(2, 1), first_half(2, 0), ANY],
        (latent, edge_square, node_first, proc_send),
        flops=2 * grid_flops,
        moved=5 << 20,
        name="grid",
    )
    def half(t):
        return (t // LON ^ 1) * LON + (t % LON)

    partner = lax.ppermute(proc_send, "lat", [(i, i ^ 1) for i in range(8)])
    low = lax.ppermute(coarse_own, "lon", [(i, i ^ 2) for i in range(LON)])
    cross = lax.ppermute(coarse_own, both, [(t, half(t) ^ 2) for t in range(tiles)])
    beside, onward = kernel_call(
        partner_body,
        (shaped((4 * COARSE_DEV, WIDTH), BF), shaped(mesh_rows, BF)),
        [V, V, V, V, ANY],
        (coarse_own, partner, low, cross, grid_recv),
        name="partner",
    )
    edge_total = 3 * COARSE_EDGES
    c_edges, c_count = kernel_call(
        coarse_prep_body,
        (shaped((edge_total, 16), F32), shaped((1, 1), I32)),
        [SMEM, V, V, V],
        (place, coarse_list, coarse_next, far_list),
        [pltpu.VMEM((8, COARSE_EDGES), F32)],
        flops=mesh_flops,
        name="coarse_edges",
        out_specs=(V, SMEM),
    )
    quarter = [beside] + [lax.ppermute(beside, "lon", along_y(s)) for s in (1, 2, 3)]
    below = lax.ppermute(onward, "lat", along_z(1))
    above = lax.ppermute(onward, "lat", along_z(3))
    rows, triple = kernel_call(
        bands_body,
        (shaped((16 * COARSE_DEV, WIDTH), BF), shaped((3,) + mesh_rows, BF)),
        [SMEM] + [V] * 8 + [ANY],
        (place, proc_send, onward, below, above, *quarter, c_edges),
        name="bands",
    )
    left, right = second_stage(triple)
    quarter = [rows] + [lax.ppermute(rows, "lat", along_z(s)) for s in (1, 2, 3)]
    swapped = [lax.ppermute(part, "lon", [(i, i ^ 1) for i in range(LON)]) for part in quarter]
    fine = kernel_call(
        fine_body,
        shaped(mesh_rows, F32),
        [V] * 5 + [geom_of(1), ANY, ANY],
        (m_edges, left, triple, right, proc_recv, geom, quarter[1], c_edges),
        [pltpu.VMEM((9 * MESH_NODES, WIDTH), BF)],
        flops=2 * grid_flops,
        moved=3 << 20,
        name="fine",
    )
    dec_send = kernel_call(
        mesh_body,
        shaped(mesh_rows, BF),
        [SMEM] + [V] * 12 + [geom_of(1)] + [V] * 5,
        (c_count, fine, c_edges, *quarter, *swapped, proc_recv, mesh_one, geom, *kept[6:11]),
        [pltpu.VMEM((128 * COARSE_DEV, WIDTH), BF), pltpu.VMEM(mesh_rows, F32)],
        flops=4 * grid_flops,
        moved=6 << 20,
        name="mesh",
    )
    up, down, left, right = first_stage(dec_send)
    pair = paired(up, down, dec_send)
    left_pair, right_pair = second_stage(pair)
    early = kernel_call(
        decode_early_body,
        shaped((GRID_DEGREE,) + grid_rows, F32),
        [V, V, V, V, V, V, geom_of(2)],
        (d_edges, left, dec_send, right, pair, grid_recv, geom),
        [pltpu.VMEM((5 * MESH_NODES, WIDTH), BF)],
        flops=4 * grid_flops,
        moved=8 << 20,
        name="early",
    )
    outputs = kernel_call(
        decode_body,
        shaped((head.shape[1], GRID_NODES), BF),
        [V] * 8,
        (d_edges, early, left_pair, right_pair, grid_base, *kept[11:13], head.T),
        [pltpu.VMEM((4 * MESH_NODES, WIDTH), BF), pltpu.VMEM(grid_rows, BF)],
        flops=5 * grid_flops,
        moved=8 << 20,
        name="decode",
    )
    return outputs.T[None, None]


def solution(mesh):
    return jax.shard_map(
        per_device,
        mesh=mesh,
        in_specs=(
            P("lat", "lon", None, None),
            P("lat", "lon", None, None),
            P(),
            P(),
            P(),
            P(),
            P(),
            P(),
            P(),
            P("lat", "lon", None),
            P("lat", "lon", None),
            P("lat", "lon"),
            P("lat", "lon", None, None),
            P("lat", "lon", None),
            P("lat", "lon", None, None),
            P("lat", "lon", None),
            P("lat", "lon", None),
            P("lat", "lon", None, None),
            P("lat", "lon", None),
            P("lat", "lon", None, None),
        ),
        out_specs=P("lat", "lon", None, None),
        check_vma=False,
    )
```

```python
import functools

import jax
import jax.numpy as jnp
from jax import lax
from jax.experimental import pallas as pl
from jax.experimental.pallas import tpu as pltpu
from jax.sharding import PartitionSpec as P

BF = jnp.bfloat16
F32 = jnp.float32
I32 = jnp.int32
WIDTH = 512
GRID_NODES = 1024
MESH_NODES = 128
MESH_DEGREE = 6
GRID_DEGREE = 3
COARSE_DEV = 16
SLOTS = 2048
CHUNK = 512
CHUNKS = SLOTS // CHUNK
LISTED = MESH_NODES + 8 * CHUNKS
PAYLOAD = LISTED + 16
COARSE_EDGES = 256
LON = 16
NEAR_SLOTS = 160
COARSE_SLOTS = 320
GROUPS = (5, 3, 7, 0, 1, 2, 6, 4, 8)
VMEM_BYTES = 14 * 1024 * 1024


def mm(left, right):
    return jnp.dot(left, right, preferred_element_type=F32)


def mm_t(left, right):
    return lax.dot_general(left, right, (((0,), (0,)), ((), ())), preferred_element_type=F32)


def mm_nt(left, right):
    return lax.dot_general(left, right, (((1,), (1,)), ((), ())), preferred_element_type=F32)


def silu(v):
    half = 0.5 * v
    return half + half * jnp.tanh(half)


def one_hot(column, width):
    spots = lax.broadcasted_iota(I32, (column.shape[0], width), 1)
    return jnp.where(spots == column, 1.0, 0.0).astype(BF)


class Load:
    def __init__(self, index, shape):
        self.index, self.shape = index, shape


class View:
    def __init__(self, index):
        self.index = index


class Arriving:
    def __init__(self, copy, ref):
        self.copy, self.ref = copy, ref
        self.shape = ref.shape

    def ready(self):
        if self.copy is not None:
            self.copy.wait()
            self.copy = None
        return self.ref

    def __getitem__(self, index):
        return self.ready()[index]


V = pl.BlockSpec(memory_space=pltpu.VMEM)
SMEM = pl.BlockSpec(memory_space=pltpu.SMEM)
ANY = pl.BlockSpec(memory_space=pl.ANY)
HBM = pl.BlockSpec(memory_space=pltpu.HBM)


def square(block, kind):
    return Load((block, kind), (WIDTH, WIDTH))


def first_half(block, half):
    return Load((block, slice(WIDTH * half, WIDTH * (half + 1))), (WIDTH, WIDTH))


def second_of(block):
    return Load((block,), (WIDTH, WIDTH))


KEPT = (
    ("first", first_half(0, 0)), ("second", second_of(0)), ("square", square(1, 0)), ("square", square(1, 1)),
    ("first", first_half(1, 0)), ("second", second_of(1)), ("square", square(2, 0)),
)
ENCODER = (square(0, 0),)


def kernel_call(body, outs, specs, args, scratch=(), flops=0, moved=0, name=None, out_specs=None):
    loads = [(k, spec, args[k].dtype) for k, spec in enumerate(specs) if isinstance(spec, Load)]
    n_in, n_loads = len(specs), len(loads)

    def run(*refs):
        given, rest = list(refs[:n_in]), list(refs[n_in:])
        if n_loads:
            sems = rest[-1]
            buffers = rest[-1 - n_loads : -1]
            rest = rest[: -1 - n_loads]
            for at, ((k, spec, _), buffer) in enumerate(zip(loads, buffers)):
                source = given[k].at[spec.index] if spec.index else given[k]
                copy = pltpu.make_async_copy(source, buffer, sems.at[at])
                copy.start()
                given[k] = Arriving(copy, buffer)
        for k, spec in enumerate(specs):
            if isinstance(spec, View):
                given[k] = given[k].at[spec.index]
        body(*given, *rest)
        for part in given:
            if isinstance(part, Arriving):
                part.ready()

    extra = [pltpu.VMEM(spec.shape, dtype) for _, spec, dtype in loads]
    if loads:
        extra.append(pltpu.SemaphoreType.DMA((n_loads,)))
    many = isinstance(outs, tuple)
    args = [
        pltpu.with_memory_space_constraint(arg, pltpu.HBM) if spec is HBM or isinstance(spec, Load) else arg
        for spec, arg in zip(specs, args)
    ]
    return pl.pallas_call(
        run,
        out_shape=outs,
        in_specs=[HBM if isinstance(q, Load) else V if isinstance(q, View) else q for q in specs],
        out_specs=out_specs if out_specs is not None else (V,) * len(outs) if many else V,
        scratch_shapes=list(scratch) + extra,
        compiler_params=pltpu.CompilerParams(vmem_limit_bytes=VMEM_BYTES),
        cost_estimate=pl.CostEstimate(flops=flops, bytes_accessed=moved, transcendentals=0),
        name=name,
    )(*args)


def shaped(shape, dtype):
    return jax.ShapeDtypeStruct(shape, dtype)


def fill_list(scr, width, indices, geometry):
    for row, value in enumerate(indices):
        scr[row : row + 1, 0:width] = value.astype(F32)
    high = geometry.astype(BF).astype(F32)
    scr[4:8, 0:width] = high
    scr[8:12, 0:width] = geometry - high
    scr[12:16, 0:width] = high


def pack_body(
    count, senders, receivers, geometry, state, c_senders, c_receivers, c_geometry, weight,
    out, own, coarse, w_out, scr, short,
):
    for c in range(CHUNKS):
        cols = slice(c * CHUNK, (c + 1) * CHUNK)
        s = senders[:, cols]
        edge = lax.broadcasted_iota(I32, (1, CHUNK), 1) + c * CHUNK
        code = jnp.where(edge < count[0, 0], lax.shift_right_logical(s, 10) + 1, 0)
        local = s & (GRID_NODES - 1)
        fill_list(
            scr, CHUNK, (code, lax.shift_right_logical(local, 8), local & 255, receivers[:, cols]), geometry[:, cols]
        )
        own[16 * c : 16 * (c + 1), :] = scr[...].astype(BF)
        short[8 * c : 8 * (c + 1), :] = scr[0:8, :]
    out[MESH_NODES:LISTED, :] = short[...].astype(BF)
    s = c_senders[...]
    r = c_receivers[...]
    n = s.shape[1]
    fill_list(
        scr, n, (lax.shift_right_logical(s, 8), s & 255, lax.shift_right_logical(r, 4), r & 15), c_geometry[...]
    )
    out[LISTED:PAYLOAD, :] = scr[...].astype(BF)
    coarse[...] = scr[:, 0:n].astype(BF)
    zero = jnp.zeros((4, WIDTH), F32)
    for k in range(3):
        w = weight[k]
        high = w.astype(BF).astype(F32)
        scr[0:4, :] = zero
        scr[4:8, :] = high
        scr[8:12, :] = high
        scr[12:16, :] = w - high
        w_out[k] = scr[...].astype(BF)
        if k == 0:
            scr[8:12, :] = zero
            w_out[3] = scr[...].astype(BF)
    out[0:MESH_NODES, :] = state[...]


def prep_body(m_senders, m_geometry, d_senders, d_geometry, left, right, order, *refs):
    n = len(KEPT)
    sources, (m_out, d_out, o_left, o_right) = refs[:n], refs[n : n + 4]
    kept, (scr, turned, sems) = refs[n + 4 : -3], refs[-3:]
    o_left[...] = left[...]
    o_right[...] = right[...]
    copies = bring(sources, [load for _, load in KEPT], kept, sems)
    for senders, geometry, degree, out in (
        (m_senders, m_geometry, MESH_DEGREE, m_out),
        (d_senders, d_geometry, GRID_DEGREE, d_out),
    ):
        n = senders.shape[1]
        s = senders[...]
        near = lax.shift_right_logical(s, 7)
        spot = jnp.zeros_like(near)
        for place, group in enumerate(GROUPS):
            spot = jnp.where(near == place, group, spot)
        spot = spot * MESH_NODES + (s & (MESH_NODES - 1))
        zero = jnp.zeros((1, n), F32)
        fill_list(scr, n, (spot, zero, zero, zero), geometry[...])
        turned[0:n, :] = scr[:, 0:n].T
        for t in range(degree):
            out[t] = turned[pl.ds(t, n // degree, stride=degree), :]
    for copy in copies:
        copy.wait()


def embed_body(x, w_in, w_out, source, latent, w_send, sems):
    copies = bring((source,), ENCODER, (w_send,), sems)
    for b in range(4):
        rows = slice(256 * b, 256 * (b + 1))
        hidden = silu(mm_t(x[:, rows], w_in[...])).astype(BF)
        latent[rows, :] = mm(hidden, w_out[...]).astype(BF)
    for copy in copies:
        copy.wait()


def send_body(latent, w_send, order, order_too, send):
    for b in range(4):
        rows = slice(256 * b, 256 * (b + 1))
        send[rows, :] = mm(latent[rows, :], w_send[...]).astype(BF)


def grid_body(latent, w_recv, w_first, order, recv, base):
    for b in range(4):
        rows = slice(256 * b, 256 * (b + 1))
        recv[rows, :] = mm(latent[rows, :], w_recv[...]).astype(BF)
        base[rows, :] = mm(latent[rows, :], w_first[...])


def bring(sources, loads, outs, sems):
    copies = []
    for k, load in enumerate(loads):
        copies.append(pltpu.make_async_copy(sources[k].at[load.index], outs[k], sems.at[k]))
        copies[-1].start()
    return copies


def fold_body(*refs):
    for k in range(3):
        refs[7 + k][...] = mm(refs[2 * k][...], refs[2 * k + 1][...]).astype(BF)


def self_body(chunks, state, listed, send, w_recv, w_geom, *refs):
    total = jnp.zeros((MESH_NODES, WIDTH), F32) if len(refs) == 1 else refs[0][...]
    if len(refs) == 2 and refs[1].shape == (32, WIDTH):
        refs[1][...] = listed[32:64, :]
        out = refs[0]
        total = jnp.zeros((MESH_NODES, WIDTH), F32)
    else:
        out = refs[-1]
    q = None
    for c in chunks:
        d = listed[16 * c : 16 * (c + 1), :].astype(F32).T
        s = (d[:, 1:2] * 256.0 + d[:, 2:3]).astype(I32)
        r = jnp.where(d[:, 0:1] == 5.0, d[:, 3:4], -1.0).astype(I32)
        pick = one_hot(r, MESH_NODES)
        pre = mm(one_hot(s, GRID_NODES), send[...]) + mm(d.astype(BF), w_geom[...])
        if q is None:
            q = mm(state[...], w_recv[...]).astype(BF)
        total += mm_t(pick, silu(pre + mm(pick, q)).astype(BF))
    out[...] = total


def near_body(buckets, place, *refs):
    sources, refs = refs[: len(buckets)], refs[len(buckets) :]
    if len(refs) == 16:
        beside, order_first, order_last, *refs = refs
    send, w_recv, w_geom, *refs = refs
    outs, refs = refs[: len(buckets)], refs[len(buckets) :]
    if len(refs) == 6 and buckets[0] != 5:
        following, *refs = refs
        n = COARSE_EDGES
        last = (place[0, 4] & (LON - 1)) == LON - 1
        following[...] = jnp.where(
            last, sources[-1][LISTED:PAYLOAD, 0:n].astype(F32), beside[...].astype(F32)
        ).astype(BF)
    if len(buckets) == 4 and buckets[0] == 5:
        following, *refs = refs
        following[...] = sources[1][LISTED:PAYLOAD, 0:COARSE_EDGES]
    masks, ranks, q, edges, sums = refs
    band = lax.shift_right_logical(place[0, 4], 4)
    lists = tuple(zip(sources, buckets, outs))
    q[...] = jnp.zeros_like(q)

    def listed(src, c):
        return src[MESH_NODES:LISTED, :].astype(F32)[8 * c : 8 * (c + 1), :]

    def geometry_part(d):
        return mm(jnp.concatenate([d, d], axis=1).astype(BF), w_geom[...])

    for i, (src, bucket, _) in enumerate(lists):
        for c in range(CHUNKS):
            row = i * CHUNKS + c
            code = listed(src, c)[0:1, :]
            wanted = float(bucket + 1)
            if bucket < 3 or bucket > 5:
                wanted = jnp.where(band == (7 if bucket < 3 else 0), -1.0, wanted)
            masks[row : row + 1, :] = jnp.where(code == wanted, 1.0, 0.0)
    n = masks.shape[0]
    mask = masks[...]
    before = lax.broadcasted_iota(I32, (CHUNK, CHUNK), 0) < lax.broadcasted_iota(I32, (CHUNK, CHUNK), 1)
    inside = mm(mask.astype(BF), jnp.where(before, 1.0, 0.0).astype(BF))
    mine = lax.broadcasted_iota(I32, (n, n), 0)
    other = lax.broadcasted_iota(I32, (n, n), 1)
    same = mine // CHUNKS == other // CHUNKS
    earlier = jnp.where((other < mine) & same, 1.0, 0.0).astype(BF)
    carried = mm(earlier, mask.astype(BF)).sum(axis=1, keepdims=True)
    ranks[...] = jnp.where(mask > 0.5, inside + carried, -1.0).astype(I32)

    slot = lax.broadcasted_iota(I32, (NEAR_SLOTS, CHUNK), 0)
    for i, (src, _, _) in enumerate(lists):
        d = jnp.zeros((NEAR_SLOTS, 8), F32)
        for c in range(CHUNKS):
            row = i * CHUNKS + c
            d += mm_nt(jnp.where(slot == ranks[row : row + 1, :], 1.0, 0.0).astype(BF), listed(src, c).astype(BF))
        edges[NEAR_SLOTS * i : NEAR_SLOTS * (i + 1), :] = d
    received = mm(jnp.concatenate([src[0:MESH_NODES, :] for src in sources], axis=0), w_recv[...]).astype(BF)
    d = edges[...]
    s = (d[:, 1:2] * 256.0 + d[:, 2:3]).astype(I32)
    pre = mm(one_hot(s, GRID_NODES), send[...]) + geometry_part(d)
    r = jnp.where(d[:, 0:1] > 0.5, d[:, 3:4], -1.0).astype(I32)
    for i, bucket in enumerate(buckets):
        part = slice(NEAR_SLOTS * i, NEAR_SLOTS * (i + 1))
        rows = slice(MESH_NODES * bucket, MESH_NODES * (bucket + 1))
        mine = received[MESH_NODES * i : MESH_NODES * (i + 1), :]
        q[rows, :] = mine
        pick = one_hot(r[part, :], MESH_NODES)
        sums[rows, :] = mm_t(pick, silu(pre[part, :] + mm(pick, mine)).astype(BF))

    count = mm(jnp.where(same, 1.0, 0.0).astype(BF), mask.astype(BF)).sum(axis=1, keepdims=True)
    over = jnp.maximum(count - NEAR_SLOTS, 0.0)
    total = lax.shift_right_logical(jnp.sum(over).astype(I32), 2)

    @pl.when(total > 0)
    def _():
        across = lax.broadcasted_iota(I32, (n, 1), 0) // CHUNKS
        base = jnp.zeros((n, 1), F32)
        for i in range(len(lists) - 1):
            base += jnp.where(across > i, over[i * CHUNKS : i * CHUNKS + 1, :], 0.0)
        rank = ranks[...]
        ranks[...] = jnp.where(rank >= NEAR_SLOTS, rank - NEAR_SLOTS + base.astype(I32), -1)

        @pl.loop(0, lax.shift_right_logical(total + 127, 7))
        def _(k):
            late = lax.broadcasted_iota(I32, (128, CHUNK), 0) + k * 128
            d = jnp.zeros((128, 8), F32)
            for i, (src, _, _) in enumerate(lists):
                for c in range(CHUNKS):
                    row = i * CHUNKS + c
                    d += mm_nt(jnp.where(late == ranks[row : row + 1, :], 1.0, 0.0).astype(BF), listed(src, c).astype(BF))
            s = (d[:, 1:2] * 256.0 + d[:, 2:3]).astype(I32)
            code = d[:, 0:1]
            r = jnp.where(code > 0.5, (code - 1.0) * float(MESH_NODES) + d[:, 3:4], -1.0).astype(I32)
            pick = one_hot(r, 9 * MESH_NODES)
            pre = mm(one_hot(s, GRID_NODES), send[...]) + mm(pick, q[...]) + geometry_part(d)
            sums[...] += mm_t(pick, silu(pre).astype(BF))

    for _, bucket, dst in lists:
        dst[...] = sums[MESH_NODES * bucket : MESH_NODES * (bucket + 1), :].astype(BF)


def corner_body(a, b, c, d, left, right):
    left[0] = a[...]
    left[1] = b[...]
    right[0] = c[...]
    right[1] = d[...]


def side_sum_body(place, above, below, from_left, from_right, order, first, second):
    odd = odd_band(place)
    for k, middle, when_odd, when_even in ((0, above, first, second), (1, below, second, first)):
        total = (middle[...].astype(F32) + from_left[k].astype(F32) + from_right[k].astype(F32)).astype(BF)

        @pl.when(odd)
        def _(total=total, out=when_odd):
            out[...] = total

        @pl.when(jnp.logical_not(odd))
        def _(total=total, out=when_even):
            out[...] = total


def join_body(parts, out):
    n = parts[0].shape[0]
    for k, part in enumerate(parts):
        out[n * k : n * (k + 1), :] = part[...]


def odd_band(place):
    return (lax.shift_right_logical(place[0, 4], 4) & 1) == 1


def pair_body(place, first, second, order, out):
    odd = odd_band(place)

    @pl.when(odd)
    def _():
        out[0] = first[...]
        out[1] = second[...]

    @pl.when(jnp.logical_not(odd))
    def _():
        out[0] = second[...]
        out[1] = first[...]


def partner_body(own, partner, low, both, order, out, onward):
    n = COARSE_DEV
    onward[...] = partner[...]
    for k, part in enumerate((own[...], partner[0:n, :], low[...], both[...])):
        out[n * k : n * (k + 1), :] = part


def bands_body(place, own, partner, below, above, a, b, c, d, order, out, triple):
    join_body((a, b, c, d), out)
    triple[1] = own[...]
    odd = place[0, 2] >= 2

    @pl.when(odd)
    def _():
        triple[0] = partner[...]
        triple[2] = above[...]

    @pl.when(jnp.logical_not(odd))
    def _():
        triple[0] = below[...]
        triple[2] = partner[...]


def node_rows(v, hidden_total, first_node, folded, second):
    u = silu(mm(v, first_node) + mm(hidden_total.astype(BF), folded)).astype(BF)
    return (v.astype(F32) + mm(u, second)).astype(BF)


def node_body(
    own, from_left, from_right, up, down, state, folded, first_node, second, w_send, w_recv, order,
    mesh_one, send, recv, coarse,
):
    total = own[...] + from_left[...].astype(F32) + from_right[...].astype(F32)
    total = total + up[...].astype(F32) + down[...].astype(F32)
    one = node_rows(state[...], total, first_node[...], folded[...], second[...])
    mesh_one[...] = one
    sent = mm(one, w_send[...]).astype(BF)
    send[...] = sent
    coarse[...] = sent[0:COARSE_DEV, :]
    recv[...] = mm(one, w_recv[...]).astype(BF)


def fine_body(edges, left, own, right, recv, w_geom, order, order_too, out, rows):
    parts = (left[1], own[1], right[1], own[0], own[2], left[0], left[2], right[0], right[2])
    for k, part in enumerate(parts):
        rows[MESH_NODES * k : MESH_NODES * (k + 1), :] = part
    q = recv[...].astype(F32)
    total = jnp.zeros((MESH_NODES, WIDTH), F32)
    for t in range(MESH_DEGREE):
        d = edges[t]
        spread = one_hot(d[:, 0:1].astype(I32), 9 * MESH_NODES)
        pre = q + mm(spread, rows[...]) + mm(d.astype(BF), w_geom[...])
        total += silu(pre)
    out[...] = total


def coarse_prep_body(place, own, following, far, out, count, row):
    z, y, x, core, tile = (place[0, k] for k in range(5))
    n = COARSE_EDGES
    lists = (own[...], following[...], far[...])
    for k, edges in enumerate(lists):
        owner = edges.astype(F32)[2:3, :].astype(I32)
        row[k : k + 1, :] = jnp.where(owner == tile, 1.0, 0.0)
    row[3:8, :] = jnp.zeros((5, n), F32)
    mask = row[...]
    before = lax.broadcasted_iota(I32, (n, n), 0) < lax.broadcasted_iota(I32, (n, n), 1)
    inside = mm(mask.astype(BF), jnp.where(before, 1.0, 0.0).astype(BF))
    earlier = lax.broadcasted_iota(I32, (8, 8), 1) < lax.broadcasted_iota(I32, (8, 8), 0)
    carried = mm(jnp.where(earlier, 1.0, 0.0).astype(BF), mask.astype(BF)).sum(axis=1, keepdims=True)
    rank = jnp.where(mask > 0.5, inside + carried, -1.0).astype(I32)
    slot = lax.broadcasted_iota(I32, (3 * n, n), 0)
    d = jnp.zeros((3 * n, 16), F32)
    for k, edges in enumerate(lists):
        d += mm_nt(jnp.where(slot == rank[k : k + 1, :], 1.0, 0.0).astype(BF), edges)
    s = (d[:, 0:1] * 256.0 + d[:, 1:2]).astype(I32)
    t = lax.shift_right_logical(s, 4)
    lat = lax.shift_right_logical(t, 4)
    lon = t & 15
    gz = (z - lax.shift_right_logical(lat, 1)) & 3
    gy = (y - lax.shift_right_logical(lon, 2)) & 3
    g_high = (lax.shift_right_logical(x, 1) + lat) & 1
    g_low = (x + lax.shift_right_logical(lon, 1)) & 1
    gc = (core + lon) & 1
    spot = ((((gc * 4 + gz) * 4 + gy) * 2 + g_low) * 2 + g_high) * 16 + (s & 15)
    total = jnp.sum(mask).astype(I32)
    used = lax.broadcasted_iota(I32, (3 * n, 1), 0) < total
    r = jnp.where(used, d[:, 3:4], -1.0)
    lane = lax.broadcasted_iota(I32, (3 * n, 16), 1)
    out[...] = jnp.where(lane == 0, spot.astype(F32), jnp.where(lane == 1, r, d))
    count[0, 0] = total


def mesh_body(
    count, fine, edges, a0, a1, a2, a3, b0, b1, b2, b3, recv, mesh_one, w_geom, folded, first_node, second, w_send,
    send, rows, total,
):
    parts = (a0, a1, a2, a3, b0, b1, b2, b3)
    n = a0.shape[0]
    for k, part in enumerate(parts):
        rows[n * k : n * (k + 1), :] = part[...]
    q = recv[0:COARSE_DEV, :]

    def hidden_sum(d):
        pick = one_hot(d[:, 1:2].astype(I32), MESH_NODES)
        pre = mm(one_hot(d[:, 0:1].astype(I32), len(parts) * n), rows[...])
        pre += mm(pick[:, 0:COARSE_DEV], q) + mm(d.astype(BF), w_geom[...])
        return mm_t(pick, silu(pre).astype(BF))

    total[...] = fine[...] + hidden_sum(edges[0:COARSE_SLOTS, :])

    @pl.loop(COARSE_SLOTS // 64, lax.shift_right_logical(count[0, 0] + 63, 6))
    def _(k):
        total[...] += hidden_sum(edges[pl.ds(pl.multiple_of(64 * k, 64), 64), :])

    two = node_rows(mesh_one[...], total[...], first_node[...], folded[...], second[...])
    send[...] = mm(two, w_send[...]).astype(BF)


def decode_early_body(edges, left, own, right, pair, recv, w_geom, out, rows):
    for k, part in enumerate((left, own, right, pair.at[0], pair.at[1])):
        rows[MESH_NODES * k : MESH_NODES * (k + 1), :] = part[...]
    n = 5 * MESH_NODES

    @pl.loop(0, 4)
    def _(b):
        span = pl.ds(pl.multiple_of(256 * b, 256), 256)
        q = recv[span, :].astype(F32)
        for t in range(GRID_DEGREE):
            d = edges[t, span, :]
            spread = one_hot(d[:, 0:1].astype(I32), n)
            out[t, span, :] = q + mm(spread, rows[0:n, :]) + mm(d.astype(BF), w_geom[...])


def decode_body(edges, early, left_pair, right_pair, base, folded, head, out, rows, totals):
    for k, part in enumerate((left_pair.at[0], left_pair.at[1], right_pair.at[0], right_pair.at[1])):
        rows[MESH_NODES * k : MESH_NODES * (k + 1), :] = part[...]
    for b in range(4):
        span = slice(256 * b, 256 * (b + 1))
        total = jnp.zeros((256, WIDTH), F32)
        for t in range(GRID_DEGREE):
            spot = edges[t, span, :][:, 0:1].astype(I32) - 5 * MESH_NODES
            total += silu(early[t, span, :] + mm(one_hot(spot, 4 * MESH_NODES), rows[...]))
        totals[span, :] = total.astype(BF)
    for b in range(2):
        span = slice(512 * b, 512 * (b + 1))
        hidden = silu(base[span, :] + mm(totals[span, :], folded[...])).astype(BF)
        out[:, span] = mm_nt(head[...], hidden).astype(BF)


def shift(value, axis, step, periodic):
    n = lax.axis_size(axis)
    pairs = [(i, (i + step) % n) for i in range(n) if periodic or 0 <= i + step < n]
    return lax.ppermute(value, axis, pairs)


def swap_bands(first, second, wrap=False):
    later = [(i, (i + 1) % 8) for i in (1, 3, 5, 7) if wrap or i < 7]
    later += [(target, source) for source, target in later]
    second = lax.ppermute(second, "lat", later)
    return lax.ppermute(first, "lat", [(i, i ^ 1) for i in range(8)]), second


def first_stage(value, wrap=False):
    first, second = swap_bands(value, value, wrap)
    return first, second, shift(value, "lon", 1, True), shift(value, "lon", -1, True)


def second_stage(pair):
    return shift(pair, "lon", 1, True), shift(pair, "lon", -1, True)


def along_z(s):
    return [(i, ((i // 2 + s) % 4) * 2 + i % 2) for i in range(8)]


def along_y(s):
    return [(i, ((i // 4 + s) % 4) * 4 + i % 4) for i in range(16)]


def per_device(
    grid_inputs,
    mesh_state,
    embed_in,
    embed_out,
    edge_square,
    edge_geom_weight,
    node_first,
    node_second,
    head,
    g2m_senders,
    g2m_receivers,
    g2m_counts,
    g2m_geom,
    mesh_senders,
    mesh_geom,
    coarse_senders,
    coarse_receivers,
    coarse_geom,
    m2g_senders,
    m2g_geom,
):
    mesh_rows = (MESH_NODES, WIDTH)
    grid_rows = (GRID_NODES, WIDTH)
    pair_rows = (2,) + mesh_rows
    grid_flops = 2 * GRID_NODES * WIDTH * WIDTH
    mesh_flops = grid_flops // 8
    both = ("lat", "lon")
    tiles = lax.axis_size(both)
    lat, lon = lax.axis_index("lat"), lax.axis_index("lon")
    place = jnp.stack([lat // 2, lon // 4, (lat % 2) * 2 + (lon // 2) % 2, lon % 2, lat * LON + lon])[None]
    place = place.astype(I32)

    pack_args = (
        g2m_senders, g2m_receivers, g2m_geom, mesh_state, coarse_senders, coarse_receivers, coarse_geom
    )

    def part_of(array):
        n = array.ndim - 2
        return Load((0,) if n == 1 else (0, 0), array.shape[1:] if n == 1 else array.shape[2:])

    payload, own_list, coarse_list, geom = kernel_call(
        pack_body,
        (
            shaped((PAYLOAD, WIDTH), BF), shaped((16 * CHUNKS, WIDTH), BF), shaped((16, COARSE_EDGES), BF),
            shaped((4, 16, WIDTH), BF),
        ),
        [SMEM] + [part_of(a) for a in pack_args] + [Load((), edge_geom_weight.shape)],
        (g2m_counts,) + pack_args + (edge_geom_weight,),
        [pltpu.VMEM((16, CHUNK), F32), pltpu.VMEM((8 * CHUNKS, CHUNK), F32)],
        name="pack",
    )
    first, second, near_left, near_right = first_stage(payload, True)
    turned_inputs = jnp.swapaxes(grid_inputs, 2, 3)
    latent, w_send = kernel_call(
        embed_body,
        (shaped(grid_rows, BF), shaped((WIDTH, WIDTH), BF)),
        [part_of(turned_inputs), Load((), embed_in.shape), Load((), embed_out.shape), HBM],
        (turned_inputs, embed_in, embed_out, edge_square),
        [pltpu.SemaphoreType.DMA((1,))],
        flops=2 * grid_flops,
        moved=4 << 20,
        name="embed",
    )
    grid_send = kernel_call(
        send_body,
        shaped(grid_rows, BF),
        [V, V, ANY, ANY],
        (latent, w_send, near_left, near_right),
        flops=grid_flops,
        moved=3 << 20,
        name="send",
    )

    def geom_of(k):
        return View(k)

    own_specs = [part_of(mesh_state), V, V, square(0, 1), geom_of(0)]
    own_args = (mesh_state, own_list, grid_send, edge_square, geom)

    def paired(first, second, order):
        shape = (2,) + first.shape
        return kernel_call(
            pair_body, shaped(shape, BF), [SMEM, V, V, ANY], (place, first, second, order), name="pair"
        )

    own_first, list_rest = kernel_call(
        functools.partial(self_body, (0, 1)),
        (shaped(mesh_rows, F32), shaped((32, WIDTH), BF)),
        own_specs,
        own_args,
        flops=2 * grid_flops,
        moved=3 << 20,
        name="own_first",
    )
    near_middle = paired(first, second, own_first)
    near_left_pair, near_right_pair = second_stage(near_middle)
    own_sum = kernel_call(
        functools.partial(self_body, (0, 1)),
        shaped(mesh_rows, F32),
        own_specs + [V],
        (mesh_state, list_rest, grid_send, edge_square, geom, own_first),
        flops=2 * grid_flops,
        moved=3 << 20,
        name="own_last",
    )
    near_scratch = [
        pltpu.VMEM((4 * CHUNKS, CHUNK), F32),
        pltpu.VMEM((4 * CHUNKS, CHUNK), I32),
        pltpu.VMEM((9 * MESH_NODES, WIDTH), BF),
        pltpu.VMEM((4 * NEAR_SLOTS, 8), F32),
        pltpu.VMEM((9 * MESH_NODES, WIDTH), F32),
    ]
    near_weights = [V, square(0, 1), geom_of(3)]
    to_left, to_right, to_above, to_below, right_list = kernel_call(
        functools.partial(near_body, (5, 3, 7, 1)),
        (shaped(mesh_rows, BF),) * 4 + (shaped((16, COARSE_EDGES), BF),),
        [SMEM, V, V, View(0), View(1)] + near_weights,
        (place, near_left, near_right, near_middle, near_middle, grid_send, edge_square, geom),
        near_scratch,
        flops=2 * grid_flops,
        moved=5 << 20,
        name="beside",
    )
    *to_corners, coarse_next = kernel_call(
        functools.partial(near_body, (8, 2, 6, 0)),
        (shaped(mesh_rows, BF),) * 4 + (shaped((16, COARSE_EDGES), BF),),
        [SMEM, View(0), View(1), View(0), View(1), V, ANY, ANY] + near_weights,
        (
            place, near_left_pair, near_left_pair, near_right_pair, near_right_pair, right_list, own_sum, to_left,
            grid_send, edge_square, geom,
        ),
        near_scratch,
        flops=2 * grid_flops,
        moved=5 << 20,
        name="corners",
    )
    to_left_pair, to_right_pair = kernel_call(
        corner_body, (shaped(pair_rows, BF),) * 2, [V] * 4, tuple(to_corners), name="corner_pairs"
    )
    pair_left = shift(to_right_pair, "lon", 1, True)
    pair_right = shift(to_left_pair, "lon", -1, True)
    prep_args = (mesh_senders, mesh_geom, m2g_senders, m2g_geom)
    stored = {"square": edge_square, "first": node_first, "second": node_second}
    m_edges, d_edges, to_left, to_right, *kept = kernel_call(
        prep_body,
        (
            shaped((MESH_DEGREE, MESH_NODES, 16), F32),
            shaped((GRID_DEGREE, GRID_NODES, 16), F32),
            shaped(mesh_rows, BF),
            shaped(mesh_rows, BF),
        ) + (shaped((WIDTH, WIDTH), BF),) * len(KEPT),
        [part_of(a) for a in prep_args] + [V, V, ANY] + [HBM] * len(KEPT),
        prep_args + (to_left, to_right, to_left_pair) + tuple(stored[name] for name, _ in KEPT),
        [pltpu.VMEM((16, 3072), F32), pltpu.VMEM((3072, 16), F32), pltpu.SemaphoreType.DMA((len(KEPT),))],
        flops=grid_flops,
        name="prep",
    )
    to_first, to_second = kernel_call(
        side_sum_body,
        (shaped(mesh_rows, BF),) * 2,
        [SMEM, V, V, V, V, ANY],
        (place, to_above, to_below, pair_left, pair_right, m_edges),
        name="sides",
    )
    up, down = swap_bands(to_first, to_second)
    folded = kernel_call(
        fold_body,
        (shaped((WIDTH, WIDTH), BF),) * 3,
        [part for k in range(3) for part in (square(k, 2), first_half(k, 1))] + [ANY],
        (edge_square, node_first) * 3 + (to_first,),
        flops=3 * grid_flops // 2,
        moved=4 << 20,
        name="fold",
    )
    from_left = shift(to_right, "lon", 1, True)
    from_right = shift(to_left, "lon", -1, True)
    far_list = lax.ppermute(coarse_list, both, [(t, (t + tiles // 2) % tiles) for t in range(tiles)])
    mesh_one, proc_send, proc_recv, coarse_own = kernel_call(
        node_body,
        (shaped(mesh_rows, BF),) * 3 + (shaped((COARSE_DEV, WIDTH), BF),),
        [V] * 5 + [part_of(mesh_state)] + [V] * 5 + [ANY],
        (own_sum, from_left, from_right, up, down, mesh_state, folded[0], *kept[0:4], far_list),
        flops=7 * mesh_flops,
        moved=4 << 20,
        name="node",
    )
    grid_recv, grid_base = kernel_call(
        grid_body,
        (shaped(grid_rows, BF), shaped(grid_rows, F32)),
        [V, square(2, 1), first_half(2, 0), ANY],
        (latent, edge_square, node_first, proc_send),
        flops=2 * grid_flops,
        moved=5 << 20,
        name="grid",
    )
    def half(t):
        return (t // LON ^ 1) * LON + (t % LON)

    partner = lax.ppermute(proc_send, "lat", [(i, i ^ 1) for i in range(8)])
    low = lax.ppermute(coarse_own, "lon", [(i, i ^ 2) for i in range(LON)])
    cross = lax.ppermute(coarse_own, both, [(t, half(t) ^ 2) for t in range(tiles)])
    beside, onward = kernel_call(
        partner_body,
        (shaped((4 * COARSE_DEV, WIDTH), BF), shaped(mesh_rows, BF)),
        [V, V, V, V, ANY],
        (coarse_own, partner, low, cross, grid_recv),
        name="partner",
    )
    edge_total = 3 * COARSE_EDGES
    c_edges, c_count = kernel_call(
        coarse_prep_body,
        (shaped((edge_total, 16), F32), shaped((1, 1), I32)),
        [SMEM, V, V, V],
        (place, coarse_list, coarse_next, far_list),
        [pltpu.VMEM((8, COARSE_EDGES), F32)],
        flops=mesh_flops,
        name="coarse_edges",
        out_specs=(V, SMEM),
    )
    quarter = [beside] + [lax.ppermute(beside, "lon", along_y(s)) for s in (1, 2, 3)]
    below = lax.ppermute(onward, "lat", along_z(1))
    above = lax.ppermute(onward, "lat", along_z(3))
    rows, triple = kernel_call(
        bands_body,
        (shaped((16 * COARSE_DEV, WIDTH), BF), shaped((3,) + mesh_rows, BF)),
        [SMEM] + [V] * 8 + [ANY],
        (place, proc_send, onward, below, above, *quarter, c_edges),
        name="bands",
    )
    left, right = second_stage(triple)
    quarter = [rows] + [lax.ppermute(rows, "lat", along_z(s)) for s in (1, 2, 3)]
    swapped = [lax.ppermute(part, "lon", [(i, i ^ 1) for i in range(LON)]) for part in quarter]
    fine = kernel_call(
        fine_body,
        shaped(mesh_rows, F32),
        [V] * 5 + [geom_of(1), ANY, ANY],
        (m_edges, left, triple, right, proc_recv, geom, quarter[1], c_edges),
        [pltpu.VMEM((9 * MESH_NODES, WIDTH), BF)],
        flops=2 * grid_flops,
        moved=3 << 20,
        name="fine",
    )
    dec_send = kernel_call(
        mesh_body,
        shaped(mesh_rows, BF),
        [SMEM] + [V] * 12 + [geom_of(1)] + [V] * 4,
        (c_count, fine, c_edges, *quarter, *swapped, proc_recv, mesh_one, geom, folded[1], *kept[4:7]),
        [pltpu.VMEM((128 * COARSE_DEV, WIDTH), BF), pltpu.VMEM(mesh_rows, F32)],
        flops=4 * grid_flops,
        moved=6 << 20,
        name="mesh",
    )
    first, second, left, right = first_stage(dec_send)
    pair = paired(first, second, dec_send)
    left_pair, right_pair = second_stage(pair)
    early = kernel_call(
        decode_early_body,
        shaped((GRID_DEGREE,) + grid_rows, F32),
        [V, V, V, V, V, V, geom_of(2)],
        (d_edges, left, dec_send, right, pair, grid_recv, geom),
        [pltpu.VMEM((5 * MESH_NODES, WIDTH), BF)],
        flops=4 * grid_flops,
        moved=8 << 20,
        name="early",
    )
    outputs = kernel_call(
        decode_body,
        shaped((head.shape[1], GRID_NODES), BF),
        [V] * 7,
        (d_edges, early, left_pair, right_pair, grid_base, folded[2], head.T),
        [pltpu.VMEM((4 * MESH_NODES, WIDTH), BF), pltpu.VMEM(grid_rows, BF)],
        flops=5 * grid_flops,
        moved=8 << 20,
        name="decode",
    )
    return outputs.T[None, None]


def solution(mesh):
    return jax.shard_map(
        per_device,
        mesh=mesh,
        in_specs=(
            P("lat", "lon", None, None),
            P("lat", "lon", None, None),
            P(),
            P(),
            P(),
            P(),
            P(),
            P(),
            P(),
            P("lat", "lon", None),
            P("lat", "lon", None),
            P("lat", "lon"),
            P("lat", "lon", None, None),
            P("lat", "lon", None),
            P("lat", "lon", None, None),
            P("lat", "lon", None),
            P("lat", "lon", None),
            P("lat", "lon", None, None),
            P("lat", "lon", None),
            P("lat", "lon", None, None),
        ),
        out_specs=P("lat", "lon", None, None),
        check_vma=False,
    )
```

```python
import functools

import jax
import jax.numpy as jnp
from jax import lax
from jax.experimental import pallas as pl
from jax.experimental.pallas import tpu as pltpu
from jax.sharding import PartitionSpec as P

BF = jnp.bfloat16
F32 = jnp.float32
I32 = jnp.int32
WIDTH = 512
GRID_NODES = 1024
MESH_NODES = 128
MESH_DEGREE = 6
GRID_DEGREE = 3
COARSE_DEV = 16
SLOTS = 2048
CHUNK = 512
CHUNKS = SLOTS // CHUNK
LISTED = MESH_NODES + 8 * CHUNKS
PAYLOAD = LISTED + 16
COARSE_EDGES = 256
LON = 16
NEAR_SLOTS = 160
COARSE_SLOTS = 320
GROUPS = (5, 3, 7, 0, 1, 2, 6, 4, 8)
VMEM_BYTES = 14 * 1024 * 1024


def mm(left, right):
    return jnp.dot(left, right, preferred_element_type=F32)


def mm_t(left, right):
    return lax.dot_general(left, right, (((0,), (0,)), ((), ())), preferred_element_type=F32)


def mm_nt(left, right):
    return lax.dot_general(left, right, (((1,), (1,)), ((), ())), preferred_element_type=F32)


def silu(v):
    half = 0.5 * v
    return half + half * jnp.tanh(half)


def one_hot(column, width):
    spots = lax.broadcasted_iota(I32, (column.shape[0], width), 1)
    return jnp.where(spots == column, 1.0, 0.0).astype(BF)


class Load:
    def __init__(self, index, shape):
        self.index, self.shape = index, shape


class View:
    def __init__(self, index):
        self.index = index


class Arriving:
    def __init__(self, copy, ref):
        self.copy, self.ref = copy, ref
        self.shape = ref.shape

    def ready(self):
        if self.copy is not None:
            self.copy.wait()
            self.copy = None
        return self.ref

    def __getitem__(self, index):
        return self.ready()[index]


V = pl.BlockSpec(memory_space=pltpu.VMEM)
SMEM = pl.BlockSpec(memory_space=pltpu.SMEM)
ANY = pl.BlockSpec(memory_space=pl.ANY)
HBM = pl.BlockSpec(memory_space=pltpu.HBM)


def square(block, kind):
    return Load((block, kind), (WIDTH, WIDTH))


def first_half(block, half):
    return Load((block, slice(WIDTH * half, WIDTH * (half + 1))), (WIDTH, WIDTH))


def second_of(block):
    return Load((block,), (WIDTH, WIDTH))


KEPT = (
    ("first", first_half(0, 0)), ("second", second_of(0)), ("square", square(1, 0)), ("square", square(1, 1)),
    ("first", first_half(1, 0)), ("second", second_of(1)), ("square", square(2, 0)),
)
ENCODER = (square(0, 0),)


def kernel_call(body, outs, specs, args, scratch=(), flops=0, moved=0, name=None, out_specs=None):
    loads = [(k, spec, args[k].dtype) for k, spec in enumerate(specs) if isinstance(spec, Load)]
    n_in, n_loads = len(specs), len(loads)

    def run(*refs):
        given, rest = list(refs[:n_in]), list(refs[n_in:])
        if n_loads:
            sems = rest[-1]
            buffers = rest[-1 - n_loads : -1]
            rest = rest[: -1 - n_loads]
            for at, ((k, spec, _), buffer) in enumerate(zip(loads, buffers)):
                source = given[k].at[spec.index] if spec.index else given[k]
                copy = pltpu.make_async_copy(source, buffer, sems.at[at])
                copy.start()
                given[k] = Arriving(copy, buffer)
        for k, spec in enumerate(specs):
            if isinstance(spec, View):
                given[k] = given[k].at[spec.index]
        body(*given, *rest)
        for part in given:
            if isinstance(part, Arriving):
                part.ready()

    extra = [pltpu.VMEM(spec.shape, dtype) for _, spec, dtype in loads]
    if loads:
        extra.append(pltpu.SemaphoreType.DMA((n_loads,)))
    many = isinstance(outs, tuple)
    args = [
        pltpu.with_memory_space_constraint(arg, pltpu.HBM) if spec is HBM or isinstance(spec, Load) else arg
        for spec, arg in zip(specs, args)
    ]
    return pl.pallas_call(
        run,
        out_shape=outs,
        in_specs=[HBM if isinstance(q, Load) else V if isinstance(q, View) else q for q in specs],
        out_specs=out_specs if out_specs is not None else (V,) * len(outs) if many else V,
        scratch_shapes=list(scratch) + extra,
        compiler_params=pltpu.CompilerParams(vmem_limit_bytes=VMEM_BYTES),
        cost_estimate=pl.CostEstimate(flops=flops, bytes_accessed=moved, transcendentals=0),
        name=name,
    )(*args)


def shaped(shape, dtype):
    return jax.ShapeDtypeStruct(shape, dtype)


def fill_list(scr, width, indices, geometry):
    for row, value in enumerate(indices):
        scr[row : row + 1, 0:width] = value.astype(F32)
    high = geometry.astype(BF).astype(F32)
    scr[4:8, 0:width] = high
    scr[8:12, 0:width] = geometry - high
    scr[12:16, 0:width] = high


def pack_body(
    count, senders, receivers, geometry, state, c_senders, c_receivers, c_geometry, weight,
    out, own, coarse, w_out, scr, short,
):
    for c in range(CHUNKS):
        cols = slice(c * CHUNK, (c + 1) * CHUNK)
        s = senders[:, cols]
        edge = lax.broadcasted_iota(I32, (1, CHUNK), 1) + c * CHUNK
        code = jnp.where(edge < count[0, 0], lax.shift_right_logical(s, 10) + 1, 0)
        local = s & (GRID_NODES - 1)
        fill_list(
            scr, CHUNK, (code, lax.shift_right_logical(local, 8), local & 255, receivers[:, cols]), geometry[:, cols]
        )
        own[16 * c : 16 * (c + 1), :] = scr[...].astype(BF)
        short[8 * c : 8 * (c + 1), :] = scr[0:8, :]
    out[MESH_NODES:LISTED, :] = short[...].astype(BF)
    s = c_senders[...]
    r = c_receivers[...]
    n = s.shape[1]
    fill_list(
        scr, n, (lax.shift_right_logical(s, 8), s & 255, lax.shift_right_logical(r, 4), r & 15), c_geometry[...]
    )
    out[LISTED:PAYLOAD, :] = scr[...].astype(BF)
    coarse[...] = scr[:, 0:n].astype(BF)
    zero = jnp.zeros((4, WIDTH), F32)
    for k in range(3):
        w = weight[k]
        high = w.astype(BF).astype(F32)
        scr[0:4, :] = zero
        scr[4:8, :] = high
        scr[8:12, :] = high
        scr[12:16, :] = w - high
        w_out[k] = scr[...].astype(BF)
        if k == 0:
            scr[8:12, :] = zero
            w_out[3] = scr[...].astype(BF)
    out[0:MESH_NODES, :] = state[...]


def prep_body(m_senders, m_geometry, d_senders, d_geometry, left, right, order, *refs):
    n = len(KEPT)
    sources, (m_out, d_out, o_left, o_right) = refs[:n], refs[n : n + 4]
    kept, (scr, turned, sems) = refs[n + 4 : -3], refs[-3:]
    o_left[...] = left[...]
    o_right[...] = right[...]
    copies = bring(sources, [load for _, load in KEPT], kept, sems)
    for senders, geometry, degree, out in (
        (m_senders, m_geometry, MESH_DEGREE, m_out),
        (d_senders, d_geometry, GRID_DEGREE, d_out),
    ):
        n = senders.shape[1]
        s = senders[...]
        near = lax.shift_right_logical(s, 7)
        spot = jnp.zeros_like(near)
        for place, group in enumerate(GROUPS):
            spot = jnp.where(near == place, group, spot)
        spot = spot * MESH_NODES + (s & (MESH_NODES - 1))
        zero = jnp.zeros((1, n), F32)
        fill_list(scr, n, (spot, zero, zero, zero), geometry[...])
        turned[0:n, :] = scr[:, 0:n].T
        for t in range(degree):
            out[t] = turned[pl.ds(t, n // degree, stride=degree), :]
    for copy in copies:
        copy.wait()


def embed_body(x, w_in, w_out, source, latent, w_send, sems):
    copies = bring((source,), ENCODER, (w_send,), sems)
    x, w_in, w_out = x.ready(), w_in.ready(), w_out.ready()

    @pl.loop(0, 4)
    def _(b):
        rows = pl.ds(pl.multiple_of(256 * b, 256), 256)
        hidden = silu(mm_t(x[:, rows], w_in[...])).astype(BF)
        latent[rows, :] = mm(hidden, w_out[...]).astype(BF)

    for copy in copies:
        copy.wait()


def send_body(latent, w_send, order, order_too, send):
    @pl.loop(0, 2)
    def _(b):
        rows = pl.ds(pl.multiple_of(512 * b, 512), 512)
        send[rows, :] = mm(latent[rows, :], w_send[...]).astype(BF)


def grid_body(latent, w_recv, w_first, order, recv, base):
    w_recv, w_first = w_recv.ready(), w_first.ready()

    @pl.loop(0, 4)
    def _(b):
        rows = pl.ds(pl.multiple_of(256 * b, 256), 256)
        recv[rows, :] = mm(latent[rows, :], w_recv[...]).astype(BF)
        base[rows, :] = mm(latent[rows, :], w_first[...])


def bring(sources, loads, outs, sems):
    copies = []
    for k, load in enumerate(loads):
        copies.append(pltpu.make_async_copy(sources[k].at[load.index], outs[k], sems.at[k]))
        copies[-1].start()
    return copies


def fold_body(*refs):
    for k in range(3):
        refs[7 + k][...] = mm(refs[2 * k][...], refs[2 * k + 1][...]).astype(BF)


def self_body(chunks, state, listed, send, w_recv, w_geom, *refs):
    total = jnp.zeros((MESH_NODES, WIDTH), F32) if len(refs) == 1 else refs[0][...]
    if len(refs) == 2 and refs[1].shape == (32, WIDTH):
        refs[1][...] = listed[32:64, :]
        out = refs[0]
        total = jnp.zeros((MESH_NODES, WIDTH), F32)
    else:
        out = refs[-1]
    q = None
    for c in chunks:
        d = listed[16 * c : 16 * (c + 1), :].astype(F32).T
        s = (d[:, 1:2] * 256.0 + d[:, 2:3]).astype(I32)
        r = jnp.where(d[:, 0:1] == 5.0, d[:, 3:4], -1.0).astype(I32)
        pick = one_hot(r, MESH_NODES)
        pre = mm(one_hot(s, GRID_NODES), send[...]) + mm(d.astype(BF), w_geom[...])
        if q is None:
            q = mm(state[...], w_recv[...]).astype(BF)
        total += mm_t(pick, silu(pre + mm(pick, q)).astype(BF))
    out[...] = total


def near_body(buckets, place, *refs):
    sources, refs = refs[: len(buckets)], refs[len(buckets) :]
    if len(refs) == 16:
        beside, order_first, order_last, *refs = refs
    send, w_recv, w_geom, *refs = refs
    outs, refs = refs[: len(buckets)], refs[len(buckets) :]
    if len(refs) == 6 and buckets[0] != 5:
        following, *refs = refs
        n = COARSE_EDGES
        last = (place[0, 4] & (LON - 1)) == LON - 1
        following[...] = jnp.where(
            last, sources[-1][LISTED:PAYLOAD, 0:n].astype(F32), beside[...].astype(F32)
        ).astype(BF)
    if len(buckets) == 4 and buckets[0] == 5:
        following, *refs = refs
        following[...] = sources[1][LISTED:PAYLOAD, 0:COARSE_EDGES]
    masks, ranks, q, edges, sums = refs
    band = lax.shift_right_logical(place[0, 4], 4)
    lists = tuple(zip(sources, buckets, outs))
    q[...] = jnp.zeros_like(q)

    def listed(src, c):
        return src[MESH_NODES:LISTED, :].astype(F32)[8 * c : 8 * (c + 1), :]

    def geometry_part(d):
        return mm(jnp.concatenate([d, d], axis=1).astype(BF), w_geom[...])

    for i, (src, bucket, _) in enumerate(lists):
        for c in range(CHUNKS):
            row = i * CHUNKS + c
            code = listed(src, c)[0:1, :]
            wanted = float(bucket + 1)
            if bucket < 3 or bucket > 5:
                wanted = jnp.where(band == (7 if bucket < 3 else 0), -1.0, wanted)
            masks[row : row + 1, :] = jnp.where(code == wanted, 1.0, 0.0)
    n = masks.shape[0]
    mask = masks[...]
    before = lax.broadcasted_iota(I32, (CHUNK, CHUNK), 0) < lax.broadcasted_iota(I32, (CHUNK, CHUNK), 1)
    inside = mm(mask.astype(BF), jnp.where(before, 1.0, 0.0).astype(BF))
    mine = lax.broadcasted_iota(I32, (n, n), 0)
    other = lax.broadcasted_iota(I32, (n, n), 1)
    same = mine // CHUNKS == other // CHUNKS
    earlier = jnp.where((other < mine) & same, 1.0, 0.0).astype(BF)
    carried = mm(earlier, mask.astype(BF)).sum(axis=1, keepdims=True)
    ranks[...] = jnp.where(mask > 0.5, inside + carried, -1.0).astype(I32)

    slot = lax.broadcasted_iota(I32, (NEAR_SLOTS, CHUNK), 0)
    for i, (src, _, _) in enumerate(lists):
        d = jnp.zeros((NEAR_SLOTS, 8), F32)
        for c in range(CHUNKS):
            row = i * CHUNKS + c
            d += mm_nt(jnp.where(slot == ranks[row : row + 1, :], 1.0, 0.0).astype(BF), listed(src, c).astype(BF))
        edges[NEAR_SLOTS * i : NEAR_SLOTS * (i + 1), :] = d
    received = mm(jnp.concatenate([src[0:MESH_NODES, :] for src in sources], axis=0), w_recv[...]).astype(BF)
    d = edges[...]
    s = (d[:, 1:2] * 256.0 + d[:, 2:3]).astype(I32)
    pre = mm(one_hot(s, GRID_NODES), send[...]) + geometry_part(d)
    r = jnp.where(d[:, 0:1] > 0.5, d[:, 3:4], -1.0).astype(I32)
    for i, bucket in enumerate(buckets):
        part = slice(NEAR_SLOTS * i, NEAR_SLOTS * (i + 1))
        rows = slice(MESH_NODES * bucket, MESH_NODES * (bucket + 1))
        mine = received[MESH_NODES * i : MESH_NODES * (i + 1), :]
        q[rows, :] = mine
        pick = one_hot(r[part, :], MESH_NODES)
        sums[rows, :] = mm_t(pick, silu(pre[part, :] + mm(pick, mine)).astype(BF))

    count = mm(jnp.where(same, 1.0, 0.0).astype(BF), mask.astype(BF)).sum(axis=1, keepdims=True)
    over = jnp.maximum(count - NEAR_SLOTS, 0.0)
    total = lax.shift_right_logical(jnp.sum(over).astype(I32), 2)

    @pl.when(total > 0)
    def _():
        across = lax.broadcasted_iota(I32, (n, 1), 0) // CHUNKS
        base = jnp.zeros((n, 1), F32)
        for i in range(len(lists) - 1):
            base += jnp.where(across > i, over[i * CHUNKS : i * CHUNKS + 1, :], 0.0)
        rank = ranks[...]
        ranks[...] = jnp.where(rank >= NEAR_SLOTS, rank - NEAR_SLOTS + base.astype(I32), -1)

        @pl.loop(0, lax.shift_right_logical(total + 127, 7))
        def _(k):
            late = lax.broadcasted_iota(I32, (128, CHUNK), 0) + k * 128
            d = jnp.zeros((128, 8), F32)
            for i, (src, _, _) in enumerate(lists):
                for c in range(CHUNKS):
                    row = i * CHUNKS + c
                    d += mm_nt(jnp.where(late == ranks[row : row + 1, :], 1.0, 0.0).astype(BF), listed(src, c).astype(BF))
            s = (d[:, 1:2] * 256.0 + d[:, 2:3]).astype(I32)
            code = d[:, 0:1]
            r = jnp.where(code > 0.5, (code - 1.0) * float(MESH_NODES) + d[:, 3:4], -1.0).astype(I32)
            pick = one_hot(r, 9 * MESH_NODES)
            pre = mm(one_hot(s, GRID_NODES), send[...]) + mm(pick, q[...]) + geometry_part(d)
            sums[...] += mm_t(pick, silu(pre).astype(BF))

    for _, bucket, dst in lists:
        dst[...] = sums[MESH_NODES * bucket : MESH_NODES * (bucket + 1), :].astype(BF)


def corner_body(a, b, c, d, left, right):
    left[0] = a[...]
    left[1] = b[...]
    right[0] = c[...]
    right[1] = d[...]


def side_sum_body(place, above, below, from_left, from_right, order, first, second):
    odd = odd_band(place)
    for k, middle, when_odd, when_even in ((0, above, first, second), (1, below, second, first)):
        total = (middle[...].astype(F32) + from_left[k].astype(F32) + from_right[k].astype(F32)).astype(BF)

        @pl.when(odd)
        def _(total=total, out=when_odd):
            out[...] = total

        @pl.when(jnp.logical_not(odd))
        def _(total=total, out=when_even):
            out[...] = total


def join_body(parts, out):
    n = parts[0].shape[0]
    for k, part in enumerate(parts):
        out[n * k : n * (k + 1), :] = part[...]


def odd_band(place):
    return (lax.shift_right_logical(place[0, 4], 4) & 1) == 1


def pair_body(place, first, second, order, out):
    odd = odd_band(place)

    @pl.when(odd)
    def _():
        out[0] = first[...]
        out[1] = second[...]

    @pl.when(jnp.logical_not(odd))
    def _():
        out[0] = second[...]
        out[1] = first[...]


def partner_body(own, partner, low, both, order, out, onward):
    n = COARSE_DEV
    onward[...] = partner[...]
    for k, part in enumerate((own[...], partner[0:n, :], low[...], both[...])):
        out[n * k : n * (k + 1), :] = part


def bands_body(place, own, partner, below, above, a, b, c, d, order, out, triple):
    join_body((a, b, c, d), out)
    triple[1] = own[...]
    odd = place[0, 2] >= 2

    @pl.when(odd)
    def _():
        triple[0] = partner[...]
        triple[2] = above[...]

    @pl.when(jnp.logical_not(odd))
    def _():
        triple[0] = below[...]
        triple[2] = partner[...]


def node_rows(v, hidden_total, first_node, folded, second):
    u = silu(mm(v, first_node) + mm(hidden_total.astype(BF), folded)).astype(BF)
    return (v.astype(F32) + mm(u, second)).astype(BF)


def node_body(
    own, from_left, from_right, up, down, state, folded, first_node, second, w_send, w_recv, order,
    mesh_one, send, recv, coarse,
):
    total = own[...] + from_left[...].astype(F32) + from_right[...].astype(F32)
    total = total + up[...].astype(F32) + down[...].astype(F32)
    one = node_rows(state[...], total, first_node[...], folded[...], second[...])
    mesh_one[...] = one
    sent = mm(one, w_send[...]).astype(BF)
    send[...] = sent
    coarse[...] = sent[0:COARSE_DEV, :]
    recv[...] = mm(one, w_recv[...]).astype(BF)


def fine_body(edges, left, own, right, recv, w_geom, order, order_too, out, rows):
    parts = (left[1], own[1], right[1], own[0], own[2], left[0], left[2], right[0], right[2])
    for k, part in enumerate(parts):
        rows[MESH_NODES * k : MESH_NODES * (k + 1), :] = part
    q = recv[...].astype(F32)
    total = jnp.zeros((MESH_NODES, WIDTH), F32)
    for t in range(MESH_DEGREE):
        d = edges[t]
        spread = one_hot(d[:, 0:1].astype(I32), 9 * MESH_NODES)
        pre = q + mm(spread, rows[...]) + mm(d.astype(BF), w_geom[...])
        total += silu(pre)
    out[...] = total


def coarse_prep_body(place, own, following, far, out, count, row):
    z, y, x, core, tile = (place[0, k] for k in range(5))
    n = COARSE_EDGES
    lists = (own[...], following[...], far[...])
    for k, edges in enumerate(lists):
        owner = edges.astype(F32)[2:3, :].astype(I32)
        row[k : k + 1, :] = jnp.where(owner == tile, 1.0, 0.0)
    row[3:8, :] = jnp.zeros((5, n), F32)
    mask = row[...]
    before = lax.broadcasted_iota(I32, (n, n), 0) < lax.broadcasted_iota(I32, (n, n), 1)
    inside = mm(mask.astype(BF), jnp.where(before, 1.0, 0.0).astype(BF))
    earlier = lax.broadcasted_iota(I32, (8, 8), 1) < lax.broadcasted_iota(I32, (8, 8), 0)
    carried = mm(jnp.where(earlier, 1.0, 0.0).astype(BF), mask.astype(BF)).sum(axis=1, keepdims=True)
    rank = jnp.where(mask > 0.5, inside + carried, -1.0).astype(I32)
    slot = lax.broadcasted_iota(I32, (3 * n, n), 0)
    d = jnp.zeros((3 * n, 16), F32)
    for k, edges in enumerate(lists):
        d += mm_nt(jnp.where(slot == rank[k : k + 1, :], 1.0, 0.0).astype(BF), edges)
    s = (d[:, 0:1] * 256.0 + d[:, 1:2]).astype(I32)
    t = lax.shift_right_logical(s, 4)
    lat = lax.shift_right_logical(t, 4)
    lon = t & 15
    gz = (z - lax.shift_right_logical(lat, 1)) & 3
    gy = (y - lax.shift_right_logical(lon, 2)) & 3
    g_high = (lax.shift_right_logical(x, 1) + lat) & 1
    g_low = (x + lax.shift_right_logical(lon, 1)) & 1
    gc = (core + lon) & 1
    spot = ((((gc * 4 + gz) * 4 + gy) * 2 + g_low) * 2 + g_high) * 16 + (s & 15)
    total = jnp.sum(mask).astype(I32)
    used = lax.broadcasted_iota(I32, (3 * n, 1), 0) < total
    r = jnp.where(used, d[:, 3:4], -1.0)
    lane = lax.broadcasted_iota(I32, (3 * n, 16), 1)
    out[...] = jnp.where(lane == 0, spot.astype(F32), jnp.where(lane == 1, r, d))
    count[0, 0] = total


def mesh_body(
    count, fine, edges, a0, a1, a2, a3, b0, b1, b2, b3, recv, mesh_one, w_geom, folded, first_node, second, w_send,
    send, rows, total,
):
    parts = (a0, a1, a2, a3, b0, b1, b2, b3)
    n = a0.shape[0]
    for k, part in enumerate(parts):
        rows[n * k : n * (k + 1), :] = part[...]
    q = recv[0:COARSE_DEV, :]

    def hidden_sum(d):
        pick = one_hot(d[:, 1:2].astype(I32), MESH_NODES)
        pre = mm(one_hot(d[:, 0:1].astype(I32), len(parts) * n), rows[...])
        pre += mm(pick[:, 0:COARSE_DEV], q) + mm(d.astype(BF), w_geom[...])
        return mm_t(pick, silu(pre).astype(BF))

    total[...] = fine[...] + hidden_sum(edges[0:COARSE_SLOTS, :])

    @pl.loop(COARSE_SLOTS // 64, lax.shift_right_logical(count[0, 0] + 63, 6))
    def _(k):
        total[...] += hidden_sum(edges[pl.ds(pl.multiple_of(64 * k, 64), 64), :])

    two = node_rows(mesh_one[...], total[...], first_node[...], folded[...], second[...])
    send[...] = mm(two, w_send[...]).astype(BF)


def decode_early_body(edges, left, own, right, pair, recv, w_geom, out, rows):
    for k, part in enumerate((left, own, right, pair.at[0], pair.at[1])):
        rows[MESH_NODES * k : MESH_NODES * (k + 1), :] = part[...]
    n = 5 * MESH_NODES

    @pl.loop(0, 4)
    def _(b):
        span = pl.ds(pl.multiple_of(256 * b, 256), 256)
        q = recv[span, :].astype(F32)
        for t in range(GRID_DEGREE):
            d = edges[t, span, :]
            spread = one_hot(d[:, 0:1].astype(I32), n)
            out[t, span, :] = q + mm(spread, rows[0:n, :]) + mm(d.astype(BF), w_geom[...])


def decode_body(edges, early, left_pair, right_pair, base, folded, head, out, rows, totals):
    for k, part in enumerate((left_pair.at[0], left_pair.at[1], right_pair.at[0], right_pair.at[1])):
        rows[MESH_NODES * k : MESH_NODES * (k + 1), :] = part[...]
    @pl.loop(0, 4)
    def _(b):
        span = pl.ds(pl.multiple_of(256 * b, 256), 256)
        total = jnp.zeros((256, WIDTH), F32)
        for t in range(GRID_DEGREE):
            spot = edges[t, span, :][:, 0:1].astype(I32) - 5 * MESH_NODES
            total += silu(early[t, span, :] + mm(one_hot(spot, 4 * MESH_NODES), rows[...]))
        totals[span, :] = total.astype(BF)

    @pl.loop(0, 2)
    def _(b):
        span = pl.ds(pl.multiple_of(512 * b, 512), 512)
        hidden = silu(base[span, :] + mm(totals[span, :], folded[...])).astype(BF)
        out[:, span] = mm_nt(head[...], hidden).astype(BF)


def shift(value, axis, step, periodic):
    n = lax.axis_size(axis)
    pairs = [(i, (i + step) % n) for i in range(n) if periodic or 0 <= i + step < n]
    return lax.ppermute(value, axis, pairs)


def swap_bands(first, second, wrap=False):
    later = [(i, (i + 1) % 8) for i in (1, 3, 5, 7) if wrap or i < 7]
    later += [(target, source) for source, target in later]
    second = lax.ppermute(second, "lat", later)
    return lax.ppermute(first, "lat", [(i, i ^ 1) for i in range(8)]), second


def first_stage(value, wrap=False):
    first, second = swap_bands(value, value, wrap)
    return first, second, shift(value, "lon", 1, True), shift(value, "lon", -1, True)


def second_stage(pair):
    return shift(pair, "lon", 1, True), shift(pair, "lon", -1, True)


def along_z(s):
    return [(i, ((i // 2 + s) % 4) * 2 + i % 2) for i in range(8)]


def along_y(s):
    return [(i, ((i // 4 + s) % 4) * 4 + i % 4) for i in range(16)]


def per_device(
    grid_inputs,
    mesh_state,
    embed_in,
    embed_out,
    edge_square,
    edge_geom_weight,
    node_first,
    node_second,
    head,
    g2m_senders,
    g2m_receivers,
    g2m_counts,
    g2m_geom,
    mesh_senders,
    mesh_geom,
    coarse_senders,
    coarse_receivers,
    coarse_geom,
    m2g_senders,
    m2g_geom,
):
    mesh_rows = (MESH_NODES, WIDTH)
    grid_rows = (GRID_NODES, WIDTH)
    pair_rows = (2,) + mesh_rows
    grid_flops = 2 * GRID_NODES * WIDTH * WIDTH
    mesh_flops = grid_flops // 8
    both = ("lat", "lon")
    tiles = lax.axis_size(both)
    lat, lon = lax.axis_index("lat"), lax.axis_index("lon")
    place = jnp.stack([lat // 2, lon // 4, (lat % 2) * 2 + (lon // 2) % 2, lon % 2, lat * LON + lon])[None]
    place = place.astype(I32)

    pack_args = (
        g2m_senders, g2m_receivers, g2m_geom, mesh_state, coarse_senders, coarse_receivers, coarse_geom
    )

    def part_of(array):
        n = array.ndim - 2
        return Load((0,) if n == 1 else (0, 0), array.shape[1:] if n == 1 else array.shape[2:])

    payload, own_list, coarse_list, geom = kernel_call(
        pack_body,
        (
            shaped((PAYLOAD, WIDTH), BF), shaped((16 * CHUNKS, WIDTH), BF), shaped((16, COARSE_EDGES), BF),
            shaped((4, 16, WIDTH), BF),
        ),
        [SMEM] + [part_of(a) for a in pack_args] + [Load((), edge_geom_weight.shape)],
        (g2m_counts,) + pack_args + (edge_geom_weight,),
        [pltpu.VMEM((16, CHUNK), F32), pltpu.VMEM((8 * CHUNKS, CHUNK), F32)],
        name="pack",
    )
    first, second, near_left, near_right = first_stage(payload, True)
    turned_inputs = jnp.swapaxes(grid_inputs, 2, 3)
    latent, w_send = kernel_call(
        embed_body,
        (shaped(grid_rows, BF), shaped((WIDTH, WIDTH), BF)),
        [part_of(turned_inputs), Load((), embed_in.shape), Load((), embed_out.shape), HBM],
        (turned_inputs, embed_in, embed_out, edge_square),
        [pltpu.SemaphoreType.DMA((1,))],
        flops=2 * grid_flops,
        moved=4 << 20,
        name="embed",
    )
    grid_send = kernel_call(
        send_body,
        shaped(grid_rows, BF),
        [V, V, ANY, ANY],
        (latent, w_send, near_left, near_right),
        flops=grid_flops,
        moved=3 << 20,
        name="send",
    )

    def geom_of(k):
        return View(k)

    own_specs = [part_of(mesh_state), V, V, square(0, 1), geom_of(0)]
    own_args = (mesh_state, own_list, grid_send, edge_square, geom)

    def paired(first, second, order):
        shape = (2,) + first.shape
        return kernel_call(
            pair_body, shaped(shape, BF), [SMEM, V, V, ANY], (place, first, second, order), name="pair"
        )

    own_first, list_rest = kernel_call(
        functools.partial(self_body, (0, 1)),
        (shaped(mesh_rows, F32), shaped((32, WIDTH), BF)),
        own_specs,
        own_args,
        flops=2 * grid_flops,
        moved=3 << 20,
        name="own_first",
    )
    near_middle = paired(first, second, own_first)
    near_left_pair, near_right_pair = second_stage(near_middle)
    own_sum = kernel_call(
        functools.partial(self_body, (0, 1)),
        shaped(mesh_rows, F32),
        own_specs + [V],
        (mesh_state, list_rest, grid_send, edge_square, geom, own_first),
        flops=2 * grid_flops,
        moved=3 << 20,
        name="own_last",
    )
    near_scratch = [
        pltpu.VMEM((4 * CHUNKS, CHUNK), F32),
        pltpu.VMEM((4 * CHUNKS, CHUNK), I32),
        pltpu.VMEM((9 * MESH_NODES, WIDTH), BF),
        pltpu.VMEM((4 * NEAR_SLOTS, 8), F32),
        pltpu.VMEM((9 * MESH_NODES, WIDTH), F32),
    ]
    near_weights = [V, square(0, 1), geom_of(3)]
    to_left, to_right, to_above, to_below, right_list = kernel_call(
        functools.partial(near_body, (5, 3, 7, 1)),
        (shaped(mesh_rows, BF),) * 4 + (shaped((16, COARSE_EDGES), BF),),
        [SMEM, V, V, View(0), View(1)] + near_weights,
        (place, near_left, near_right, near_middle, near_middle, grid_send, edge_square, geom),
        near_scratch,
        flops=2 * grid_flops,
        moved=5 << 20,
        name="beside",
    )
    *to_corners, coarse_next = kernel_call(
        functools.partial(near_body, (8, 2, 6, 0)),
        (shaped(mesh_rows, BF),) * 4 + (shaped((16, COARSE_EDGES), BF),),
        [SMEM, View(0), View(1), View(0), View(1), V, ANY, ANY] + near_weights,
        (
            place, near_left_pair, near_left_pair, near_right_pair, near_right_pair, right_list, own_sum, to_left,
            grid_send, edge_square, geom,
        ),
        near_scratch,
        flops=2 * grid_flops,
        moved=5 << 20,
        name="corners",
    )
    to_left_pair, to_right_pair = kernel_call(
        corner_body, (shaped(pair_rows, BF),) * 2, [V] * 4, tuple(to_corners), name="corner_pairs"
    )
    pair_left = shift(to_right_pair, "lon", 1, True)
    pair_right = shift(to_left_pair, "lon", -1, True)
    prep_args = (mesh_senders, mesh_geom, m2g_senders, m2g_geom)
    stored = {"square": edge_square, "first": node_first, "second": node_second}
    m_edges, d_edges, to_left, to_right, *kept = kernel_call(
        prep_body,
        (
            shaped((MESH_DEGREE, MESH_NODES, 16), F32),
            shaped((GRID_DEGREE, GRID_NODES, 16), F32),
            shaped(mesh_rows, BF),
            shaped(mesh_rows, BF),
        ) + (shaped((WIDTH, WIDTH), BF),) * len(KEPT),
        [part_of(a) for a in prep_args] + [V, V, ANY] + [HBM] * len(KEPT),
        prep_args + (to_left, to_right, to_left_pair) + tuple(stored[name] for name, _ in KEPT),
        [pltpu.VMEM((16, 3072), F32), pltpu.VMEM((3072, 16), F32), pltpu.SemaphoreType.DMA((len(KEPT),))],
        flops=grid_flops,
        name="prep",
    )
    to_first, to_second = kernel_call(
        side_sum_body,
        (shaped(mesh_rows, BF),) * 2,
        [SMEM, V, V, V, V, ANY],
        (place, to_above, to_below, pair_left, pair_right, m_edges),
        name="sides",
    )
    up, down = swap_bands(to_first, to_second)
    folded = kernel_call(
        fold_body,
        (shaped((WIDTH, WIDTH), BF),) * 3,
        [part for k in range(3) for part in (square(k, 2), first_half(k, 1))] + [ANY],
        (edge_square, node_first) * 3 + (to_first,),
        flops=3 * grid_flops // 2,
        moved=4 << 20,
        name="fold",
    )
    from_left = shift(to_right, "lon", 1, True)
    from_right = shift(to_left, "lon", -1, True)
    far_list = lax.ppermute(coarse_list, both, [(t, (t + tiles // 2) % tiles) for t in range(tiles)])
    mesh_one, proc_send, proc_recv, coarse_own = kernel_call(
        node_body,
        (shaped(mesh_rows, BF),) * 3 + (shaped((COARSE_DEV, WIDTH), BF),),
        [V] * 5 + [part_of(mesh_state)] + [V] * 5 + [ANY],
        (own_sum, from_left, from_right, up, down, mesh_state, folded[0], *kept[0:4], far_list),
        flops=7 * mesh_flops,
        moved=4 << 20,
        name="node",
    )
    grid_recv, grid_base = kernel_call(
        grid_body,
        (shaped(grid_rows, BF), shaped(grid_rows, F32)),
        [V, square(2, 1), first_half(2, 0), ANY],
        (latent, edge_square, node_first, proc_send),
        flops=2 * grid_flops,
        moved=5 << 20,
        name="grid",
    )
    def half(t):
        return (t // LON ^ 1) * LON + (t % LON)

    partner = lax.ppermute(proc_send, "lat", [(i, i ^ 1) for i in range(8)])
    low = lax.ppermute(coarse_own, "lon", [(i, i ^ 2) for i in range(LON)])
    cross = lax.ppermute(coarse_own, both, [(t, half(t) ^ 2) for t in range(tiles)])
    beside, onward = kernel_call(
        partner_body,
        (shaped((4 * COARSE_DEV, WIDTH), BF), shaped(mesh_rows, BF)),
        [V, V, V, V, ANY],
        (coarse_own, partner, low, cross, grid_recv),
        name="partner",
    )
    edge_total = 3 * COARSE_EDGES
    c_edges, c_count = kernel_call(
        coarse_prep_body,
        (shaped((edge_total, 16), F32), shaped((1, 1), I32)),
        [SMEM, V, V, V],
        (place, coarse_list, coarse_next, far_list),
        [pltpu.VMEM((8, COARSE_EDGES), F32)],
        flops=mesh_flops,
        name="coarse_edges",
        out_specs=(V, SMEM),
    )
    quarter = [beside] + [lax.ppermute(beside, "lon", along_y(s)) for s in (1, 2, 3)]
    below = lax.ppermute(onward, "lat", along_z(1))
    above = lax.ppermute(onward, "lat", along_z(3))
    rows, triple = kernel_call(
        bands_body,
        (shaped((16 * COARSE_DEV, WIDTH), BF), shaped((3,) + mesh_rows, BF)),
        [SMEM] + [V] * 8 + [ANY],
        (place, proc_send, onward, below, above, *quarter, c_edges),
        name="bands",
    )
    left, right = second_stage(triple)
    quarter = [rows] + [lax.ppermute(rows, "lat", along_z(s)) for s in (1, 2, 3)]
    swapped = [lax.ppermute(part, "lon", [(i, i ^ 1) for i in range(LON)]) for part in quarter]
    fine = kernel_call(
        fine_body,
        shaped(mesh_rows, F32),
        [V] * 5 + [geom_of(1), ANY, ANY],
        (m_edges, left, triple, right, proc_recv, geom, quarter[1], c_edges),
        [pltpu.VMEM((9 * MESH_NODES, WIDTH), BF)],
        flops=2 * grid_flops,
        moved=3 << 20,
        name="fine",
    )
    dec_send = kernel_call(
        mesh_body,
        shaped(mesh_rows, BF),
        [SMEM] + [V] * 12 + [geom_of(1)] + [V] * 4,
        (c_count, fine, c_edges, *quarter, *swapped, proc_recv, mesh_one, geom, folded[1], *kept[4:7]),
        [pltpu.VMEM((128 * COARSE_DEV, WIDTH), BF), pltpu.VMEM(mesh_rows, F32)],
        flops=4 * grid_flops,
        moved=6 << 20,
        name="mesh",
    )
    first, second, left, right = first_stage(dec_send)
    pair = paired(first, second, dec_send)
    left_pair, right_pair = second_stage(pair)
    early = kernel_call(
        decode_early_body,
        shaped((GRID_DEGREE,) + grid_rows, F32),
        [V, V, V, V, V, V, geom_of(2)],
        (d_edges, left, dec_send, right, pair, grid_recv, geom),
        [pltpu.VMEM((5 * MESH_NODES, WIDTH), BF)],
        flops=4 * grid_flops,
        moved=8 << 20,
        name="early",
    )
    outputs = kernel_call(
        decode_body,
        shaped((head.shape[1], GRID_NODES), BF),
        [V] * 7,
        (d_edges, early, left_pair, right_pair, grid_base, folded[2], head.T),
        [pltpu.VMEM((4 * MESH_NODES, WIDTH), BF), pltpu.VMEM(grid_rows, BF)],
        flops=5 * grid_flops,
        moved=8 << 20,
        name="decode",
    )
    return outputs.T[None, None]


def solution(mesh):
    return jax.shard_map(
        per_device,
        mesh=mesh,
        in_specs=(
            P("lat", "lon", None, None),
            P("lat", "lon", None, None),
            P(),
            P(),
            P(),
            P(),
            P(),
            P(),
            P(),
            P("lat", "lon", None),
            P("lat", "lon", None),
            P("lat", "lon"),
            P("lat", "lon", None, None),
            P("lat", "lon", None),
            P("lat", "lon", None, None),
            P("lat", "lon", None),
            P("lat", "lon", None),
            P("lat", "lon", None, None),
            P("lat", "lon", None),
            P("lat", "lon", None, None),
        ),
        out_specs=P("lat", "lon", None, None),
        check_vma=False,
    )
```

```python
import functools

import jax
import jax.numpy as jnp
from jax import lax
from jax.experimental import pallas as pl
from jax.experimental.pallas import tpu as pltpu
from jax.sharding import PartitionSpec as P

BF = jnp.bfloat16
F32 = jnp.float32
I32 = jnp.int32
WIDTH = 512
GRID_NODES = 1024
MESH_NODES = 128
MESH_DEGREE = 6
GRID_DEGREE = 3
COARSE_DEV = 16
SLOTS = 2048
CHUNK = 512
CHUNKS = SLOTS // CHUNK
LISTED = MESH_NODES + 8 * CHUNKS
PAYLOAD = LISTED + 16
COARSE_EDGES = 256
LON = 16
NEAR_SLOTS = 160
COARSE_SLOTS = 320
GROUPS = (5, 3, 7, 0, 1, 2, 6, 4, 8)
VMEM_BYTES = 14 * 1024 * 1024


def mm(left, right):
    return jnp.dot(left, right, preferred_element_type=F32)


def mm_t(left, right):
    return lax.dot_general(left, right, (((0,), (0,)), ((), ())), preferred_element_type=F32)


def mm_nt(left, right):
    return lax.dot_general(left, right, (((1,), (1,)), ((), ())), preferred_element_type=F32)


def silu(v):
    half = 0.5 * v
    return half + half * jnp.tanh(half)


def one_hot(column, width):
    spots = lax.broadcasted_iota(I32, (column.shape[0], width), 1)
    return jnp.where(spots == column, 1.0, 0.0).astype(BF)


class Load:
    def __init__(self, index, shape):
        self.index, self.shape = index, shape


class View:
    def __init__(self, index):
        self.index = index


class Arriving:
    def __init__(self, copy, ref):
        self.copy, self.ref = copy, ref
        self.shape = ref.shape

    def ready(self):
        if self.copy is not None:
            self.copy.wait()
            self.copy = None
        return self.ref

    def __getitem__(self, index):
        return self.ready()[index]


V = pl.BlockSpec(memory_space=pltpu.VMEM)
SMEM = pl.BlockSpec(memory_space=pltpu.SMEM)
ANY = pl.BlockSpec(memory_space=pl.ANY)
HBM = pl.BlockSpec(memory_space=pltpu.HBM)


def square(block, kind):
    return Load((block, kind), (WIDTH, WIDTH))


def first_half(block, half):
    return Load((block, slice(WIDTH * half, WIDTH * (half + 1))), (WIDTH, WIDTH))


def second_of(block):
    return Load((block,), (WIDTH, WIDTH))


KEPT = (
    ("first", first_half(0, 0)), ("second", second_of(0)), ("square", square(1, 0)), ("square", square(1, 1)),
    ("first", first_half(1, 0)), ("second", second_of(1)), ("square", square(2, 0)),
)
ENCODER = (square(0, 0),)


def kernel_call(body, outs, specs, args, scratch=(), flops=0, moved=0, name=None, out_specs=None):
    loads = [(k, spec, args[k].dtype) for k, spec in enumerate(specs) if isinstance(spec, Load)]
    n_in, n_loads = len(specs), len(loads)

    def run(*refs):
        given, rest = list(refs[:n_in]), list(refs[n_in:])
        if n_loads:
            sems = rest[-1]
            buffers = rest[-1 - n_loads : -1]
            rest = rest[: -1 - n_loads]
            for at, ((k, spec, _), buffer) in enumerate(zip(loads, buffers)):
                source = given[k].at[spec.index] if spec.index else given[k]
                copy = pltpu.make_async_copy(source, buffer, sems.at[at])
                copy.start()
                given[k] = Arriving(copy, buffer)
        for k, spec in enumerate(specs):
            if isinstance(spec, View):
                given[k] = given[k].at[spec.index]
        body(*given, *rest)
        for part in given:
            if isinstance(part, Arriving):
                part.ready()

    extra = [pltpu.VMEM(spec.shape, dtype) for _, spec, dtype in loads]
    if loads:
        extra.append(pltpu.SemaphoreType.DMA((n_loads,)))
    many = isinstance(outs, tuple)
    args = [
        pltpu.with_memory_space_constraint(arg, pltpu.HBM) if spec is HBM or isinstance(spec, Load) else arg
        for spec, arg in zip(specs, args)
    ]
    return pl.pallas_call(
        run,
        out_shape=outs,
        in_specs=[HBM if isinstance(q, Load) else V if isinstance(q, View) else q for q in specs],
        out_specs=out_specs if out_specs is not None else (V,) * len(outs) if many else V,
        scratch_shapes=list(scratch) + extra,
        compiler_params=pltpu.CompilerParams(vmem_limit_bytes=VMEM_BYTES),
        cost_estimate=pl.CostEstimate(flops=flops, bytes_accessed=moved, transcendentals=0),
        name=name,
    )(*args)


def shaped(shape, dtype):
    return jax.ShapeDtypeStruct(shape, dtype)


def fill_list(scr, width, indices, geometry):
    for row, value in enumerate(indices):
        scr[row : row + 1, 0:width] = value.astype(F32)
    high = geometry.astype(BF).astype(F32)
    scr[4:8, 0:width] = high
    scr[8:12, 0:width] = geometry - high
    scr[12:16, 0:width] = high


def pack_body(
    count, senders, receivers, geometry, state, c_senders, c_receivers, c_geometry, weight,
    out, own, coarse, w_out, scr, short,
):
    for c in range(CHUNKS):
        cols = slice(c * CHUNK, (c + 1) * CHUNK)
        s = senders[:, cols]
        edge = lax.broadcasted_iota(I32, (1, CHUNK), 1) + c * CHUNK
        code = jnp.where(edge < count[0, 0], lax.shift_right_logical(s, 10) + 1, 0)
        local = s & (GRID_NODES - 1)
        fill_list(
            scr, CHUNK, (code, lax.shift_right_logical(local, 8), local & 255, receivers[:, cols]), geometry[:, cols]
        )
        own[16 * c : 16 * (c + 1), :] = scr[...].astype(BF)
        short[8 * c : 8 * (c + 1), :] = scr[0:8, :]
    out[MESH_NODES:LISTED, :] = short[...].astype(BF)
    s = c_senders[...]
    r = c_receivers[...]
    n = s.shape[1]
    fill_list(
        scr, n, (lax.shift_right_logical(s, 8), s & 255, lax.shift_right_logical(r, 4), r & 15), c_geometry[...]
    )
    out[LISTED:PAYLOAD, :] = scr[...].astype(BF)
    coarse[...] = scr[:, 0:n].astype(BF)
    zero = jnp.zeros((4, WIDTH), F32)
    for k in range(3):
        w = weight[k]
        high = w.astype(BF).astype(F32)
        scr[0:4, :] = zero
        scr[4:8, :] = high
        scr[8:12, :] = high
        scr[12:16, :] = w - high
        w_out[k] = scr[...].astype(BF)
        if k == 0:
            scr[8:12, :] = zero
            w_out[3] = scr[...].astype(BF)
    out[0:MESH_NODES, :] = state[...]


def prep_body(m_senders, m_geometry, d_senders, d_geometry, left, right, order, *refs):
    n = len(KEPT)
    sources, (m_out, d_out, o_left, o_right) = refs[:n], refs[n : n + 4]
    kept, (scr, turned, sems) = refs[n + 4 : -3], refs[-3:]
    o_left[...] = left[...]
    o_right[...] = right[...]
    copies = bring(sources, [load for _, load in KEPT], kept, sems)
    for senders, geometry, degree, out in (
        (m_senders, m_geometry, MESH_DEGREE, m_out),
        (d_senders, d_geometry, GRID_DEGREE, d_out),
    ):
        n = senders.shape[1]
        s = senders[...]
        near = lax.shift_right_logical(s, 7)
        spot = jnp.zeros_like(near)
        for place, group in enumerate(GROUPS):
            spot = jnp.where(near == place, group, spot)
        spot = spot * MESH_NODES + (s & (MESH_NODES - 1))
        zero = jnp.zeros((1, n), F32)
        fill_list(scr, n, (spot, zero, zero, zero), geometry[...])
        turned[0:n, :] = scr[:, 0:n].T
        for t in range(degree):
            out[t] = turned[pl.ds(t, n // degree, stride=degree), :]
    for copy in copies:
        copy.wait()


def embed_body(x, w_in, w_out, source, latent, w_send, sems):
    copies = bring((source,), ENCODER, (w_send,), sems)
    x, w_in, w_out = x.ready(), w_in.ready(), w_out.ready()

    @pl.loop(0, 4)
    def _(b):
        rows = pl.ds(pl.multiple_of(256 * b, 256), 256)
        hidden = silu(mm_t(x[:, rows], w_in[...])).astype(BF)
        latent[rows, :] = mm(hidden, w_out[...]).astype(BF)

    for copy in copies:
        copy.wait()


def send_body(latent, w_send, order, order_too, send):
    @pl.loop(0, 2)
    def _(b):
        rows = pl.ds(pl.multiple_of(512 * b, 512), 512)
        send[rows, :] = mm(latent[rows, :], w_send[...]).astype(BF)


def grid_body(latent, w_recv, w_first, order, recv, base):
    w_recv, w_first = w_recv.ready(), w_first.ready()

    @pl.loop(0, 4)
    def _(b):
        rows = pl.ds(pl.multiple_of(256 * b, 256), 256)
        recv[rows, :] = mm(latent[rows, :], w_recv[...]).astype(BF)
        base[rows, :] = mm(latent[rows, :], w_first[...])


def bring(sources, loads, outs, sems):
    copies = []
    for k, load in enumerate(loads):
        copies.append(pltpu.make_async_copy(sources[k].at[load.index], outs[k], sems.at[k]))
        copies[-1].start()
    return copies


def fold_body(*refs):
    for k in range(3):
        refs[7 + k][...] = mm(refs[2 * k][...], refs[2 * k + 1][...]).astype(BF)


def self_body(chunks, state, listed, send, w_recv, w_geom, *refs):
    total = jnp.zeros((MESH_NODES, WIDTH), F32) if len(refs) == 1 else refs[0][...]
    if len(refs) == 2 and refs[1].shape == (32, WIDTH):
        refs[1][...] = listed[32:64, :]
        out = refs[0]
        total = jnp.zeros((MESH_NODES, WIDTH), F32)
    else:
        out = refs[-1]
    q = None
    for c in chunks:
        d = listed[16 * c : 16 * (c + 1), :].astype(F32).T
        s = (d[:, 1:2] * 256.0 + d[:, 2:3]).astype(I32)
        r = jnp.where(d[:, 0:1] == 5.0, d[:, 3:4], -1.0).astype(I32)
        pick = one_hot(r, MESH_NODES)
        pre = mm(one_hot(s, GRID_NODES), send[...]) + mm(d.astype(BF), w_geom[...])
        if q is None:
            q = mm(state[...], w_recv[...]).astype(BF)
        total += mm_t(pick, silu(pre + mm(pick, q)).astype(BF))
    out[...] = total


def near_body(buckets, place, *refs):
    sources, refs = refs[: len(buckets)], refs[len(buckets) :]
    if len(refs) == 16:
        beside, order_first, order_last, *refs = refs
    send, w_recv, w_geom, *refs = refs
    outs, refs = refs[: len(buckets)], refs[len(buckets) :]
    if len(refs) == 6 and buckets[0] != 5:
        following, *refs = refs
        n = COARSE_EDGES
        last = (place[0, 4] & (LON - 1)) == LON - 1
        following[...] = jnp.where(
            last, sources[-1][LISTED:PAYLOAD, 0:n].astype(F32), beside[...].astype(F32)
        ).astype(BF)
    if len(buckets) == 4 and buckets[0] == 5:
        following, *refs = refs
        following[...] = sources[1][LISTED:PAYLOAD, 0:COARSE_EDGES]
    masks, ranks, q, edges, sums = refs
    band = lax.shift_right_logical(place[0, 4], 4)
    lists = tuple(zip(sources, buckets, outs))
    q[...] = jnp.zeros_like(q)

    def listed(src, c):
        return src[MESH_NODES:LISTED, :].astype(F32)[8 * c : 8 * (c + 1), :]

    def geometry_part(d):
        return mm(jnp.concatenate([d, d], axis=1).astype(BF), w_geom[...])

    for i, (src, bucket, _) in enumerate(lists):
        for c in range(CHUNKS):
            row = i * CHUNKS + c
            code = listed(src, c)[0:1, :]
            wanted = float(bucket + 1)
            if bucket < 3 or bucket > 5:
                wanted = jnp.where(band == (7 if bucket < 3 else 0), -1.0, wanted)
            masks[row : row + 1, :] = jnp.where(code == wanted, 1.0, 0.0)
    n = masks.shape[0]
    mask = masks[...]
    before = lax.broadcasted_iota(I32, (CHUNK, CHUNK), 0) < lax.broadcasted_iota(I32, (CHUNK, CHUNK), 1)
    inside = mm(mask.astype(BF), jnp.where(before, 1.0, 0.0).astype(BF))
    mine = lax.broadcasted_iota(I32, (n, n), 0)
    other = lax.broadcasted_iota(I32, (n, n), 1)
    same = mine // CHUNKS == other // CHUNKS
    earlier = jnp.where((other < mine) & same, 1.0, 0.0).astype(BF)
    carried = mm(earlier, mask.astype(BF)).sum(axis=1, keepdims=True)
    ranks[...] = jnp.where(mask > 0.5, inside + carried, -1.0).astype(I32)

    slot = lax.broadcasted_iota(I32, (NEAR_SLOTS, CHUNK), 0)
    for i, (src, _, _) in enumerate(lists):
        d = jnp.zeros((NEAR_SLOTS, 8), F32)
        for c in range(CHUNKS):
            row = i * CHUNKS + c
            d += mm_nt(jnp.where(slot == ranks[row : row + 1, :], 1.0, 0.0).astype(BF), listed(src, c).astype(BF))
        edges[NEAR_SLOTS * i : NEAR_SLOTS * (i + 1), :] = d
    received = mm(jnp.concatenate([src[0:MESH_NODES, :] for src in sources], axis=0), w_recv[...]).astype(BF)
    d = edges[...]
    s = (d[:, 1:2] * 256.0 + d[:, 2:3]).astype(I32)
    pre = mm(one_hot(s, GRID_NODES), send[...]) + geometry_part(d)
    r = jnp.where(d[:, 0:1] > 0.5, d[:, 3:4], -1.0).astype(I32)
    for i, bucket in enumerate(buckets):
        part = slice(NEAR_SLOTS * i, NEAR_SLOTS * (i + 1))
        rows = slice(MESH_NODES * bucket, MESH_NODES * (bucket + 1))
        mine = received[MESH_NODES * i : MESH_NODES * (i + 1), :]
        q[rows, :] = mine
        pick = one_hot(r[part, :], MESH_NODES)
        sums[rows, :] = mm_t(pick, silu(pre[part, :] + mm(pick, mine)).astype(BF))

    count = mm(jnp.where(same, 1.0, 0.0).astype(BF), mask.astype(BF)).sum(axis=1, keepdims=True)
    over = jnp.maximum(count - NEAR_SLOTS, 0.0)
    total = lax.shift_right_logical(jnp.sum(over).astype(I32), 2)

    @pl.when(total > 0)
    def _():
        across = lax.broadcasted_iota(I32, (n, 1), 0) // CHUNKS
        base = jnp.zeros((n, 1), F32)
        for i in range(len(lists) - 1):
            base += jnp.where(across > i, over[i * CHUNKS : i * CHUNKS + 1, :], 0.0)
        rank = ranks[...]
        ranks[...] = jnp.where(rank >= NEAR_SLOTS, rank - NEAR_SLOTS + base.astype(I32), -1)

        @pl.loop(0, lax.shift_right_logical(total + 127, 7))
        def _(k):
            late = lax.broadcasted_iota(I32, (128, CHUNK), 0) + k * 128
            d = jnp.zeros((128, 8), F32)
            for i, (src, _, _) in enumerate(lists):
                for c in range(CHUNKS):
                    row = i * CHUNKS + c
                    d += mm_nt(jnp.where(late == ranks[row : row + 1, :], 1.0, 0.0).astype(BF), listed(src, c).astype(BF))
            s = (d[:, 1:2] * 256.0 + d[:, 2:3]).astype(I32)
            code = d[:, 0:1]
            r = jnp.where(code > 0.5, (code - 1.0) * float(MESH_NODES) + d[:, 3:4], -1.0).astype(I32)
            pick = one_hot(r, 9 * MESH_NODES)
            pre = mm(one_hot(s, GRID_NODES), send[...]) + mm(pick, q[...]) + geometry_part(d)
            sums[...] += mm_t(pick, silu(pre).astype(BF))

    for _, bucket, dst in lists:
        dst[...] = sums[MESH_NODES * bucket : MESH_NODES * (bucket + 1), :].astype(BF)


def corner_body(a, b, c, d, left, right):
    left[0] = a[...]
    left[1] = b[...]
    right[0] = c[...]
    right[1] = d[...]


def side_sum_body(place, above, below, from_left, from_right, order, first, second):
    odd = odd_band(place)
    for k, middle, when_odd, when_even in ((0, above, first, second), (1, below, second, first)):
        total = (middle[...].astype(F32) + from_left[k].astype(F32) + from_right[k].astype(F32)).astype(BF)

        @pl.when(odd)
        def _(total=total, out=when_odd):
            out[...] = total

        @pl.when(jnp.logical_not(odd))
        def _(total=total, out=when_even):
            out[...] = total


def join_body(parts, out):
    n = parts[0].shape[0]
    for k, part in enumerate(parts):
        out[n * k : n * (k + 1), :] = part[...]


def odd_band(place):
    return (lax.shift_right_logical(place[0, 4], 4) & 1) == 1


def pair_body(place, first, second, order, out):
    odd = odd_band(place)

    @pl.when(odd)
    def _():
        out[0] = first[...]
        out[1] = second[...]

    @pl.when(jnp.logical_not(odd))
    def _():
        out[0] = second[...]
        out[1] = first[...]


def partner_body(own, partner, low, both, order, out, onward):
    n = COARSE_DEV
    onward[...] = partner[...]
    for k, part in enumerate((own[...], partner[0:n, :], low[...], both[...])):
        out[n * k : n * (k + 1), :] = part


def bands_body(place, own, partner, below, above, a, b, c, d, order, out, triple):
    join_body((a, b, c, d), out)
    triple[1] = own[...]
    odd = place[0, 2] >= 2

    @pl.when(odd)
    def _():
        triple[0] = partner[...]
        triple[2] = above[...]

    @pl.when(jnp.logical_not(odd))
    def _():
        triple[0] = below[...]
        triple[2] = partner[...]


def node_rows(v, hidden_total, first_node, folded, second):
    u = silu(mm(v, first_node) + mm(hidden_total.astype(BF), folded)).astype(BF)
    return (v.astype(F32) + mm(u, second)).astype(BF)


def node_body(
    own, from_left, from_right, up, down, state, folded, first_node, second, w_send, w_recv, order,
    mesh_one, send, recv, coarse,
):
    total = own[...] + from_left[...].astype(F32) + from_right[...].astype(F32)
    total = total + up[...].astype(F32) + down[...].astype(F32)
    one = node_rows(state[...], total, first_node[...], folded[...], second[...])
    mesh_one[...] = one
    sent = mm(one, w_send[...]).astype(BF)
    send[...] = sent
    coarse[...] = sent[0:COARSE_DEV, :]
    recv[...] = mm(one, w_recv[...]).astype(BF)


def fine_body(edges, left, own, right, recv, w_geom, order, order_too, out, rows):
    parts = (left[1], own[1], right[1], own[0], own[2], left[0], left[2], right[0], right[2])
    for k, part in enumerate(parts):
        rows[MESH_NODES * k : MESH_NODES * (k + 1), :] = part
    q = recv[...].astype(F32)
    total = jnp.zeros((MESH_NODES, WIDTH), F32)
    for t in range(MESH_DEGREE):
        d = edges[t]
        spread = one_hot(d[:, 0:1].astype(I32), 9 * MESH_NODES)
        pre = q + mm(spread, rows[...]) + mm(d.astype(BF), w_geom[...])
        total += silu(pre)
    out[...] = total


def coarse_prep_body(place, own, following, far, out, count, row):
    z, y, x, core, tile = (place[0, k] for k in range(5))
    n = COARSE_EDGES
    lists = (own[...], following[...], far[...])
    for k, edges in enumerate(lists):
        owner = edges.astype(F32)[2:3, :].astype(I32)
        row[k : k + 1, :] = jnp.where(owner == tile, 1.0, 0.0)
    row[3:8, :] = jnp.zeros((5, n), F32)
    mask = row[...]
    before = lax.broadcasted_iota(I32, (n, n), 0) < lax.broadcasted_iota(I32, (n, n), 1)
    inside = mm(mask.astype(BF), jnp.where(before, 1.0, 0.0).astype(BF))
    earlier = lax.broadcasted_iota(I32, (8, 8), 1) < lax.broadcasted_iota(I32, (8, 8), 0)
    carried = mm(jnp.where(earlier, 1.0, 0.0).astype(BF), mask.astype(BF)).sum(axis=1, keepdims=True)
    rank = jnp.where(mask > 0.5, inside + carried, -1.0).astype(I32)
    slot = lax.broadcasted_iota(I32, (3 * n, n), 0)
    d = jnp.zeros((3 * n, 16), F32)
    for k, edges in enumerate(lists):
        d += mm_nt(jnp.where(slot == rank[k : k + 1, :], 1.0, 0.0).astype(BF), edges)
    s = (d[:, 0:1] * 256.0 + d[:, 1:2]).astype(I32)
    t = lax.shift_right_logical(s, 4)
    lat = lax.shift_right_logical(t, 4)
    lon = t & 15
    gz = (z - lax.shift_right_logical(lat, 1)) & 3
    gy = (y - lax.shift_right_logical(lon, 2)) & 3
    g_high = (lax.shift_right_logical(x, 1) + lat) & 1
    g_low = (x + lax.shift_right_logical(lon, 1)) & 1
    gc = (core + lon) & 1
    spot = ((((gc * 4 + gz) * 4 + gy) * 2 + g_low) * 2 + g_high) * 16 + (s & 15)
    total = jnp.sum(mask).astype(I32)
    used = lax.broadcasted_iota(I32, (3 * n, 1), 0) < total
    r = jnp.where(used, d[:, 3:4], -1.0)
    lane = lax.broadcasted_iota(I32, (3 * n, 16), 1)
    out[...] = jnp.where(lane == 0, spot.astype(F32), jnp.where(lane == 1, r, d))
    count[0, 0] = total


def mesh_body(
    count, fine, edges, a0, a1, a2, a3, b0, b1, b2, b3, recv, mesh_one, w_geom, folded, first_node, second, w_send,
    send, rows, total,
):
    parts = (a0, a1, a2, a3, b0, b1, b2, b3)
    n = a0.shape[0]
    for k, part in enumerate(parts):
        rows[n * k : n * (k + 1), :] = part[...]
    q = recv[0:COARSE_DEV, :]

    def hidden_sum(d):
        pick = one_hot(d[:, 1:2].astype(I32), MESH_NODES)
        pre = mm(one_hot(d[:, 0:1].astype(I32), len(parts) * n), rows[...])
        pre += mm(pick[:, 0:COARSE_DEV], q) + mm(d.astype(BF), w_geom[...])
        return mm_t(pick, silu(pre).astype(BF))

    total[...] = fine[...] + hidden_sum(edges[0:COARSE_SLOTS, :])

    @pl.loop(COARSE_SLOTS // 64, lax.shift_right_logical(count[0, 0] + 63, 6))
    def _(k):
        total[...] += hidden_sum(edges[pl.ds(pl.multiple_of(64 * k, 64), 64), :])

    two = node_rows(mesh_one[...], total[...], first_node[...], folded[...], second[...])
    send[...] = mm(two, w_send[...]).astype(BF)


def decode_early_body(edges, left, own, right, pair, recv, w_geom, out, rows):
    for k, part in enumerate((left, own, right, pair.at[0], pair.at[1])):
        rows[MESH_NODES * k : MESH_NODES * (k + 1), :] = part[...]
    n = 5 * MESH_NODES

    @pl.loop(0, 4)
    def _(b):
        span = pl.ds(pl.multiple_of(256 * b, 256), 256)
        q = recv[span, :].astype(F32)
        for t in range(GRID_DEGREE):
            d = edges[t, span, :]
            spread = one_hot(d[:, 0:1].astype(I32), n)
            out[t, span, :] = q + mm(spread, rows[0:n, :]) + mm(d.astype(BF), w_geom[...])


def decode_body(edges, early, left_pair, right_pair, base, folded, head, out, rows, totals):
    for k, part in enumerate((left_pair.at[0], left_pair.at[1], right_pair.at[0], right_pair.at[1])):
        rows[MESH_NODES * k : MESH_NODES * (k + 1), :] = part[...]
    for b in range(4):
        span = slice(256 * b, 256 * (b + 1))
        total = jnp.zeros((256, WIDTH), F32)
        for t in range(GRID_DEGREE):
            spot = edges[t, span, :][:, 0:1].astype(I32) - 5 * MESH_NODES
            total += silu(early[t, span, :] + mm(one_hot(spot, 4 * MESH_NODES), rows[...]))
        totals[span, :] = total.astype(BF)

    for b in range(2):
        span = slice(512 * b, 512 * (b + 1))
        hidden = silu(base[span, :] + mm(totals[span, :], folded[...])).astype(BF)
        out[:, span] = mm_nt(head[...], hidden).astype(BF)


def shift(value, axis, step, periodic):
    n = lax.axis_size(axis)
    pairs = [(i, (i + step) % n) for i in range(n) if periodic or 0 <= i + step < n]
    return lax.ppermute(value, axis, pairs)


def swap_bands(first, second, wrap=False):
    later = [(i, (i + 1) % 8) for i in (1, 3, 5, 7) if wrap or i < 7]
    later += [(target, source) for source, target in later]
    second = lax.ppermute(second, "lat", later)
    return lax.ppermute(first, "lat", [(i, i ^ 1) for i in range(8)]), second


def first_stage(value, wrap=False):
    first, second = swap_bands(value, value, wrap)
    return first, second, shift(value, "lon", 1, True), shift(value, "lon", -1, True)


def second_stage(pair):
    return shift(pair, "lon", 1, True), shift(pair, "lon", -1, True)


def along_z(s):
    return [(i, ((i // 2 + s) % 4) * 2 + i % 2) for i in range(8)]


def along_y(s):
    return [(i, ((i // 4 + s) % 4) * 4 + i % 4) for i in range(16)]


def per_device(
    grid_inputs,
    mesh_state,
    embed_in,
    embed_out,
    edge_square,
    edge_geom_weight,
    node_first,
    node_second,
    head,
    g2m_senders,
    g2m_receivers,
    g2m_counts,
    g2m_geom,
    mesh_senders,
    mesh_geom,
    coarse_senders,
    coarse_receivers,
    coarse_geom,
    m2g_senders,
    m2g_geom,
):
    mesh_rows = (MESH_NODES, WIDTH)
    grid_rows = (GRID_NODES, WIDTH)
    pair_rows = (2,) + mesh_rows
    grid_flops = 2 * GRID_NODES * WIDTH * WIDTH
    mesh_flops = grid_flops // 8
    both = ("lat", "lon")
    tiles = lax.axis_size(both)
    lat, lon = lax.axis_index("lat"), lax.axis_index("lon")
    place = jnp.stack([lat // 2, lon // 4, (lat % 2) * 2 + (lon // 2) % 2, lon % 2, lat * LON + lon])[None]
    place = place.astype(I32)

    pack_args = (
        g2m_senders, g2m_receivers, g2m_geom, mesh_state, coarse_senders, coarse_receivers, coarse_geom
    )

    def part_of(array):
        n = array.ndim - 2
        return Load((0,) if n == 1 else (0, 0), array.shape[1:] if n == 1 else array.shape[2:])

    payload, own_list, coarse_list, geom = kernel_call(
        pack_body,
        (
            shaped((PAYLOAD, WIDTH), BF), shaped((16 * CHUNKS, WIDTH), BF), shaped((16, COARSE_EDGES), BF),
            shaped((4, 16, WIDTH), BF),
        ),
        [SMEM] + [part_of(a) for a in pack_args] + [Load((), edge_geom_weight.shape)],
        (g2m_counts,) + pack_args + (edge_geom_weight,),
        [pltpu.VMEM((16, CHUNK), F32), pltpu.VMEM((8 * CHUNKS, CHUNK), F32)],
        name="pack",
    )
    first, second, near_left, near_right = first_stage(payload, True)
    turned_inputs = jnp.swapaxes(grid_inputs, 2, 3)
    latent, w_send = kernel_call(
        embed_body,
        (shaped(grid_rows, BF), shaped((WIDTH, WIDTH), BF)),
        [part_of(turned_inputs), Load((), embed_in.shape), Load((), embed_out.shape), HBM],
        (turned_inputs, embed_in, embed_out, edge_square),
        [pltpu.SemaphoreType.DMA((1,))],
        flops=2 * grid_flops,
        moved=4 << 20,
        name="embed",
    )
    grid_send = kernel_call(
        send_body,
        shaped(grid_rows, BF),
        [V, V, ANY, ANY],
        (latent, w_send, near_left, near_right),
        flops=grid_flops,
        moved=3 << 20,
        name="send",
    )

    def geom_of(k):
        return View(k)

    own_specs = [part_of(mesh_state), V, V, square(0, 1), geom_of(0)]
    own_args = (mesh_state, own_list, grid_send, edge_square, geom)

    def paired(first, second, order):
        shape = (2,) + first.shape
        return kernel_call(
            pair_body, shaped(shape, BF), [SMEM, V, V, ANY], (place, first, second, order), name="pair"
        )

    own_first, list_rest = kernel_call(
        functools.partial(self_body, (0, 1)),
        (shaped(mesh_rows, F32), shaped((32, WIDTH), BF)),
        own_specs,
        own_args,
        flops=2 * grid_flops,
        moved=3 << 20,
        name="own_first",
    )
    near_middle = paired(first, second, own_first)
    near_left_pair, near_right_pair = second_stage(near_middle)
    own_sum = kernel_call(
        functools.partial(self_body, (0, 1)),
        shaped(mesh_rows, F32),
        own_specs + [V],
        (mesh_state, list_rest, grid_send, edge_square, geom, own_first),
        flops=2 * grid_flops,
        moved=3 << 20,
        name="own_last",
    )
    near_scratch = [
        pltpu.VMEM((4 * CHUNKS, CHUNK), F32),
        pltpu.VMEM((4 * CHUNKS, CHUNK), I32),
        pltpu.VMEM((9 * MESH_NODES, WIDTH), BF),
        pltpu.VMEM((4 * NEAR_SLOTS, 8), F32),
        pltpu.VMEM((9 * MESH_NODES, WIDTH), F32),
    ]
    near_weights = [V, square(0, 1), geom_of(3)]
    to_left, to_right, to_above, to_below, right_list = kernel_call(
        functools.partial(near_body, (5, 3, 7, 1)),
        (shaped(mesh_rows, BF),) * 4 + (shaped((16, COARSE_EDGES), BF),),
        [SMEM, V, V, View(0), View(1)] + near_weights,
        (place, near_left, near_right, near_middle, near_middle, grid_send, edge_square, geom),
        near_scratch,
        flops=2 * grid_flops,
        moved=5 << 20,
        name="beside",
    )
    *to_corners, coarse_next = kernel_call(
        functools.partial(near_body, (8, 2, 6, 0)),
        (shaped(mesh_rows, BF),) * 4 + (shaped((16, COARSE_EDGES), BF),),
        [SMEM, View(0), View(1), View(0), View(1), V, ANY, ANY] + near_weights,
        (
            place, near_left_pair, near_left_pair, near_right_pair, near_right_pair, right_list, own_sum, to_left,
            grid_send, edge_square, geom,
        ),
        near_scratch,
        flops=2 * grid_flops,
        moved=5 << 20,
        name="corners",
    )
    to_left_pair, to_right_pair = kernel_call(
        corner_body, (shaped(pair_rows, BF),) * 2, [V] * 4, tuple(to_corners), name="corner_pairs"
    )
    pair_left = shift(to_right_pair, "lon", 1, True)
    pair_right = shift(to_left_pair, "lon", -1, True)
    prep_args = (mesh_senders, mesh_geom, m2g_senders, m2g_geom)
    stored = {"square": edge_square, "first": node_first, "second": node_second}
    m_edges, d_edges, to_left, to_right, *kept = kernel_call(
        prep_body,
        (
            shaped((MESH_DEGREE, MESH_NODES, 16), F32),
            shaped((GRID_DEGREE, GRID_NODES, 16), F32),
            shaped(mesh_rows, BF),
            shaped(mesh_rows, BF),
        ) + (shaped((WIDTH, WIDTH), BF),) * len(KEPT),
        [part_of(a) for a in prep_args] + [V, V, ANY] + [HBM] * len(KEPT),
        prep_args + (to_left, to_right, to_left_pair) + tuple(stored[name] for name, _ in KEPT),
        [pltpu.VMEM((16, 3072), F32), pltpu.VMEM((3072, 16), F32), pltpu.SemaphoreType.DMA((len(KEPT),))],
        flops=grid_flops,
        name="prep",
    )
    to_first, to_second = kernel_call(
        side_sum_body,
        (shaped(mesh_rows, BF),) * 2,
        [SMEM, V, V, V, V, ANY],
        (place, to_above, to_below, pair_left, pair_right, m_edges),
        name="sides",
    )
    up, down = swap_bands(to_first, to_second)
    folded = kernel_call(
        fold_body,
        (shaped((WIDTH, WIDTH), BF),) * 3,
        [part for k in range(3) for part in (square(k, 2), first_half(k, 1))] + [ANY],
        (edge_square, node_first) * 3 + (to_first,),
        flops=3 * grid_flops // 2,
        moved=4 << 20,
        name="fold",
    )
    from_left = shift(to_right, "lon", 1, True)
    from_right = shift(to_left, "lon", -1, True)
    far_list = lax.ppermute(coarse_list, both, [(t, (t + tiles // 2) % tiles) for t in range(tiles)])
    mesh_one, proc_send, proc_recv, coarse_own = kernel_call(
        node_body,
        (shaped(mesh_rows, BF),) * 3 + (shaped((COARSE_DEV, WIDTH), BF),),
        [V] * 5 + [part_of(mesh_state)] + [V] * 5 + [ANY],
        (own_sum, from_left, from_right, up, down, mesh_state, folded[0], *kept[0:4], far_list),
        flops=7 * mesh_flops,
        moved=4 << 20,
        name="node",
    )
    grid_recv, grid_base = kernel_call(
        grid_body,
        (shaped(grid_rows, BF), shaped(grid_rows, F32)),
        [V, square(2, 1), first_half(2, 0), ANY],
        (latent, edge_square, node_first, proc_send),
        flops=2 * grid_flops,
        moved=5 << 20,
        name="grid",
    )
    def half(t):
        return (t // LON ^ 1) * LON + (t % LON)

    partner = lax.ppermute(proc_send, "lat", [(i, i ^ 1) for i in range(8)])
    low = lax.ppermute(coarse_own, "lon", [(i, i ^ 2) for i in range(LON)])
    cross = lax.ppermute(coarse_own, both, [(t, half(t) ^ 2) for t in range(tiles)])
    beside, onward = kernel_call(
        partner_body,
        (shaped((4 * COARSE_DEV, WIDTH), BF), shaped(mesh_rows, BF)),
        [V, V, V, V, ANY],
        (coarse_own, partner, low, cross, grid_recv),
        name="partner",
    )
    edge_total = 3 * COARSE_EDGES
    c_edges, c_count = kernel_call(
        coarse_prep_body,
        (shaped((edge_total, 16), F32), shaped((1, 1), I32)),
        [SMEM, V, V, V],
        (place, coarse_list, coarse_next, far_list),
        [pltpu.VMEM((8, COARSE_EDGES), F32)],
        flops=mesh_flops,
        name="coarse_edges",
        out_specs=(V, SMEM),
    )
    quarter = [beside] + [lax.ppermute(beside, "lon", along_y(s)) for s in (1, 2, 3)]
    below = lax.ppermute(onward, "lat", along_z(1))
    above = lax.ppermute(onward, "lat", along_z(3))
    rows, triple = kernel_call(
        bands_body,
        (shaped((16 * COARSE_DEV, WIDTH), BF), shaped((3,) + mesh_rows, BF)),
        [SMEM] + [V] * 8 + [ANY],
        (place, proc_send, onward, below, above, *quarter, c_edges),
        name="bands",
    )
    left, right = second_stage(triple)
    quarter = [rows] + [lax.ppermute(rows, "lat", along_z(s)) for s in (1, 2, 3)]
    swapped = [lax.ppermute(part, "lon", [(i, i ^ 1) for i in range(LON)]) for part in quarter]
    fine = kernel_call(
        fine_body,
        shaped(mesh_rows, F32),
        [V] * 5 + [geom_of(1), ANY, ANY],
        (m_edges, left, triple, right, proc_recv, geom, quarter[1], c_edges),
        [pltpu.VMEM((9 * MESH_NODES, WIDTH), BF)],
        flops=2 * grid_flops,
        moved=3 << 20,
        name="fine",
    )
    dec_send = kernel_call(
        mesh_body,
        shaped(mesh_rows, BF),
        [SMEM] + [V] * 12 + [geom_of(1)] + [V] * 4,
        (c_count, fine, c_edges, *quarter, *swapped, proc_recv, mesh_one, geom, folded[1], *kept[4:7]),
        [pltpu.VMEM((128 * COARSE_DEV, WIDTH), BF), pltpu.VMEM(mesh_rows, F32)],
        flops=4 * grid_flops,
        moved=6 << 20,
        name="mesh",
    )
    first, second, left, right = first_stage(dec_send)
    pair = paired(first, second, dec_send)
    left_pair, right_pair = second_stage(pair)
    early = kernel_call(
        decode_early_body,
        shaped((GRID_DEGREE,) + grid_rows, F32),
        [V, V, V, V, V, V, geom_of(2)],
        (d_edges, left, dec_send, right, pair, grid_recv, geom),
        [pltpu.VMEM((5 * MESH_NODES, WIDTH), BF)],
        flops=4 * grid_flops,
        moved=8 << 20,
        name="early",
    )
    outputs = kernel_call(
        decode_body,
        shaped((head.shape[1], GRID_NODES), BF),
        [V] * 7,
        (d_edges, early, left_pair, right_pair, grid_base, folded[2], head.T),
        [pltpu.VMEM((4 * MESH_NODES, WIDTH), BF), pltpu.VMEM(grid_rows, BF)],
        flops=5 * grid_flops,
        moved=8 << 20,
        name="decode",
    )
    return outputs.T[None, None]


def solution(mesh):
    return jax.shard_map(
        per_device,
        mesh=mesh,
        in_specs=(
            P("lat", "lon", None, None),
            P("lat", "lon", None, None),
            P(),
            P(),
            P(),
            P(),
            P(),
            P(),
            P(),
            P("lat", "lon", None),
            P("lat", "lon", None),
            P("lat", "lon"),
            P("lat", "lon", None, None),
            P("lat", "lon", None),
            P("lat", "lon", None, None),
            P("lat", "lon", None),
            P("lat", "lon", None),
            P("lat", "lon", None, None),
            P("lat", "lon", None),
            P("lat", "lon", None, None),
        ),
        out_specs=P("lat", "lon", None, None),
        check_vma=False,
    )
```

```python
import functools

import jax
import jax.numpy as jnp
from jax import lax
from jax.experimental import pallas as pl
from jax.experimental.pallas import tpu as pltpu
from jax.sharding import PartitionSpec as P

BF = jnp.bfloat16
F32 = jnp.float32
I32 = jnp.int32
WIDTH = 512
GRID_NODES = 1024
MESH_NODES = 128
MESH_DEGREE = 6
GRID_DEGREE = 3
COARSE_DEV = 16
SLOTS = 2048
CHUNK = 512
CHUNKS = SLOTS // CHUNK
LISTED = MESH_NODES + 8 * CHUNKS
PAYLOAD = LISTED + 16
COARSE_EDGES = 256
LON = 16
NEAR_SLOTS = 160
COARSE_SLOTS = 320
GROUPS = (5, 3, 7, 0, 1, 2, 6, 4, 8)
VMEM_BYTES = 14 * 1024 * 1024


def mm(left, right):
    return jnp.dot(left, right, preferred_element_type=F32)


def mm_t(left, right):
    return lax.dot_general(left, right, (((0,), (0,)), ((), ())), preferred_element_type=F32)


def mm_nt(left, right):
    return lax.dot_general(left, right, (((1,), (1,)), ((), ())), preferred_element_type=F32)


def silu(v):
    half = 0.5 * v
    return half + half * jnp.tanh(half)


def one_hot(column, width):
    spots = lax.broadcasted_iota(I32, (column.shape[0], width), 1)
    return jnp.where(spots == column, 1.0, 0.0).astype(BF)


class Load:
    def __init__(self, index, shape):
        self.index, self.shape = index, shape


class View:
    def __init__(self, index):
        self.index = index


class Arriving:
    def __init__(self, copy, ref):
        self.copy, self.ref = copy, ref
        self.shape = ref.shape

    def ready(self):
        if self.copy is not None:
            self.copy.wait()
            self.copy = None
        return self.ref

    def __getitem__(self, index):
        return self.ready()[index]


V = pl.BlockSpec(memory_space=pltpu.VMEM)
SMEM = pl.BlockSpec(memory_space=pltpu.SMEM)
ANY = pl.BlockSpec(memory_space=pl.ANY)
HBM = pl.BlockSpec(memory_space=pltpu.HBM)


def square(block, kind):
    return Load((block, kind), (WIDTH, WIDTH))


def first_half(block, half):
    return Load((block, slice(WIDTH * half, WIDTH * (half + 1))), (WIDTH, WIDTH))


def second_of(block):
    return Load((block,), (WIDTH, WIDTH))


KEPT = (
    ("first", first_half(0, 0)), ("second", second_of(0)), ("square", square(1, 0)), ("square", square(1, 1)),
    ("first", first_half(1, 0)), ("second", second_of(1)), ("square", square(2, 0)),
)
ENCODER = (square(0, 0),)


def kernel_call(body, outs, specs, args, scratch=(), flops=0, moved=0, name=None, out_specs=None):
    loads = [(k, spec, args[k].dtype) for k, spec in enumerate(specs) if isinstance(spec, Load)]
    n_in, n_loads = len(specs), len(loads)

    def run(*refs):
        given, rest = list(refs[:n_in]), list(refs[n_in:])
        if n_loads:
            sems = rest[-1]
            buffers = rest[-1 - n_loads : -1]
            rest = rest[: -1 - n_loads]
            for at, ((k, spec, _), buffer) in enumerate(zip(loads, buffers)):
                source = given[k].at[spec.index] if spec.index else given[k]
                copy = pltpu.make_async_copy(source, buffer, sems.at[at])
                copy.start()
                given[k] = Arriving(copy, buffer)
        for k, spec in enumerate(specs):
            if isinstance(spec, View):
                given[k] = given[k].at[spec.index]
        body(*given, *rest)
        for part in given:
            if isinstance(part, Arriving):
                part.ready()

    extra = [pltpu.VMEM(spec.shape, dtype) for _, spec, dtype in loads]
    if loads:
        extra.append(pltpu.SemaphoreType.DMA((n_loads,)))
    many = isinstance(outs, tuple)
    args = [
        pltpu.with_memory_space_constraint(arg, pltpu.HBM) if spec is HBM or isinstance(spec, Load) else arg
        for spec, arg in zip(specs, args)
    ]
    return pl.pallas_call(
        run,
        out_shape=outs,
        in_specs=[HBM if isinstance(q, Load) else V if isinstance(q, View) else q for q in specs],
        out_specs=out_specs if out_specs is not None else (V,) * len(outs) if many else V,
        scratch_shapes=list(scratch) + extra,
        compiler_params=pltpu.CompilerParams(vmem_limit_bytes=VMEM_BYTES),
        cost_estimate=pl.CostEstimate(flops=flops, bytes_accessed=moved, transcendentals=0),
        name=name,
    )(*args)


def shaped(shape, dtype):
    return jax.ShapeDtypeStruct(shape, dtype)


def fill_list(scr, width, indices, geometry):
    for row, value in enumerate(indices):
        scr[row : row + 1, 0:width] = value.astype(F32)
    high = geometry.astype(BF).astype(F32)
    scr[4:8, 0:width] = high
    scr[8:12, 0:width] = geometry - high
    scr[12:16, 0:width] = high


def pack_body(
    count, senders, receivers, geometry, state, c_senders, c_receivers, c_geometry, weight,
    out, own, coarse, w_out, scr, short,
):
    for c in range(CHUNKS):
        cols = slice(c * CHUNK, (c + 1) * CHUNK)
        s = senders[:, cols]
        edge = lax.broadcasted_iota(I32, (1, CHUNK), 1) + c * CHUNK
        code = jnp.where(edge < count[0, 0], lax.shift_right_logical(s, 10) + 1, 0)
        local = s & (GRID_NODES - 1)
        fill_list(
            scr, CHUNK, (code, lax.shift_right_logical(local, 8), local & 255, receivers[:, cols]), geometry[:, cols]
        )
        own[16 * c : 16 * (c + 1), :] = scr[...].astype(BF)
        short[8 * c : 8 * (c + 1), :] = scr[0:8, :]
    out[MESH_NODES:LISTED, :] = short[...].astype(BF)
    s = c_senders[...]
    r = c_receivers[...]
    n = s.shape[1]
    fill_list(
        scr, n, (lax.shift_right_logical(s, 8), s & 255, lax.shift_right_logical(r, 4), r & 15), c_geometry[...]
    )
    out[LISTED:PAYLOAD, :] = scr[...].astype(BF)
    coarse[...] = scr[:, 0:n].astype(BF)
    zero = jnp.zeros((4, WIDTH), F32)
    for k in range(3):
        w = weight[k]
        high = w.astype(BF).astype(F32)
        scr[0:4, :] = zero
        scr[4:8, :] = high
        scr[8:12, :] = high
        scr[12:16, :] = w - high
        w_out[k] = scr[...].astype(BF)
        if k == 0:
            scr[8:12, :] = zero
            w_out[3] = scr[...].astype(BF)
    out[0:MESH_NODES, :] = state[...]


def prep_body(m_senders, m_geometry, d_senders, d_geometry, left, right, order, *refs):
    n = len(KEPT)
    sources, (m_out, d_out, o_left, o_right) = refs[:n], refs[n : n + 4]
    kept, (scr, turned, sems) = refs[n + 4 : -3], refs[-3:]
    o_left[...] = left[...]
    o_right[...] = right[...]
    copies = bring(sources, [load for _, load in KEPT], kept, sems)
    for senders, geometry, degree, out in (
        (m_senders, m_geometry, MESH_DEGREE, m_out),
        (d_senders, d_geometry, GRID_DEGREE, d_out),
    ):
        n = senders.shape[1]
        s = senders[...]
        near = lax.shift_right_logical(s, 7)
        spot = jnp.zeros_like(near)
        for place, group in enumerate(GROUPS):
            spot = jnp.where(near == place, group, spot)
        spot = spot * MESH_NODES + (s & (MESH_NODES - 1))
        zero = jnp.zeros((1, n), F32)
        fill_list(scr, n, (spot, zero, zero, zero), geometry[...])
        turned[0:n, :] = scr[:, 0:n].T
        for t in range(degree):
            out[t] = turned[pl.ds(t, n // degree, stride=degree), :]
    for copy in copies:
        copy.wait()


def embed_body(x, w_in, w_out, source, latent, w_send, sems):
    copies = bring((source,), ENCODER, (w_send,), sems)
    x, w_in, w_out = x.ready(), w_in.ready(), w_out.ready()

    @pl.loop(0, 4)
    def _(b):
        rows = pl.ds(pl.multiple_of(256 * b, 256), 256)
        hidden = silu(mm_t(x[:, rows], w_in[...])).astype(BF)
        latent[rows, :] = mm(hidden, w_out[...]).astype(BF)

    for copy in copies:
        copy.wait()


def send_body(latent, w_send, order, order_too, send):
    @pl.loop(0, 2)
    def _(b):
        rows = pl.ds(pl.multiple_of(512 * b, 512), 512)
        send[rows, :] = mm(latent[rows, :], w_send[...]).astype(BF)


def grid_body(latent, w_recv, w_first, order, recv, base):
    w_recv, w_first = w_recv.ready(), w_first.ready()

    @pl.loop(0, 4)
    def _(b):
        rows = pl.ds(pl.multiple_of(256 * b, 256), 256)
        recv[rows, :] = mm(latent[rows, :], w_recv[...]).astype(BF)
        base[rows, :] = mm(latent[rows, :], w_first[...])


def bring(sources, loads, outs, sems):
    copies = []
    for k, load in enumerate(loads):
        copies.append(pltpu.make_async_copy(sources[k].at[load.index], outs[k], sems.at[k]))
        copies[-1].start()
    return copies


def fold_body(*refs):
    for k in range(3):
        refs[7 + k][...] = mm(refs[2 * k][...], refs[2 * k + 1][...]).astype(BF)


def self_body(chunks, state, listed, send, w_recv, w_geom, *refs):
    total = jnp.zeros((MESH_NODES, WIDTH), F32) if len(refs) == 1 else refs[0][...]
    if len(refs) == 2 and refs[1].shape == (32, WIDTH):
        refs[1][...] = listed[32:64, :]
        out = refs[0]
        total = jnp.zeros((MESH_NODES, WIDTH), F32)
    else:
        out = refs[-1]
    q = None
    for c in chunks:
        d = listed[16 * c : 16 * (c + 1), :].astype(F32).T
        s = (d[:, 1:2] * 256.0 + d[:, 2:3]).astype(I32)
        r = jnp.where(d[:, 0:1] == 5.0, d[:, 3:4], -1.0).astype(I32)
        pick = one_hot(r, MESH_NODES)
        pre = mm(one_hot(s, GRID_NODES), send[...]) + mm(d.astype(BF), w_geom[...])
        if q is None:
            q = mm(state[...], w_recv[...]).astype(BF)
        total += mm_t(pick, silu(pre + mm(pick, q)).astype(BF))
    out[...] = total


def near_body(buckets, place, *refs):
    sources, refs = refs[: len(buckets)], refs[len(buckets) :]
    if len(refs) == 16:
        beside, order_first, order_last, *refs = refs
    send, w_recv, w_geom, *refs = refs
    outs, refs = refs[: len(buckets)], refs[len(buckets) :]
    if len(refs) == 6 and buckets[0] != 5:
        following, *refs = refs
        n = COARSE_EDGES
        last = (place[0, 4] & (LON - 1)) == LON - 1
        following[...] = jnp.where(
            last, sources[-1][LISTED:PAYLOAD, 0:n].astype(F32), beside[...].astype(F32)
        ).astype(BF)
    if len(buckets) == 4 and buckets[0] == 5:
        following, *refs = refs
        following[...] = sources[1][LISTED:PAYLOAD, 0:COARSE_EDGES]
    masks, ranks, q, edges, sums = refs
    band = lax.shift_right_logical(place[0, 4], 4)
    lists = tuple(zip(sources, buckets, outs))

    def listed(src, c):
        return src[MESH_NODES:LISTED, :].astype(F32)[8 * c : 8 * (c + 1), :]

    def geometry_part(d):
        return mm(jnp.concatenate([d, d], axis=1).astype(BF), w_geom[...])

    for i, (src, bucket, _) in enumerate(lists):
        for c in range(CHUNKS):
            row = i * CHUNKS + c
            code = listed(src, c)[0:1, :]
            wanted = float(bucket + 1)
            if bucket < 3 or bucket > 5:
                wanted = jnp.where(band == (7 if bucket < 3 else 0), -1.0, wanted)
            masks[row : row + 1, :] = jnp.where(code == wanted, 1.0, 0.0)
    n = masks.shape[0]
    mask = masks[...]
    before = lax.broadcasted_iota(I32, (CHUNK, CHUNK), 0) < lax.broadcasted_iota(I32, (CHUNK, CHUNK), 1)
    inside = mm(mask.astype(BF), jnp.where(before, 1.0, 0.0).astype(BF))
    mine = lax.broadcasted_iota(I32, (n, n), 0)
    other = lax.broadcasted_iota(I32, (n, n), 1)
    same = mine // CHUNKS == other // CHUNKS
    earlier = jnp.where((other < mine) & same, 1.0, 0.0).astype(BF)
    carried = mm(earlier, mask.astype(BF)).sum(axis=1, keepdims=True)
    ranks[...] = jnp.where(mask > 0.5, inside + carried, -1.0).astype(I32)

    slot = lax.broadcasted_iota(I32, (NEAR_SLOTS, CHUNK), 0)
    for i, (src, _, _) in enumerate(lists):
        d = jnp.zeros((NEAR_SLOTS, 8), F32)
        for c in range(CHUNKS):
            row = i * CHUNKS + c
            d += mm_nt(jnp.where(slot == ranks[row : row + 1, :], 1.0, 0.0).astype(BF), listed(src, c).astype(BF))
        edges[NEAR_SLOTS * i : NEAR_SLOTS * (i + 1), :] = d
    received = mm(jnp.concatenate([src[0:MESH_NODES, :] for src in sources], axis=0), w_recv[...]).astype(BF)
    d = edges[...]
    s = (d[:, 1:2] * 256.0 + d[:, 2:3]).astype(I32)
    pre = mm(one_hot(s, GRID_NODES), send[...]) + geometry_part(d)
    r = jnp.where(d[:, 0:1] > 0.5, d[:, 3:4], -1.0).astype(I32)
    for i, bucket in enumerate(buckets):
        part = slice(NEAR_SLOTS * i, NEAR_SLOTS * (i + 1))
        rows = slice(MESH_NODES * bucket, MESH_NODES * (bucket + 1))
        mine = received[MESH_NODES * i : MESH_NODES * (i + 1), :]
        q[rows, :] = mine
        pick = one_hot(r[part, :], MESH_NODES)
        sums[rows, :] = mm_t(pick, silu(pre[part, :] + mm(pick, mine)).astype(BF))

    count = mm(jnp.where(same, 1.0, 0.0).astype(BF), mask.astype(BF)).sum(axis=1, keepdims=True)
    over = jnp.maximum(count - NEAR_SLOTS, 0.0)
    total = lax.shift_right_logical(jnp.sum(over).astype(I32), 2)

    @pl.when(total > 0)
    def _():
        for bucket in sorted(set(range(9)) - set(buckets)):
            q[MESH_NODES * bucket : MESH_NODES * (bucket + 1), :] = jnp.zeros((MESH_NODES, WIDTH), BF)
            sums[MESH_NODES * bucket : MESH_NODES * (bucket + 1), :] = jnp.zeros((MESH_NODES, WIDTH), F32)
        across = lax.broadcasted_iota(I32, (n, 1), 0) // CHUNKS
        base = jnp.zeros((n, 1), F32)
        for i in range(len(lists) - 1):
            base += jnp.where(across > i, over[i * CHUNKS : i * CHUNKS + 1, :], 0.0)
        rank = ranks[...]
        ranks[...] = jnp.where(rank >= NEAR_SLOTS, rank - NEAR_SLOTS + base.astype(I32), -1)

        @pl.loop(0, lax.shift_right_logical(total + 127, 7))
        def _(k):
            late = lax.broadcasted_iota(I32, (128, CHUNK), 0) + k * 128
            d = jnp.zeros((128, 8), F32)
            for i, (src, _, _) in enumerate(lists):
                for c in range(CHUNKS):
                    row = i * CHUNKS + c
                    d += mm_nt(jnp.where(late == ranks[row : row + 1, :], 1.0, 0.0).astype(BF), listed(src, c).astype(BF))
            s = (d[:, 1:2] * 256.0 + d[:, 2:3]).astype(I32)
            code = d[:, 0:1]
            r = jnp.where(code > 0.5, (code - 1.0) * float(MESH_NODES) + d[:, 3:4], -1.0).astype(I32)
            pick = one_hot(r, 9 * MESH_NODES)
            pre = mm(one_hot(s, GRID_NODES), send[...]) + mm(pick, q[...]) + geometry_part(d)
            sums[...] += mm_t(pick, silu(pre).astype(BF))

    for _, bucket, dst in lists:
        dst[...] = sums[MESH_NODES * bucket : MESH_NODES * (bucket + 1), :].astype(BF)


def corner_body(a, b, c, d, left, right):
    left[0] = a[...]
    left[1] = b[...]
    right[0] = c[...]
    right[1] = d[...]


def side_sum_body(place, above, below, from_left, from_right, order, first, second):
    odd = odd_band(place)
    for k, middle, when_odd, when_even in ((0, above, first, second), (1, below, second, first)):
        total = (middle[...].astype(F32) + from_left[k].astype(F32) + from_right[k].astype(F32)).astype(BF)

        @pl.when(odd)
        def _(total=total, out=when_odd):
            out[...] = total

        @pl.when(jnp.logical_not(odd))
        def _(total=total, out=when_even):
            out[...] = total


def join_body(parts, out):
    n = parts[0].shape[0]
    for k, part in enumerate(parts):
        out[n * k : n * (k + 1), :] = part[...]


def odd_band(place):
    return (lax.shift_right_logical(place[0, 4], 4) & 1) == 1


def pair_body(place, first, second, order, out):
    odd = odd_band(place)

    @pl.when(odd)
    def _():
        out[0] = first[...]
        out[1] = second[...]

    @pl.when(jnp.logical_not(odd))
    def _():
        out[0] = second[...]
        out[1] = first[...]


def partner_body(own, partner, low, both, order, out, onward):
    n = COARSE_DEV
    onward[...] = partner[...]
    for k, part in enumerate((own[...], partner[0:n, :], low[...], both[...])):
        out[n * k : n * (k + 1), :] = part


def bands_body(place, own, partner, below, above, a, b, c, d, order, out, triple):
    join_body((a, b, c, d), out)
    triple[1] = own[...]
    odd = place[0, 2] >= 2

    @pl.when(odd)
    def _():
        triple[0] = partner[...]
        triple[2] = above[...]

    @pl.when(jnp.logical_not(odd))
    def _():
        triple[0] = below[...]
        triple[2] = partner[...]


def node_rows(v, hidden_total, first_node, folded, second):
    u = silu(mm(v, first_node) + mm(hidden_total.astype(BF), folded)).astype(BF)
    return (v.astype(F32) + mm(u, second)).astype(BF)


def node_body(
    own, from_left, from_right, up, down, state, folded, first_node, second, w_send, w_recv, order,
    mesh_one, send, recv, coarse,
):
    total = own[...] + from_left[...].astype(F32) + from_right[...].astype(F32)
    total = total + up[...].astype(F32) + down[...].astype(F32)
    one = node_rows(state[...], total, first_node[...], folded[...], second[...])
    mesh_one[...] = one
    sent = mm(one, w_send[...]).astype(BF)
    send[...] = sent
    coarse[...] = sent[0:COARSE_DEV, :]
    recv[...] = mm(one, w_recv[...]).astype(BF)


def fine_body(edges, left, own, right, recv, w_geom, order, order_too, out, rows):
    parts = (left[1], own[1], right[1], own[0], own[2], left[0], left[2], right[0], right[2])
    for k, part in enumerate(parts):
        rows[MESH_NODES * k : MESH_NODES * (k + 1), :] = part
    q = recv[...].astype(F32)
    total = jnp.zeros((MESH_NODES, WIDTH), F32)
    for t in range(MESH_DEGREE):
        d = edges[t]
        spread = one_hot(d[:, 0:1].astype(I32), 9 * MESH_NODES)
        pre = q + mm(spread, rows[...]) + mm(d.astype(BF), w_geom[...])
        total += silu(pre)
    out[...] = total


def coarse_prep_body(place, own, following, far, out, count, row):
    z, y, x, core, tile = (place[0, k] for k in range(5))
    n = COARSE_EDGES
    lists = (own[...], following[...], far[...])
    for k, edges in enumerate(lists):
        owner = edges.astype(F32)[2:3, :].astype(I32)
        row[k : k + 1, :] = jnp.where(owner == tile, 1.0, 0.0)
    row[3:8, :] = jnp.zeros((5, n), F32)
    mask = row[...]
    before = lax.broadcasted_iota(I32, (n, n), 0) < lax.broadcasted_iota(I32, (n, n), 1)
    inside = mm(mask.astype(BF), jnp.where(before, 1.0, 0.0).astype(BF))
    earlier = lax.broadcasted_iota(I32, (8, 8), 1) < lax.broadcasted_iota(I32, (8, 8), 0)
    carried = mm(jnp.where(earlier, 1.0, 0.0).astype(BF), mask.astype(BF)).sum(axis=1, keepdims=True)
    rank = jnp.where(mask > 0.5, inside + carried, -1.0).astype(I32)
    slot = lax.broadcasted_iota(I32, (3 * n, n), 0)
    d = jnp.zeros((3 * n, 16), F32)
    for k, edges in enumerate(lists):
        d += mm_nt(jnp.where(slot == rank[k : k + 1, :], 1.0, 0.0).astype(BF), edges)
    s = (d[:, 0:1] * 256.0 + d[:, 1:2]).astype(I32)
    t = lax.shift_right_logical(s, 4)
    lat = lax.shift_right_logical(t, 4)
    lon = t & 15
    gz = (z - lax.shift_right_logical(lat, 1)) & 3
    gy = (y - lax.shift_right_logical(lon, 2)) & 3
    g_high = (lax.shift_right_logical(x, 1) + lat) & 1
    g_low = (x + lax.shift_right_logical(lon, 1)) & 1
    gc = (core + lon) & 1
    spot = ((((gc * 4 + gz) * 4 + gy) * 2 + g_low) * 2 + g_high) * 16 + (s & 15)
    total = jnp.sum(mask).astype(I32)
    used = lax.broadcasted_iota(I32, (3 * n, 1), 0) < total
    r = jnp.where(used, d[:, 3:4], -1.0)
    lane = lax.broadcasted_iota(I32, (3 * n, 16), 1)
    out[...] = jnp.where(lane == 0, spot.astype(F32), jnp.where(lane == 1, r, d))
    count[0, 0] = total


def mesh_body(
    count, fine, edges, a0, a1, a2, a3, b0, b1, b2, b3, recv, mesh_one, w_geom, folded, first_node, second, w_send,
    send, total,
):
    parts = (a0, a1, a2, a3, b0, b1, b2, b3)
    n = a0.shape[0]
    q = recv[0:COARSE_DEV, :]

    def hidden_sum(d):
        pick = one_hot(d[:, 1:2].astype(I32), MESH_NODES)
        spread = one_hot(d[:, 0:1].astype(I32), len(parts) * n)
        pre = mm(spread[:, 0:n], parts[0][...])
        for k in range(1, len(parts)):
            pre += mm(spread[:, n * k : n * (k + 1)], parts[k][...])
        pre += mm(pick[:, 0:COARSE_DEV], q) + mm(d.astype(BF), w_geom[...])
        return mm_t(pick, silu(pre).astype(BF))

    total[...] = fine[...] + hidden_sum(edges[0:COARSE_SLOTS, :])

    @pl.loop(COARSE_SLOTS // 64, lax.shift_right_logical(count[0, 0] + 63, 6))
    def _(k):
        total[...] += hidden_sum(edges[pl.ds(pl.multiple_of(64 * k, 64), 64), :])

    two = node_rows(mesh_one[...], total[...], first_node[...], folded[...], second[...])
    send[...] = mm(two, w_send[...]).astype(BF)


def decode_early_body(edges, left, own, right, pair, recv, w_geom, out, rows):
    for k, part in enumerate((left, own, right, pair.at[0], pair.at[1])):
        rows[MESH_NODES * k : MESH_NODES * (k + 1), :] = part[...]
    n = 5 * MESH_NODES

    @pl.loop(0, 4)
    def _(b):
        span = pl.ds(pl.multiple_of(256 * b, 256), 256)
        q = recv[span, :].astype(F32)
        for t in range(GRID_DEGREE):
            d = edges[t, span, :]
            spread = one_hot(d[:, 0:1].astype(I32), n)
            out[t, span, :] = q + mm(spread, rows[0:n, :]) + mm(d.astype(BF), w_geom[...])


def decode_body(edges, early, left_pair, right_pair, base, folded, head, out, rows, totals):
    for k, part in enumerate((left_pair.at[0], left_pair.at[1], right_pair.at[0], right_pair.at[1])):
        rows[MESH_NODES * k : MESH_NODES * (k + 1), :] = part[...]
    for b in range(4):
        span = slice(256 * b, 256 * (b + 1))
        total = jnp.zeros((256, WIDTH), F32)
        for t in range(GRID_DEGREE):
            spot = edges[t, span, :][:, 0:1].astype(I32) - 5 * MESH_NODES
            total += silu(early[t, span, :] + mm(one_hot(spot, 4 * MESH_NODES), rows[...]))
        totals[span, :] = total.astype(BF)

    for b in range(2):
        span = slice(512 * b, 512 * (b + 1))
        hidden = silu(base[span, :] + mm(totals[span, :], folded[...])).astype(BF)
        out[:, span] = mm_nt(head[...], hidden).astype(BF)


def shift(value, axis, step, periodic):
    n = lax.axis_size(axis)
    pairs = [(i, (i + step) % n) for i in range(n) if periodic or 0 <= i + step < n]
    return lax.ppermute(value, axis, pairs)


def swap_bands(first, second, wrap=False):
    later = [(i, (i + 1) % 8) for i in (1, 3, 5, 7) if wrap or i < 7]
    later += [(target, source) for source, target in later]
    second = lax.ppermute(second, "lat", later)
    return lax.ppermute(first, "lat", [(i, i ^ 1) for i in range(8)]), second


def first_stage(value, wrap=False):
    first, second = swap_bands(value, value, wrap)
    return first, second, shift(value, "lon", 1, True), shift(value, "lon", -1, True)


def second_stage(pair):
    return shift(pair, "lon", 1, True), shift(pair, "lon", -1, True)


def along_z(s):
    return [(i, ((i // 2 + s) % 4) * 2 + i % 2) for i in range(8)]


def along_y(s):
    return [(i, ((i // 4 + s) % 4) * 4 + i % 4) for i in range(16)]


def per_device(
    grid_inputs,
    mesh_state,
    embed_in,
    embed_out,
    edge_square,
    edge_geom_weight,
    node_first,
    node_second,
    head,
    g2m_senders,
    g2m_receivers,
    g2m_counts,
    g2m_geom,
    mesh_senders,
    mesh_geom,
    coarse_senders,
    coarse_receivers,
    coarse_geom,
    m2g_senders,
    m2g_geom,
):
    mesh_rows = (MESH_NODES, WIDTH)
    grid_rows = (GRID_NODES, WIDTH)
    pair_rows = (2,) + mesh_rows
    grid_flops = 2 * GRID_NODES * WIDTH * WIDTH
    mesh_flops = grid_flops // 8
    both = ("lat", "lon")
    tiles = lax.axis_size(both)
    lat, lon = lax.axis_index("lat"), lax.axis_index("lon")
    place = jnp.stack([lat // 2, lon // 4, (lat % 2) * 2 + (lon // 2) % 2, lon % 2, lat * LON + lon])[None]
    place = place.astype(I32)

    pack_args = (
        g2m_senders, g2m_receivers, g2m_geom, mesh_state, coarse_senders, coarse_receivers, coarse_geom
    )

    def part_of(array):
        n = array.ndim - 2
        return Load((0,) if n == 1 else (0, 0), array.shape[1:] if n == 1 else array.shape[2:])

    payload, own_list, coarse_list, geom = kernel_call(
        pack_body,
        (
            shaped((PAYLOAD, WIDTH), BF), shaped((16 * CHUNKS, WIDTH), BF), shaped((16, COARSE_EDGES), BF),
            shaped((4, 16, WIDTH), BF),
        ),
        [SMEM] + [part_of(a) for a in pack_args] + [Load((), edge_geom_weight.shape)],
        (g2m_counts,) + pack_args + (edge_geom_weight,),
        [pltpu.VMEM((16, CHUNK), F32), pltpu.VMEM((8 * CHUNKS, CHUNK), F32)],
        name="pack",
    )
    first, second, near_left, near_right = first_stage(payload, True)
    turned_inputs = jnp.swapaxes(grid_inputs, 2, 3)
    latent, w_send = kernel_call(
        embed_body,
        (shaped(grid_rows, BF), shaped((WIDTH, WIDTH), BF)),
        [part_of(turned_inputs), Load((), embed_in.shape), Load((), embed_out.shape), HBM],
        (turned_inputs, embed_in, embed_out, edge_square),
        [pltpu.SemaphoreType.DMA((1,))],
        flops=2 * grid_flops,
        moved=4 << 20,
        name="embed",
    )
    grid_send = kernel_call(
        send_body,
        shaped(grid_rows, BF),
        [V, V, ANY, ANY],
        (latent, w_send, near_left, near_right),
        flops=grid_flops,
        moved=3 << 20,
        name="send",
    )

    def geom_of(k):
        return View(k)

    own_specs = [part_of(mesh_state), V, V, square(0, 1), geom_of(0)]
    own_args = (mesh_state, own_list, grid_send, edge_square, geom)

    def paired(first, second, order):
        shape = (2,) + first.shape
        return kernel_call(
            pair_body, shaped(shape, BF), [SMEM, V, V, ANY], (place, first, second, order), name="pair"
        )

    own_first, list_rest = kernel_call(
        functools.partial(self_body, (0, 1)),
        (shaped(mesh_rows, F32), shaped((32, WIDTH), BF)),
        own_specs,
        own_args,
        flops=2 * grid_flops,
        moved=3 << 20,
        name="own_first",
    )
    near_middle = paired(first, second, own_first)
    near_left_pair, near_right_pair = second_stage(near_middle)
    own_sum = kernel_call(
        functools.partial(self_body, (0, 1)),
        shaped(mesh_rows, F32),
        own_specs + [V],
        (mesh_state, list_rest, grid_send, edge_square, geom, own_first),
        flops=2 * grid_flops,
        moved=3 << 20,
        name="own_last",
    )
    near_scratch = [
        pltpu.VMEM((4 * CHUNKS, CHUNK), F32),
        pltpu.VMEM((4 * CHUNKS, CHUNK), I32),
        pltpu.VMEM((9 * MESH_NODES, WIDTH), BF),
        pltpu.VMEM((4 * NEAR_SLOTS, 8), F32),
        pltpu.VMEM((9 * MESH_NODES, WIDTH), F32),
    ]
    near_weights = [V, square(0, 1), geom_of(3)]
    to_left, to_right, to_above, to_below, right_list = kernel_call(
        functools.partial(near_body, (5, 3, 7, 1)),
        (shaped(mesh_rows, BF),) * 4 + (shaped((16, COARSE_EDGES), BF),),
        [SMEM, V, V, View(0), View(1)] + near_weights,
        (place, near_left, near_right, near_middle, near_middle, grid_send, edge_square, geom),
        near_scratch,
        flops=2 * grid_flops,
        moved=5 << 20,
        name="beside",
    )
    *to_corners, coarse_next = kernel_call(
        functools.partial(near_body, (8, 2, 6, 0)),
        (shaped(mesh_rows, BF),) * 4 + (shaped((16, COARSE_EDGES), BF),),
        [SMEM, View(0), View(1), View(0), View(1), V, ANY, ANY] + near_weights,
        (
            place, near_left_pair, near_left_pair, near_right_pair, near_right_pair, right_list, own_sum, to_left,
            grid_send, edge_square, geom,
        ),
        near_scratch,
        flops=2 * grid_flops,
        moved=5 << 20,
        name="corners",
    )
    to_left_pair, to_right_pair = kernel_call(
        corner_body, (shaped(pair_rows, BF),) * 2, [V] * 4, tuple(to_corners), name="corner_pairs"
    )
    pair_left = shift(to_right_pair, "lon", 1, True)
    pair_right = shift(to_left_pair, "lon", -1, True)
    prep_args = (mesh_senders, mesh_geom, m2g_senders, m2g_geom)
    stored = {"square": edge_square, "first": node_first, "second": node_second}
    m_edges, d_edges, to_left, to_right, *kept = kernel_call(
        prep_body,
        (
            shaped((MESH_DEGREE, MESH_NODES, 16), F32),
            shaped((GRID_DEGREE, GRID_NODES, 16), F32),
            shaped(mesh_rows, BF),
            shaped(mesh_rows, BF),
        ) + (shaped((WIDTH, WIDTH), BF),) * len(KEPT),
        [part_of(a) for a in prep_args] + [V, V, ANY] + [HBM] * len(KEPT),
        prep_args + (to_left, to_right, to_left_pair) + tuple(stored[name] for name, _ in KEPT),
        [pltpu.VMEM((16, 3072), F32), pltpu.VMEM((3072, 16), F32), pltpu.SemaphoreType.DMA((len(KEPT),))],
        flops=grid_flops,
        name="prep",
    )
    to_first, to_second = kernel_call(
        side_sum_body,
        (shaped(mesh_rows, BF),) * 2,
        [SMEM, V, V, V, V, ANY],
        (place, to_above, to_below, pair_left, pair_right, m_edges),
        name="sides",
    )
    up, down = swap_bands(to_first, to_second)
    folded = kernel_call(
        fold_body,
        (shaped((WIDTH, WIDTH), BF),) * 3,
        [part for k in range(3) for part in (square(k, 2), first_half(k, 1))] + [ANY],
        (edge_square, node_first) * 3 + (to_first,),
        flops=3 * grid_flops // 2,
        moved=4 << 20,
        name="fold",
    )
    from_left = shift(to_right, "lon", 1, True)
    from_right = shift(to_left, "lon", -1, True)
    far_list = lax.ppermute(coarse_list, both, [(t, (t + tiles // 2) % tiles) for t in range(tiles)])
    mesh_one, proc_send, proc_recv, coarse_own = kernel_call(
        node_body,
        (shaped(mesh_rows, BF),) * 3 + (shaped((COARSE_DEV, WIDTH), BF),),
        [V] * 5 + [part_of(mesh_state)] + [V] * 5 + [ANY],
        (own_sum, from_left, from_right, up, down, mesh_state, folded[0], *kept[0:4], far_list),
        flops=7 * mesh_flops,
        moved=4 << 20,
        name="node",
    )
    grid_recv, grid_base = kernel_call(
        grid_body,
        (shaped(grid_rows, BF), shaped(grid_rows, F32)),
        [V, square(2, 1), first_half(2, 0), ANY],
        (latent, edge_square, node_first, proc_send),
        flops=2 * grid_flops,
        moved=5 << 20,
        name="grid",
    )
    def half(t):
        return (t // LON ^ 1) * LON + (t % LON)

    partner = lax.ppermute(proc_send, "lat", [(i, i ^ 1) for i in range(8)])
    low = lax.ppermute(coarse_own, "lon", [(i, i ^ 2) for i in range(LON)])
    cross = lax.ppermute(coarse_own, both, [(t, half(t) ^ 2) for t in range(tiles)])
    beside, onward = kernel_call(
        partner_body,
        (shaped((4 * COARSE_DEV, WIDTH), BF), shaped(mesh_rows, BF)),
        [V, V, V, V, ANY],
        (coarse_own, partner, low, cross, grid_recv),
        name="partner",
    )
    edge_total = 3 * COARSE_EDGES
    c_edges, c_count = kernel_call(
        coarse_prep_body,
        (shaped((edge_total, 16), F32), shaped((1, 1), I32)),
        [SMEM, V, V, V],
        (place, coarse_list, coarse_next, far_list),
        [pltpu.VMEM((8, COARSE_EDGES), F32)],
        flops=mesh_flops,
        name="coarse_edges",
        out_specs=(V, SMEM),
    )
    quarter = [beside] + [lax.ppermute(beside, "lon", along_y(s)) for s in (1, 2, 3)]
    below = lax.ppermute(onward, "lat", along_z(1))
    above = lax.ppermute(onward, "lat", along_z(3))
    rows, triple = kernel_call(
        bands_body,
        (shaped((16 * COARSE_DEV, WIDTH), BF), shaped((3,) + mesh_rows, BF)),
        [SMEM] + [V] * 8 + [ANY],
        (place, proc_send, onward, below, above, *quarter, c_edges),
        name="bands",
    )
    left, right = second_stage(triple)
    quarter = [rows] + [lax.ppermute(rows, "lat", along_z(s)) for s in (1, 2, 3)]
    swapped = [lax.ppermute(part, "lon", [(i, i ^ 1) for i in range(LON)]) for part in quarter]
    fine = kernel_call(
        fine_body,
        shaped(mesh_rows, F32),
        [V] * 5 + [geom_of(1), ANY, ANY],
        (m_edges, left, triple, right, proc_recv, geom, quarter[1], c_edges),
        [pltpu.VMEM((9 * MESH_NODES, WIDTH), BF)],
        flops=2 * grid_flops,
        moved=3 << 20,
        name="fine",
    )
    dec_send = kernel_call(
        mesh_body,
        shaped(mesh_rows, BF),
        [SMEM] + [V] * 12 + [geom_of(1)] + [V] * 4,
        (c_count, fine, c_edges, *quarter, *swapped, proc_recv, mesh_one, geom, folded[1], *kept[4:7]),
        [pltpu.VMEM(mesh_rows, F32)],
        flops=4 * grid_flops,
        moved=6 << 20,
        name="mesh",
    )
    first, second, left, right = first_stage(dec_send)
    pair = paired(first, second, dec_send)
    left_pair, right_pair = second_stage(pair)
    early = kernel_call(
        decode_early_body,
        shaped((GRID_DEGREE,) + grid_rows, F32),
        [V, V, V, V, V, V, geom_of(2)],
        (d_edges, left, dec_send, right, pair, grid_recv, geom),
        [pltpu.VMEM((5 * MESH_NODES, WIDTH), BF)],
        flops=4 * grid_flops,
        moved=8 << 20,
        name="early",
    )
    outputs = kernel_call(
        decode_body,
        shaped((head.shape[1], GRID_NODES), BF),
        [V] * 7,
        (d_edges, early, left_pair, right_pair, grid_base, folded[2], head.T),
        [pltpu.VMEM((4 * MESH_NODES, WIDTH), BF), pltpu.VMEM(grid_rows, BF)],
        flops=5 * grid_flops,
        moved=8 << 20,
        name="decode",
    )
    return outputs.T[None, None]


def solution(mesh):
    return jax.shard_map(
        per_device,
        mesh=mesh,
        in_specs=(
            P("lat", "lon", None, None),
            P("lat", "lon", None, None),
            P(),
            P(),
            P(),
            P(),
            P(),
            P(),
            P(),
            P("lat", "lon", None),
            P("lat", "lon", None),
            P("lat", "lon"),
            P("lat", "lon", None, None),
            P("lat", "lon", None),
            P("lat", "lon", None, None),
            P("lat", "lon", None),
            P("lat", "lon", None),
            P("lat", "lon", None, None),
            P("lat", "lon", None),
            P("lat", "lon", None, None),
        ),
        out_specs=P("lat", "lon", None, None),
        check_vma=False,
    )
```
